32 devices in a mesh: clip: 8 (over z, x), chan: 4 (over y, core).
Axes of the slice: x: 2, y: 2, z: 4, core: 2. Of those that a mesh axis runs over, the one named last changes fastest.
Arguments:
- clip_input: bfloat16 [8, 16, 7, 7, 2048], P('clip'), may hold values from -6 to 6
- seg_count: int32 [8], P('clip'), may hold values from 8 to 16, as said below
- proj_in_master: float32 [2, 2048, 512], P(None, 'clip', 'chan'), may hold values from -0.125 to 0.125
- conv_master: float32 [2, 3, 3, 512, 512], P(None, None, None, 'clip', 'chan'), may hold values from -0.09375 to 0.09375
- proj_out_master: float32 [2, 512, 2048], P(None, 'chan', 'clip'), may hold values from -0.25 to 0.25
- head_master: float32 [2048, 174], P('clip'), may hold values from -0.5 to 0.5
- gain_first: float32 [2, 512], P(None, 'chan'), may hold values from 0.5 to 1.5
- shift_first: float32 [2, 512], P(None, 'chan'), may hold values from -3 to 3
- taps_near: float32 [2, 3, 3, 512], P(None, None, None, 'chan'), may hold values from -2 to 2
- taps_far: float32 [2, 3, 3, 512], P(None, None, None, 'chan'), may hold values from -2 to 2
- gain_second: float32 [2, 512], P(None, 'chan'), may hold values from 0.5 to 1.5
- shift_second: float32 [2, 512], P(None, 'chan'), may hold values from -3 to 3
- gain_third: float32 [2, 2048], P(None, 'chan'), may hold values from 0.5 to 1.5
- shift_third: float32 [2, 2048], P(None, 'chan'), may hold values from -3 to 3
- head_bias: float32 [174], replicated, may hold values from -3 to 3
- logit_grad: float32 [8, 174], P('clip'), may hold values from -6 to 6
Outputs:
- logits: float32 [8, 174], P('clip')
- input_grad: bfloat16 [8, 16, 7, 7, 2048], P('clip', None, None, None, 'chan')
- proj_in_grad: float32 [2, 2048, 512], P(None, 'clip', 'chan')
- conv_grad: float32 [2, 3, 3, 512, 512], P(None, None, None, 'clip', 'chan')
- proj_out_grad: float32 [2, 512, 2048], P(None, 'chan', 'clip')
- head_grad: float32 [2048, 174], P('clip')
- gain_first_grad: float32 [2, 512], P(None, 'chan')
- shift_first_grad: float32 [2, 512], P(None, 'chan')
- taps_near_grad: float32 [2, 3, 3, 512], P(None, None, None, 'chan')
- taps_far_grad: float32 [2, 3, 3, 512], P(None, None, None, 'chan')
- gain_second_grad: float32 [2, 512], P(None, 'chan')
- shift_second_grad: float32 [2, 512], P(None, 'chan')
- gain_third_grad: float32 [2, 2048], P(None, 'chan')
- shift_third_grad: float32 [2, 2048], P(None, 'chan')
- head_bias_grad: float32 [174], replicated
The draws below stay inside these ranges and needn't reach their ends.
Inputs may be any that keep to these rules, and one draw needn't show every extreme that they name: `seg_count`: each entry is half of 16 or 16; exactly half of the clips hold 16.
All inputs are finite; a program needn't handle non-finite values.
Results may differ from the reference program's by a relative error of at most 0.03.
Values may be sent and summed in bfloat16 or wider, within the bound.
No kernel may reach another device: no remote copies, remote signals or barrier semaphores. Data moves between devices by JAX's collectives and lax.ppermute only.
A program may use at most 128 MiB of HBM per device.

```python
import jax
import jax.numpy as jnp
from jax import lax

C = 2048
INNER = 512
CLASSES = 174
LAYERS = 2
SEG = 16
HH = 7
WW = 7
CLIPS = 8
N_CLIP = 8


def draw_seg_count(key, part):
    key = jax.random.fold_in(key, 3)
    order = jax.random.permutation(key, CLIPS)
    return jnp.where(order < CLIPS // 2, SEG, SEG // 2).astype(jnp.int32)


def shard_levels(key, extent, cuts, least, top_value):
    def one(position, parts):
        steps = jax.random.uniform(jax.random.fold_in(jax.random.fold_in(key, 6), position), (parts,), jnp.float32, least / len(cuts), top_value / len(cuts))
        return jnp.repeat(jnp.exp(steps), extent[position] // parts).reshape((-1,) + (1,) * (len(extent) - position - 1))

    loudness = one(*cuts[0])
    for cut in cuts[1:]:
        loudness = loudness * one(*cut)
    return loudness


def scatter_about(key, extent, width, limit, cuts=(), kind=jnp.bfloat16):
    entries = jax.random.normal(key, extent, jnp.float32) * width
    if len(cuts) > 0:
        entries = shard_levels(key, extent, cuts, -0.22, 0.18) * entries
    return jnp.clip(entries, min=-limit, max=limit).astype(kind)


def setup_inputs(seed: int = 0) -> dict:
    arg_keys = jax.random.split(jax.random.key(seed), 17)
    return {
        "clip_input": scatter_about(arg_keys[0], (CLIPS, SEG, HH, WW, C), 1.0, 6.0, ((0, 8),)),
        "seg_count": draw_seg_count(jax.random.fold_in(arg_keys[16], 71), 0),
        "proj_in_master": scatter_about(arg_keys[2], (LAYERS, C, INNER), C ** -0.5, 0.125, ((1, 8), (2, 4)), jnp.float32),
        "conv_master": scatter_about(arg_keys[3], (LAYERS, 3, 3, INNER, INNER), (9 * INNER) ** -0.5, 0.09375, ((3, 8), (4, 4)), jnp.float32),
        "proj_out_master": scatter_about(arg_keys[4], (LAYERS, INNER, C), INNER ** -0.5, 0.25, ((1, 4), (2, 8)), jnp.float32),
        "head_master": scatter_about(arg_keys[5], (C, CLASSES), (C // 16) ** -0.5, 0.5, ((0, 8),), jnp.float32),
        "gain_first": jnp.clip(1.0 + 0.1 * jax.random.normal(arg_keys[6], (LAYERS, INNER), jnp.float32), 0.5, 1.5),
        "shift_first": scatter_about(arg_keys[7], (LAYERS, INNER), 0.5, 3.0, ((1, 4),), jnp.float32),
        "taps_near": scatter_about(arg_keys[8], (LAYERS, 3, 3, INNER), 0.35, 2.0, ((3, 4),), jnp.float32),
        "taps_far": scatter_about(arg_keys[9], (LAYERS, 3, 3, INNER), 0.35, 2.0, ((3, 4),), jnp.float32),
        "gain_second": jnp.clip(1.0 + 0.1 * jax.random.normal(arg_keys[10], (LAYERS, INNER), jnp.float32), 0.5, 1.5),
        "shift_second": scatter_about(arg_keys[11], (LAYERS, INNER), 0.5, 3.0, ((1, 4),), jnp.float32),
        "gain_third": jnp.clip(1.0 + 0.1 * jax.random.normal(arg_keys[12], (LAYERS, C), jnp.float32), 0.5, 1.5),
        "shift_third": scatter_about(arg_keys[13], (LAYERS, C), 0.5, 3.0, ((1, 4),), jnp.float32),
        "head_bias": scatter_about(arg_keys[14], (CLASSES,), 0.5, 3.0, (), jnp.float32),
        "logit_grad": scatter_about(arg_keys[15], (CLIPS, CLASSES), 1.0, 6.0, ((0, 8),), jnp.float32),
    }


@jax.custom_vjp
def low(v):
    return lax.optimization_barrier(v.astype(jnp.bfloat16)).astype(jnp.float32)

@jax.custom_vjp
def low_back(v):
    return v

def low_keep(v):
    return (low(v), None)

def low_pass(kept, grad):
    return (grad,)

def back_keep(v):
    return (v, None)

def back_low(kept, grad):
    return (low(grad),)
low.defvjp(low_keep, low_pass)
low_back.defvjp(back_keep, back_low)
epsilon = 1e-05
highest = lax.Precision.HIGHEST

def norm_rows(value, valid_mask, gain, shift):
    weight = valid_mask[:, :, None, None, None]
    row_count = jnp.sum(valid_mask) * value.shape[2] * value.shape[3]
    row_mean = lax.optimization_barrier(jnp.sum(value * weight, axis=(0, 1, 2, 3))) / row_count
    centred = value - row_mean
    variance = lax.optimization_barrier(jnp.sum(centred * centred * weight, axis=(0, 1, 2, 3))) / row_count
    return centred * lax.rsqrt(variance + epsilon) * gain + shift

def differences(value, valid_mask):
    later = jnp.concatenate([value[:, 1:], jnp.zeros_like(value[:, :1])], axis=1)
    next_valid = jnp.concatenate([valid_mask[:, 1:], jnp.zeros_like(valid_mask[:, :1])], axis=1)
    return (later - value) * next_valid[:, :, None, None, None]

def depthwise(value, kernel, dilation):
    padded = jnp.pad(value, ((0, 0), (0, 0), (dilation, dilation), (dilation, dilation), (0, 0)))
    height = value.shape[2]
    across = value.shape[3]
    result = jnp.zeros_like(value)
    for row_tap in range(3):
        for col_tap in range(3):
            window = padded[:, :, row_tap * dilation:row_tap * dilation + height, col_tap * dilation:col_tap * dilation + across, :]
            result = result + window * kernel[row_tap, col_tap]
    return result

def gate_part(first_pre, valid_mask, gain, shift, kernel_near, kernel_far):
    activated = jax.nn.silu(norm_rows(first_pre, valid_mask, gain, shift))
    change = differences(activated, valid_mask)
    gate_logit = depthwise(change, kernel_near, 1) + depthwise(change, kernel_far, 2)
    return activated * (1.0 + jax.nn.sigmoid(gate_logit))

def middle_part(second_pre, valid_mask, gain, shift):
    return jax.nn.silu(norm_rows(second_pre, valid_mask, gain, shift))

def pool_part(block_out, valid_mask):
    weight = valid_mask[:, :, None, None, None]
    totals = lax.optimization_barrier(jnp.sum(block_out * weight, axis=(1, 2, 3)))
    scale = lax.optimization_barrier(jnp.sum(valid_mask, axis=1)) * block_out.shape[2] * block_out.shape[3]
    return totals / scale[:, None]

def block_layer(current, group_mask, layer_weights):
    proj_in, conv_weight, proj_out, gain_first, shift_first, taps_near, taps_far, gain_second, shift_second, gain_third, shift_third = layer_weights
    first_pre = low_back(jnp.einsum('nsabc,cd->nsabd', current, proj_in, precision=highest))
    gated = low(gate_part(first_pre, group_mask, gain_first, shift_first, taps_near, taps_far))
    flat = gated.reshape((-1,) + gated.shape[2:])
    second_flat = lax.conv_general_dilated(flat, conv_weight, (1, 1), 'SAME', dimension_numbers=('NHWC', 'HWIO', 'NHWC'), precision=highest)
    second_pre = low_back(second_flat.reshape(gated.shape[:2] + second_flat.shape[1:]))
    second_act = low(middle_part(second_pre, group_mask, gain_second, shift_second))
    branch_pre = low_back(jnp.einsum('nsabc,cd->nsabd', second_act, proj_out, precision=highest))
    return jax.nn.silu(current + norm_rows(branch_pre, group_mask, gain_third, shift_third))

def group_pass(weights, pair):
    group_x, group_mask = pair
    current = group_x
    block_out = group_x
    for layer in range(LAYERS):
        if layer > 0:
            current = low(block_out)
        block_out = block_layer(current, group_mask, tuple((item[layer] for item in weights)))
    return low(pool_part(block_out, group_mask))

def reference(clip_input, seg_count, proj_in_master, conv_master, proj_out_master, head_master, gain_first, shift_first, taps_near, taps_far, gain_second, shift_second, gain_third, shift_third, head_bias, logit_grad):
    valid_mask = (jnp.arange(SEG, dtype=jnp.int32)[None, :] < seg_count[:, None]).astype(jnp.float32)
    features = clip_input.astype(jnp.float32)
    groups_x = features.reshape((N_CLIP, CLIPS // N_CLIP) + features.shape[1:])
    groups_mask = valid_mask.reshape((N_CLIP, CLIPS // N_CLIP, SEG))
    checked = jax.checkpoint(group_pass)

    def forward(inputs, proj_in_m, conv_m, proj_out_m, head_m, gain_one, shift_one, near, far, gain_two, shift_two, gain_three, shift_three, bias):
        weights = (low(proj_in_m), low(conv_m), low(proj_out_m), gain_one, shift_one, near, far, gain_two, shift_two, gain_three, shift_three)
        inputs_grouped = inputs.reshape(groups_x.shape)
        pooled = lax.map(lambda pair: checked(weights, pair), (inputs_grouped, groups_mask))
        pooled = pooled.reshape((CLIPS, C))
        return low_back(jnp.dot(pooled, low(head_m), precision=highest) + bias)
    logits, pull = jax.vjp(forward, features, proj_in_master, conv_master, proj_out_master, head_master, gain_first, shift_first, taps_near, taps_far, gain_second, shift_second, gain_third, shift_third, head_bias)
    grads = pull(logit_grad)
    return (logits, grads[0].astype(jnp.bfloat16), grads[1], grads[2], grads[3], grads[4], grads[5], grads[6], grads[7], grads[8], grads[9], grads[10], grads[11], grads[12], grads[13])
```

```python
import types

import jax
import jax.numpy as jnp
from jax import lax
from jax.experimental import pallas as pl
from jax.experimental.pallas import tpu as pltpu
from jax.sharding import PartitionSpec as P

EPS = 1e-05
LANE = 128
WPAD = 8
CHUNK = 256
bf16 = jnp.bfloat16
f32 = jnp.float32


def call(name, body, ins, outs, scratch, flops=0, nbytes=0, limit=60):
    in_names, out_names, scratch_names = list(ins), list(outs), list(scratch)

    def kernel(*refs):
        body(types.SimpleNamespace(**dict(zip(in_names + out_names + scratch_names, refs))))

    results = pl.pallas_call(
        kernel,
        name=name,
        out_shape=[jax.ShapeDtypeStruct(*outs[n]) for n in out_names],
        in_specs=[pl.BlockSpec(memory_space=ins[n][1]) for n in in_names],
        out_specs=[pl.BlockSpec(memory_space=pltpu.VMEM) for _ in out_names],
        scratch_shapes=[scratch[n] for n in scratch_names],
        compiler_params=pltpu.CompilerParams(vmem_limit_bytes=limit * 1024 * 1024),
        cost_estimate=pl.CostEstimate(flops=flops, bytes_accessed=nbytes, transcendentals=0),
    )(*[ins[n][0] for n in in_names])
    return dict(zip(out_names, results))


VM = pltpu.VMEM
SM = pltpu.SMEM
HB = pl.ANY
COUNT, OWN, ORDER = 0, 1, 2


def lanes(start, size=LANE):
    return pl.ds(pl.multiple_of(start, LANE), size)


def dot(a, b):
    return jnp.dot(a, b, preferred_element_type=f32)


def dot_nt(a, b):
    return lax.dot_general(a, b, (((1,), (1,)), ((), ())), preferred_element_type=f32)


def sigmoid(v):
    return 1.0 / (1.0 + jnp.exp(-v))


def rotate(v, k):
    if k == 0:
        return v
    groups = v.reshape(v.shape[0] // WPAD, WPAD, v.shape[1])
    return pltpu.roll(groups, (-k) % WPAD, axis=1).reshape(v.shape)


class Geometry:
    def __init__(self, seg, high, wide):
        self.seg, self.high, self.wide = seg, high, wide
        self.step = seg * WPAD
        self.rows = high * self.step

    def block(self, h):
        return slice(h * self.step, (h + 1) * self.step)


def fill_masks(r, geo):
    count = r.meta[COUNT]
    row = lax.broadcasted_iota(jnp.int32, (geo.step, LANE), 0)
    seg = row // WPAD
    col = row - seg * WPAD
    inside = col < geo.wide
    r.mask[0] = jnp.where(inside & (seg < count), 1.0, 0.0)
    r.mask[1] = jnp.where(inside & (seg + 1 < count), 1.0, 0.0)
    r.mask[2] = jnp.where(inside, 1.0, 0.0)
    r.mask[3] = jnp.where(col >= 2, 1.0, 0.0)
    r.mask[4] = jnp.where(col < geo.wide - 2, 1.0, 0.0)


MASKS = 5


def pixel_count(r, geo):
    return r.meta[COUNT].astype(f32) * float(geo.high * geo.wide)


def column_sum(v):
    return jnp.sum(v, axis=0, keepdims=True)


def statistics(pre, cs, r, geo):
    n = pixel_count(r, geo)
    m = r.mask[0]
    total = jnp.zeros((geo.step, LANE), f32)
    for h in range(geo.high):
        total = total + pre[geo.block(h), cs] * m
    mean = column_sum(total) / n
    total = jnp.zeros((geo.step, LANE), f32)
    for h in range(geo.high):
        centred = pre[geo.block(h), cs] - mean
        total = total + centred * centred * m
    return mean, lax.rsqrt(column_sum(total) / n + EPS)


class Slots:
    def __init__(self, arrays, devices, parts, chan_n):
        self.arrays, self.devices, self.parts, self.chan_n = arrays, devices, parts, chan_n

    def operands(self):
        ins = {"slot_dev": (self.devices, SM)}
        for no, array in enumerate(self.arrays):
            ins[f"slots{no}"] = (array, HB)
        return ins

    def start(self, kind, r, dst, sem):
        base = 0
        bases = []
        for array in self.arrays:
            bases.append(base)
            base += array.shape[0]
        for no, row0, tap0, taps in self.parts[kind]:
            ref = getattr(r, f"slots{no}")

            def body(s, carry, ref=ref, base=bases[no], row0=row0, tap0=tap0, taps=taps):
                clip = r.slot_dev[0, base + s]
                chan = r.slot_dev[1, base + s]

                def copy(src, to):
                    pltpu.make_async_copy(src, to, sem).start()

                if kind == "in":
                    copy(
                        ref.at[s, pl.ds(row0, 256)],
                        dst.at[pl.ds(pl.multiple_of(clip * 256, 256), 256), lanes(chan * LANE)],
                    )
                elif kind in ("conv", "conv_t"):
                    rows = pl.ds(pl.multiple_of(clip * 64, 64), 64)
                    src = ref.at[s, pl.ds(row0, taps * 192)].reshape(taps, 3, 64, LANE)
                    if kind == "conv":
                        copy(src, dst.at[pl.ds(tap0, taps), :, rows, lanes(chan * LANE)])
                    else:
                        for b in range(3):
                            copy(
                                src.at[:, b],
                                dst.at[pl.ds(tap0, taps), rows, lanes(chan * LANE + b * 512)],
                            )
                elif kind == "out":
                    for half in range(2):
                        copy(
                            ref.at[s, pl.ds(row0 + half * 128, 128)],
                            dst.at[
                                pl.ds(pl.multiple_of(chan * 128, 128), 128),
                                lanes(clip * 256 + half * 128),
                            ],
                        )
                else:
                    for half in range(2):
                        copy(
                            ref.at[s, pl.ds(row0 + half * 64, 64)],
                            dst.at[
                                pl.ds(pl.multiple_of(clip * 256 + chan * 64, 64), 64),
                                lanes(half * 128),
                            ],
                        )
                return carry

            lax.fori_loop(0, self.arrays[no].shape[0], body, 0)


class Whole:
    def __init__(self, arrays):
        self.arrays = arrays

    def operands(self):
        return {f"whole_{kind}": (array, HB) for kind, array in self.arrays.items()}

    def start(self, kind, r, dst, sem):
        if kind == "conv_t":
            for b in range(3):
                pltpu.make_async_copy(
                    r.whole_conv.at[:, b], dst.at[:, :, pl.ds(b * 512, 512)], sem
                ).start()
        else:
            pltpu.make_async_copy(getattr(r, f"whole_{kind}"), dst, sem).start()


def arrived(dst, sem):
    pltpu.make_async_copy(dst, dst, sem).wait()


def first_matmul(r, geo, x, weight, pre):
    def body(n, carry):
        cs = lanes(n * CHUNK, CHUNK)
        pre[:, cs] = dot(x[...], weight[:, cs])
        return carry

    lax.fori_loop(0, pre.shape[1] // CHUNK, body, 0)


def conv_matmul(r, geo, g, weight, pre):
    def body(n, carry):
        cs = lanes(n * CHUNK, CHUNK)
        for a in range(3):
            w = weight[a, :, :, cs].reshape(-1, CHUNK)
            part = dot(g[a * geo.step : a * geo.step + geo.rows, :], w)
            pre[:, cs] = part if a == 0 else pre[:, cs] + part
        return carry

    lax.fori_loop(0, pre.shape[1] // CHUNK, body, 0)


def clear_edges(ref, geo, edge):
    zero = jnp.zeros((edge * geo.step, ref.shape[-1]), ref.dtype)
    lead = ref.shape[:-2]
    if lead:
        for i in range(lead[0]):
            ref[i, : edge * geo.step, :] = zero
            ref[i, (geo.high + edge) * geo.step :, :] = zero
    else:
        ref[: edge * geo.step, :] = zero
        ref[(geo.high + edge) * geo.step :, :] = zero


def store_rotated(rot, value, h, r, geo):
    at = slice((h + 2) * geo.step, (h + 3) * geo.step)
    rot[2, at, :] = value
    rot[1, at, :] = rotate(value, -1)
    rot[3, at, :] = rotate(value, 1)
    rot[0, at, :] = rotate(value, -2) * r.mask[3]
    rot[4, at, :] = rotate(value, 2) * r.mask[4]


def gate_forward(r, geo, prm, pre, keep):
    clear_edges(r.rot, geo, 2)
    clear_edges(r.g, geo, 1)
    own = r.meta[OWN]
    width = pre.shape[1]

    def body(c, carry):
        cs = lanes(c * LANE)
        mean, rr = statistics(pre, cs, r, geo)
        gain, shift = prm[0:1, cs], prm[1:2, cs]
        keep.gr1[0:1, cs] = gain * rr
        inside = r.mask[2]
        for h in range(geo.high):
            at = geo.block(h)
            xhat = (pre[at, cs] - mean) * rr
            y = xhat * gain + shift
            s = sigmoid(y)
            act = y * s
            keep.xh1[at, cs] = xhat.astype(bf16)
            keep.d1[at, cs] = (s + act * (1.0 - s)).astype(bf16)
            act = act * inside
            r.act[at, :] = act
            later = jnp.concatenate([act[WPAD:], jnp.zeros((WPAD, LANE), f32)], axis=0)
            diff = (later - act) * r.mask[1]
            store_rotated(r.rot, diff, h, r, geo)

        @pl.when(c == own)
        def _():
            keep.diff[...] = r.rot[2, 2 * geo.step : (2 + geo.high) * geo.step, :]

        for h in range(geo.high):
            at = geo.block(h)
            logit = jnp.zeros((geo.step, LANE), f32)
            for a in range(3):
                for b in range(3):
                    near = r.rot[b + 1, (h + a + 1) * geo.step : (h + a + 2) * geo.step, :]
                    logit = logit + near * prm[2 + 3 * a + b : 3 + 3 * a + b, cs]
                    far = r.rot[2 * b, (h + 2 * a) * geo.step : (h + 2 * a + 1) * geo.step, :]
                    logit = logit + far * prm[11 + 3 * a + b : 12 + 3 * a + b, cs]
            q = sigmoid(logit)
            act = r.act[at, :]
            plus = 1.0 + q
            gated = act * plus
            keep.plus[at, cs] = plus.astype(bf16)
            keep.slope[at, cs] = (act * q * (1.0 - q)).astype(bf16)
            to = slice((h + 1) * geo.step, (h + 2) * geo.step)
            for b in range(3):
                r.g[to, lanes(b * width + c * LANE)] = rotate(gated, b - 1).astype(bf16)
        return carry

    lax.fori_loop(0, width // LANE, body, 0)


def middle_forward(r, geo, prm, pre, act2, keep, transposed):
    own = r.meta[OWN]

    def body(c, carry):
        cs = lanes(c * LANE)
        mean, rr = statistics(pre, cs, r, geo)
        gain, shift = prm[20:21, cs], prm[21:22, cs]
        keep.gr2[0:1, cs] = gain * rr
        for h in range(geo.high):
            at = geo.block(h)
            xhat = (pre[at, cs] - mean) * rr
            y = xhat * gain + shift
            s = sigmoid(y)
            act = y * s
            keep.xh2[at, cs] = xhat.astype(bf16)
            keep.d2[at, cs] = (s + act * (1.0 - s)).astype(bf16)
            act2[at, cs] = act.astype(bf16)

            @pl.when(c == own)
            def _():
                transposed[:, h * geo.step : (h + 1) * geo.step] = jnp.transpose(act).astype(bf16)

        return carry

    lax.fori_loop(0, pre.shape[1] // LANE, body, 0)


def third_forward(r, geo, thr, act2, weight, x, keep):
    def body(n, carry):
        ws = lanes(n * CHUNK, CHUNK)
        r.br[...] = dot(act2[...], weight[:, ws])
        for half in range(CHUNK // LANE):
            ls = slice(half * LANE, (half + 1) * LANE)
            cs = lanes(n * CHUNK + half * LANE)
            mean, rr = statistics(r.br, ls, r, geo)
            gain, shift = thr[0:1, cs], thr[1:2, cs]
            keep.gr3[0:1, cs] = gain * rr
            for h in range(geo.high):
                at = geo.block(h)
                xhat = (r.br[at, ls] - mean) * rr
                y = x[at, cs].astype(f32) + (xhat * gain + shift)
                s = sigmoid(y)
                out = y * s
                keep.xh3[at, cs] = xhat.astype(bf16)
                keep.d3[at, cs] = (s + out * (1.0 - s)).astype(bf16)
                keep.x_next[at, cs] = out.astype(bf16)
        return carry

    lax.fori_loop(0, x.shape[1] // CHUNK, body, 0)


def by_destination(r, parts, body):
    each = parts[0].shape[0]

    def step(j, carry):
        for p, ref in enumerate(parts):
            body(r.meta[ORDER + p * each + j], ref, j)
        return carry

    lax.fori_loop(0, each, step, 0)


def third_both(r, geo, thr, act2, act2_t, weight, x, pg, parts):
    n_pix = pixel_count(r, geo)
    r.ag2[...] = jnp.zeros_like(r.ag2)

    def body(n, ref, place):
        ws = lanes(n * CHUNK, CHUNK)
        r.br[...] = dot(act2[...], weight[:, ws])
        for half in range(CHUNK // LANE):
            ls = slice(half * LANE, (half + 1) * LANE)
            cs = lanes(n * CHUNK + half * LANE)
            mean, rr = statistics(r.br, ls, r, geo)
            gain, shift = thr[0:1, cs], thr[1:2, cs]
            grad = pg[0:1, cs]
            m = r.mask[0]
            pool = jnp.zeros((geo.step, LANE), f32)
            s1 = jnp.zeros((geo.step, LANE), f32)
            s2 = jnp.zeros((geo.step, LANE), f32)
            for h in range(geo.high):
                at = geo.block(h)
                xhat = (r.br[at, ls] - mean) * rr
                y = x[at, cs].astype(f32) + (xhat * gain + shift)
                s = sigmoid(y)
                out = y * s
                d = s + out * (1.0 - s)
                pool = pool + out * m
                e = d * (grad * m)
                s1 = s1 + e
                s2 = s2 + e * xhat
                r.br[at, ls] = xhat
                r.e[at, ls] = e
                r.d3[at, cs] = d.astype(bf16)
            shift_grad, gain_grad = column_sum(s1), column_sum(s2)
            r.pooled[0:1, cs] = column_sum(pool) / n_pix
            r.third_grad[0:1, cs] = gain_grad
            r.third_grad[1:2, cs] = shift_grad
            third_scale(r, geo, ls, gain * rr, shift_grad / n_pix, gain_grad / n_pix)
        third_products(r, geo, act2_t, weight, ws, ref, place)

    by_destination(r, parts, body)


def third_scale(r, geo, ls, scale, mean1, mean2):
    m = r.mask[0]
    for h in range(geo.high):
        at = geo.block(h)
        v = scale * (r.e[at, ls] - m * (mean1 + r.br[at, ls] * mean2))
        r.bg[at, ls] = v.astype(bf16)


def third_products(r, geo, act2_t, weight, ws, ref, place):
    grad = dot(act2_t[...], r.bg[...]).astype(bf16)
    for half in range(CHUNK // LANE):
        ref[place, half * LANE : (half + 1) * LANE, :] = grad[:, half * LANE : (half + 1) * LANE]
    r.ag2[...] += dot_nt(r.bg[...], weight[:, ws])


def conv_backward(r, geo, weight_t, parts):
    clear_edges(r.sg, geo, 1)
    r.sgt[...] = jnp.zeros_like(r.sgt)
    own = r.meta[OWN]
    n_pix = pixel_count(r, geo)
    width = r.ag2.shape[1]
    m = r.mask[0]

    def body(c, carry):
        cs = lanes(c * LANE)
        s1 = jnp.zeros((geo.step, LANE), f32)
        s2 = jnp.zeros((geo.step, LANE), f32)
        for h in range(geo.high):
            at = geo.block(h)
            e = r.ag2[at, cs] * r.d2[at, cs].astype(f32)
            r.e[at, :] = e
            e = e * m
            s1 = s1 + e
            s2 = s2 + e * r.xh2[at, cs].astype(f32)
        shift_grad, gain_grad = column_sum(s1), column_sum(s2)

        @pl.when(c == own)
        def _():
            r.small[0:1, :] = gain_grad
            r.small[1:2, :] = shift_grad

        scale, mean1, mean2 = r.gr2[0:1, cs], shift_grad / n_pix, gain_grad / n_pix
        for h in range(geo.high):
            at = geo.block(h)
            v = scale * (r.e[at, :] - m * (mean1 + r.xh2[at, cs].astype(f32) * mean2))
            to = slice((h + 1) * geo.step, (h + 2) * geo.step)
            for b in range(3):
                r.sg[to, lanes(b * width + c * LANE)] = rotate(v, 1 - b).astype(bf16)

            @pl.when(c == own)
            def _():
                turned = jnp.transpose(v).astype(bf16)
                for a in range(3):
                    if 0 <= h + a - 1 < geo.high:
                        place = (h + a - 1) * geo.step
                        r.sgt[a * LANE : (a + 1) * LANE, place : place + geo.step] = turned

        return carry

    lax.fori_loop(0, width // LANE, body, 0)

    def weight_grad(k, carry):
        gs = lanes(k * CHUNK, CHUNK)
        part = dot(r.sgt[...], r.g[geo.step : geo.step + geo.rows, gs])
        b = k // (width // CHUNK)
        first = (k - b * (width // CHUNK)) * CHUNK
        for a in range(3):
            for half in range(CHUNK // LANE):
                block = part[a * LANE : (a + 1) * LANE, half * LANE : (half + 1) * LANE]
                rows = pl.ds(pl.multiple_of(first + half * LANE, LANE), LANE)
                r.wg[3 * a + b, rows, :] = jnp.transpose(block)
        return carry

    lax.fori_loop(0, 3 * width // CHUNK, weight_grad, 0)

    def hand_out(n, ref, place):
        rows = pl.ds(pl.multiple_of(n * 64, 64), 64)
        for tap in range(9):
            ref[place, tap * 64 : (tap + 1) * 64, :] = r.wg[tap, rows, :].astype(bf16)

    by_destination(r, parts, hand_out)

    def input_grad(n, carry):
        cs = lanes(n * CHUNK, CHUNK)
        rows = pl.ds(pl.multiple_of(n * CHUNK, CHUNK), CHUNK)
        for a in range(3):
            lhs = r.sg[(2 - a) * geo.step : (2 - a) * geo.step + geo.rows, :]
            part = dot_nt(lhs, weight_t[a, rows, :])
            r.gg[:, cs] = part if a == 0 else r.gg[:, cs] + part
        return carry

    lax.fori_loop(0, width // CHUNK, input_grad, 0)


def gate_backward(r, geo, prm):
    clear_edges(r.rot, geo, 2)
    own = r.meta[OWN]
    n_pix = pixel_count(r, geo)
    width = r.gg.shape[1]

    def body(c, carry):
        cs = lanes(c * LANE)
        m = r.mask[0]
        inside = r.mask[2]
        for h in range(geo.high):
            at = geo.block(h)
            grad = r.gg[at, cs] * inside
            r.e[at, :] = grad * r.plus[at, cs].astype(f32)
            store_rotated(r.rot, grad * r.slope[at, cs].astype(f32), h, r, geo)
        s1 = jnp.zeros((geo.step, LANE), f32)
        s2 = jnp.zeros((geo.step, LANE), f32)
        for h in range(geo.high):
            at = geo.block(h)
            back = jnp.zeros((geo.step, LANE), f32)
            for a in range(3):
                for b in range(3):
                    near = r.rot[3 - b, (h + 3 - a) * geo.step : (h + 4 - a) * geo.step, :]
                    back = back + near * prm[2 + 3 * a + b : 3 + 3 * a + b, cs]
                    far = r.rot[4 - 2 * b, (h + 4 - 2 * a) * geo.step : (h + 5 - 2 * a) * geo.step, :]
                    back = back + far * prm[11 + 3 * a + b : 12 + 3 * a + b, cs]
            back = back * r.mask[1]
            earlier = jnp.concatenate([jnp.zeros((WPAD, LANE), f32), back[:-WPAD]], axis=0)
            e = (r.e[at, :] + (earlier - back)) * r.d1[at, cs].astype(f32)
            r.e[at, :] = e
            e = e * m
            s1 = s1 + e
            s2 = s2 + e * r.xh1[at, cs].astype(f32)
        shift_grad, gain_grad = column_sum(s1), column_sum(s2)
        scale, mean1, mean2 = r.gr1[0:1, cs], shift_grad / n_pix, gain_grad / n_pix
        for h in range(geo.high):
            at = geo.block(h)
            v = scale * (r.e[at, :] - m * (mean1 + r.xh1[at, cs].astype(f32) * mean2))
            r.fg[at, cs] = v.astype(bf16)

            @pl.when(c == own)
            def _():
                r.fgt[:, h * geo.step : (h + 1) * geo.step] = jnp.transpose(v).astype(bf16)

        @pl.when(c == own)
        def _():
            r.small[0:1, :] = gain_grad
            r.small[1:2, :] = shift_grad
            for a in range(3):
                for b in range(3):
                    near = jnp.zeros((geo.step, LANE), f32)
                    far = jnp.zeros((geo.step, LANE), f32)
                    for h in range(geo.high):
                        diff = r.diff[geo.block(h), :]
                        near = near + diff * r.rot[3 - b, (h + 3 - a) * geo.step : (h + 4 - a) * geo.step, :]
                        far = far + diff * r.rot[4 - 2 * b, (h + 4 - 2 * a) * geo.step : (h + 5 - 2 * a) * geo.step, :]
                    r.small[2 + 3 * a + b : 3 + 3 * a + b, :] = column_sum(near)
                    r.small[11 + 3 * a + b : 12 + 3 * a + b, :] = column_sum(far)

        return carry

    lax.fori_loop(0, width // LANE, body, 0)


def first_products(r, geo, x, parts):
    def body(n, ref, place):
        part = dot(r.fgt[...], x[:, lanes(n * CHUNK, CHUNK)])
        for half in range(CHUNK // LANE):
            block = part[:, half * LANE : (half + 1) * LANE]
            ref[place, half * LANE : (half + 1) * LANE, :] = jnp.transpose(block).astype(bf16)

    by_destination(r, parts, body)


def third_backward(r, geo, weight_in, weight_out, act2_t, pg, parts):
    n_pix = pixel_count(r, geo)
    own = r.meta[OWN]
    r.ag2[...] = jnp.zeros_like(r.ag2)
    per_own = r.e3.shape[1] // CHUNK

    def body(n, ref, place):
        ws = lanes(n * CHUNK, CHUNK)
        rows = pl.ds(pl.multiple_of(n * CHUNK, CHUNK), CHUNK)
        r.br[...] = dot_nt(r.fg[...], weight_in[rows, :])
        m = r.mask[0]
        for half in range(CHUNK // LANE):
            ls = slice(half * LANE, (half + 1) * LANE)
            cs = lanes(n * CHUNK + half * LANE)
            grad = pg[0:1, cs]
            s1 = jnp.zeros((geo.step, LANE), f32)
            s2 = jnp.zeros((geo.step, LANE), f32)
            for h in range(geo.high):
                at = geo.block(h)
                out_grad = r.br[at, ls] + r.d3_next[at, cs].astype(f32) * (grad * m)
                e = out_grad * r.d3[at, cs].astype(f32)
                xhat = r.xh3[at, cs].astype(f32)
                r.ee[at, ls] = e
                r.br[at, ls] = xhat
                e = e * m
                s1 = s1 + e
                s2 = s2 + e * xhat
            shift_grad, gain_grad = column_sum(s1), column_sum(s2)
            r.third_grad[0:1, cs] = gain_grad
            r.third_grad[1:2, cs] = shift_grad
            scale, mean1, mean2 = r.gr3[0:1, cs], shift_grad / n_pix, gain_grad / n_pix
            for h in range(geo.high):
                at = geo.block(h)
                v = scale * (r.ee[at, ls] - m * (mean1 + r.br[at, ls] * mean2))
                r.bg[at, ls] = v.astype(bf16)
        owner = n // per_own

        @pl.when(owner == own)
        def _():
            r.e3[:, lanes((n - owner * per_own) * CHUNK, CHUNK)] = r.ee[...]

        third_products(r, geo, act2_t, weight_out, ws, ref, place)

    by_destination(r, parts, body)


class Sizes:
    def __init__(self, geo, inner, wide, order_n):
        self.geo, self.inner, self.wide, self.order_n = geo, inner, wide, order_n

    def mask(self):
        return VM((MASKS, self.geo.step, LANE), f32)

    def rot(self):
        return VM((5, (self.geo.high + 4) * self.geo.step, LANE), f32)

    def narrow(self, dtype=bf16):
        return ((self.geo.rows, self.inner), dtype)

    def broad(self, dtype=bf16):
        return ((self.geo.rows, self.wide), dtype)

    def stacked(self):
        return ((self.geo.rows + 2 * self.geo.step, 3 * self.inner), bf16)

    def parts(self, rows):
        return {"away": ((self.order_n // 2, rows, LANE), bf16), "home": ((self.order_n // 2, rows, LANE), bf16)}


def gate_outs(z):
    return {
        "g": z.stacked(),
        "xh1": z.narrow(),
        "d1": z.narrow(),
        "plus": z.narrow(),
        "slope": z.narrow(),
        "diff": ((z.geo.rows, LANE), f32),
        "gr1": ((1, z.inner), f32),
    }


def gate_scratch(z):
    return {"rot": z.rot(), "act": VM((z.geo.rows, LANE), f32), "mask": z.mask()}


def middle_outs(z):
    return {
        "xh2": z.narrow(),
        "d2": z.narrow(),
        "gr2": ((1, z.inner), f32),
        "act2_t": ((LANE, z.geo.rows), bf16),
    }


def kernel_gate(z, meta, source, x, prm):
    geo = z.geo

    def body(r):
        source.start("in", r, r.w_in, r.sem)
        fill_masks(r, geo)
        arrived(r.w_in, r.sem)
        first_matmul(r, geo, r.x, r.w_in, r.pre)
        gate_forward(r, geo, r.prm, r.pre, r)

    return call(
        "gate_forward",
        body,
        {"meta": (meta, SM), **source.operands(), "x": (x, VM), "prm": (prm, VM)},
        gate_outs(z),
        {
            **gate_scratch(z),
            "w_in": VM((z.wide, z.inner), bf16),
            "pre": VM((geo.rows, z.inner), f32),
            "sem": pltpu.SemaphoreType.DMA,
        },
        flops=16_000_000_000,
        nbytes=16_000_000,
    )


def kernel_block(z, meta, source, g, x, prm, thr):
    geo = z.geo

    def body(r):
        source.start("conv", r, r.w_mid, r.sem)
        source.start("out", r, r.w_out, r.sem2)
        fill_masks(r, geo)
        arrived(r.w_mid, r.sem)
        conv_matmul(r, geo, r.g, r.w_mid, r.pre)
        middle_forward(r, geo, r.prm, r.pre, r.act2, r, r.act2_t)
        arrived(r.w_out, r.sem2)
        third_forward(r, geo, r.thr, r.act2, r.w_out, r.x, r)

    return call(
        "block_forward",
        body,
        {"meta": (meta, SM), **source.operands(), "g": (g, VM), "x": (x, VM), "prm": (prm, VM), "thr": (thr, VM)},
        {
            **middle_outs(z),
            "xh3": z.broad(),
            "d3": z.broad(),
            "x_next": z.broad(),
            "gr3": ((1, z.wide), f32),
        },
        {
            "mask": z.mask(),
            "w_mid": VM((3, 3, z.inner, z.inner), bf16),
            "w_out": VM((z.inner, z.wide), bf16),
            "pre": VM((geo.rows, z.inner), f32),
            "act2": VM((geo.rows, z.inner), bf16),
            "br": VM((geo.rows, CHUNK), f32),
            "sem": pltpu.SemaphoreType.DMA,
            "sem2": pltpu.SemaphoreType.DMA,
        },
        flops=16_000_000_000,
        nbytes=16_000_000,
    )


def kernel_top(z, meta, source, x, prm, thr, grad_low, bias):
    geo = z.geo

    def body(r):
        source.start("in", r, r.w_in, r.sem)
        source.start("conv", r, r.w_mid, r.sem2)
        source.start("out", r, r.w_out, r.sem3)
        source.start("head", r, r.w_head, r.sem4)
        fill_masks(r, geo)
        arrived(r.w_in, r.sem)
        first_matmul(r, geo, r.x, r.w_in, r.pre)
        gate_forward(r, geo, r.prm, r.pre, r)
        arrived(r.w_mid, r.sem2)
        conv_matmul(r, geo, r.g, r.w_mid, r.pre)
        middle_forward(r, geo, r.prm, r.pre, r.act2, r, r.act2_t)
        arrived(r.w_out, r.sem3)
        arrived(r.w_head, r.sem4)
        n_pix = pixel_count(r, geo)
        r.pg[...] = dot_nt(r.grad[...], r.w_head[...])[0:1] / n_pix
        third_both(r, geo, r.thr, r.act2, r.act2_t, r.w_out, r.x, r.pg, [r.away, r.home])
        low = jnp.broadcast_to(r.pooled[...].astype(bf16), (16, z.wide))
        r.logits[...] = dot(low, r.w_head[...])[0:8] + r.bias[...]

    return call(
        "top_both",
        body,
        {
            "meta": (meta, SM),
            **source.operands(),
            "x": (x, VM),
            "prm": (prm, VM),
            "thr": (thr, VM),
            "grad": (grad_low, VM),
            "bias": (bias, VM),
        },
        {
            **gate_outs(z),
            **middle_outs(z),
            "d3": z.broad(),
            "pooled": ((1, z.wide), f32),
            "pg": ((1, z.wide), f32),
            "logits": ((8, bias.shape[1]), f32),
            "third_grad": ((2, z.wide), f32),
            "ag2": z.narrow(f32),
            **z.parts(256),
        },
        {
            **gate_scratch(z),
            "w_in": VM((z.wide, z.inner), bf16),
            "w_mid": VM((3, 3, z.inner, z.inner), bf16),
            "w_out": VM((z.inner, z.wide), bf16),
            "w_head": VM((z.wide, bias.shape[1]), bf16),
            "pre": VM((geo.rows, z.inner), f32),
            "act2": VM((geo.rows, z.inner), bf16),
            "br": VM((geo.rows, CHUNK), f32),
            "e": VM((geo.rows, CHUNK), f32),
            "bg": VM((geo.rows, CHUNK), bf16),
            "sem": pltpu.SemaphoreType.DMA,
            "sem2": pltpu.SemaphoreType.DMA,
            "sem3": pltpu.SemaphoreType.DMA,
            "sem4": pltpu.SemaphoreType.DMA,
        },
        flops=40_000_000_000,
        nbytes=30_000_000,
    )


def kernel_conv_back(z, meta, source, ag2, kept):
    geo = z.geo

    def body(r):
        source.start("conv_t", r, r.w_t, r.sem)
        fill_masks(r, geo)
        arrived(r.w_t, r.sem)
        conv_backward(r, geo, r.w_t, [r.away, r.home])

    return call(
        "conv_backward",
        body,
        {
            "meta": (meta, SM),
            **source.operands(),
            "ag2": (ag2, VM),
            "xh2": (kept["xh2"], VM),
            "d2": (kept["d2"], VM),
            "gr2": (kept["gr2"], VM),
            "g": (kept["g"], VM),
        },
        {"gg": z.narrow(f32), "small": ((2, LANE), f32), **z.parts(576)},
        {
            "mask": z.mask(),
            "w_t": VM((3, z.inner, 3 * z.inner), bf16),
            "sg": VM(*z.stacked()),
            "sgt": VM((3 * LANE, geo.rows), bf16),
            "wg": VM((9, z.inner, LANE), f32),
            "e": VM((geo.rows, LANE), f32),
            "sem": pltpu.SemaphoreType.DMA,
        },
        flops=20_000_000_000,
        nbytes=16_000_000,
    )


def gate_back_ins(kept, prm):
    ins = {name: (kept[name], VM) for name in ("xh1", "d1", "plus", "slope", "diff", "gr1")}
    ins["prm"] = (prm, VM)
    return ins


def gate_back_scratch(z):
    return {
        "mask": z.mask(),
        "rot": z.rot(),
        "e": VM((z.geo.rows, LANE), f32),
        "fg": VM(*z.narrow()),
        "fgt": VM((LANE, z.geo.rows), bf16),
        "w_in": VM((z.wide, z.inner), bf16),
        "sem": pltpu.SemaphoreType.DMA,
    }


def kernel_join(z, meta, source, source_below, gg, kept, below, prm, x, d3_next, pg):
    geo = z.geo
    both = {}
    for tag, item in (("a_", source), ("b_", source_below)):
        both.update({tag + name: value for name, value in item.operands().items()})

    def view(r, tag):
        picked = {k[2:]: v for k, v in vars(r).items() if k.startswith(tag)}
        return types.SimpleNamespace(**picked)

    def body(r):
        source.start("in", view(r, "a_"), r.w_in, r.sem)
        source_below.start("out", view(r, "b_"), r.w_out, r.sem2)
        fill_masks(r, geo)
        gate_backward(r, geo, r.prm)
        first_products(r, geo, r.x, [r.away_in, r.home_in])
        arrived(r.w_in, r.sem)
        arrived(r.w_out, r.sem2)
        third_backward(r, geo, r.w_in, r.w_out, r.act2_t, r.pg, [r.away, r.home])

    parts = z.parts(256)
    return call(
        "join_backward",
        body,
        {
            "meta": (meta, SM),
            **both,
            "gg": (gg, VM),
            **gate_back_ins(kept, prm),
            "x": (x, VM),
            "d3_next": (d3_next, VM),
            "pg": (pg, VM),
            "d3": (below["d3"], VM),
            "xh3": (below["xh3"], VM),
            "gr3": (below["gr3"], VM),
            "act2_t": (below["act2_t"], VM),
        },
        {
            "small": ((20, LANE), f32),
            "third_grad": ((2, z.wide), f32),
            "ag2": z.narrow(f32),
            "e3": ((geo.rows, z.wide // 4), f32),
            **parts,
            **{name + "_in": value for name, value in parts.items()},
        },
        {
            **gate_back_scratch(z),
            "w_out": VM((z.inner, z.wide), bf16),
            "br": VM((geo.rows, CHUNK), f32),
            "ee": VM((geo.rows, CHUNK), f32),
            "bg": VM((geo.rows, CHUNK), bf16),
            "sem2": pltpu.SemaphoreType.DMA,
        },
        flops=20_000_000_000,
        nbytes=30_000_000,
    )


def kernel_bottom(z, meta, source, gg, kept, prm, x, e3):
    geo = z.geo
    quarter = e3.shape[1]

    def body(r):
        source.start("in", r, r.w_in, r.sem)
        fill_masks(r, geo)
        gate_backward(r, geo, r.prm)
        first_products(r, geo, r.x, [r.away, r.home])
        arrived(r.w_in, r.sem)
        own = r.meta[OWN]
        for n in range(quarter // CHUNK):
            cs = slice(n * CHUNK, (n + 1) * CHUNK)
            rows = pl.ds(pl.multiple_of(own * quarter + n * CHUNK, CHUNK), CHUNK)
            r.x_grad[:, cs] = (dot_nt(r.fg[...], r.w_in[rows, :]) + r.e3[:, cs]).astype(bf16)

    return call(
        "bottom_backward",
        body,
        {
            "meta": (meta, SM),
            **source.operands(),
            "gg": (gg, VM),
            **gate_back_ins(kept, prm),
            "x": (x, VM),
            "e3": (e3, VM),
        },
        {"small": ((20, LANE), f32), "x_grad": ((geo.rows, quarter), bf16), **z.parts(256)},
        gate_back_scratch(z),
        flops=10_000_000_000,
        nbytes=16_000_000,
    )


def local(
    clip_input,
    seg_count,
    proj_in_master,
    conv_master,
    proj_out_master,
    head_master,
    gain_first,
    shift_first,
    taps_near,
    taps_far,
    gain_second,
    shift_second,
    gain_third,
    shift_third,
    head_bias,
    logit_grad,
    clip_n,
    chan_n,
):
    clip = lax.axis_index("clip")
    chan = lax.axis_index("chan")
    _, seg, high, wide_map, wide = clip_input.shape
    layers = proj_in_master.shape[0]
    inner = proj_in_master.shape[2] * chan_n
    classes = head_master.shape[1]
    class_pad = -(-classes // LANE) * LANE
    geo = Geometry(seg, high, wide_map)
    order_n = wide // CHUNK
    z = Sizes(geo, inner, wide, order_n)

    own_small = jnp.concatenate(
        [
            gain_first[:, None],
            shift_first[:, None],
            taps_near.reshape(layers, 9, -1),
            taps_far.reshape(layers, 9, -1),
            gain_second[:, None],
            shift_second[:, None],
            gain_third.reshape(layers, -1, LANE),
            shift_third.reshape(layers, -1, LANE),
        ],
        axis=1,
    )
    all_small = lax.all_gather(own_small, "chan", axis=0, tiled=False)
    prm = jnp.transpose(all_small[:, :, :22], (1, 2, 0, 3)).reshape(layers, 22, inner)
    thr = jnp.transpose(all_small[:, :, 22:].reshape(chan_n, layers, 2, -1), (1, 2, 0, 3)).reshape(
        layers, 2, wide
    )

    head_low = jnp.pad(head_master.astype(bf16), ((0, 0), (0, class_pad - classes)))
    sources = []
    if proj_in_master.shape[1] == 256 and chan_n == 4:
        own_head = lax.dynamic_slice_in_dim(head_low, chan * 64, 64, 0)
        own_head = jnp.transpose(own_head.reshape(64, 2, LANE), (1, 0, 2)).reshape(128, LANE)
        numbers = jnp.arange(clip_n * chan_n, dtype=jnp.int32)
        devices = jnp.stack([numbers // chan_n, numbers % chan_n])
        for layer in range(layers):
            out_low = proj_out_master[layer].astype(bf16)
            items = [
                proj_in_master[layer].astype(bf16),
                conv_master[layer].astype(bf16).reshape(-1, LANE),
                jnp.transpose(out_low.reshape(LANE, 2, LANE), (1, 0, 2)).reshape(256, LANE),
            ]
            if layer == layers - 1:
                items.append(own_head)
            packed = lax.all_gather(jnp.concatenate(items, axis=0), ("clip", "chan"), axis=0, tiled=False)
            parts = {"in": [(0, 0, 0, 0)], "conv": [(0, 256, 0, 3)], "out": [(0, 832, 0, 0)], "head": [(0, 1088, 0, 0)]}
            parts["conv_t"] = parts["conv"]
            sources.append(Slots([packed], devices, parts, chan_n))
    else:
        whole_head = lax.all_gather(head_low, "clip", axis=0, tiled=True)
        gathered = []
        for master, clip_axis, chan_axis in ((proj_in_master, 1, 2), (conv_master, 3, 4), (proj_out_master, 2, 1)):
            item = lax.all_gather(master.astype(bf16), "clip", axis=clip_axis, tiled=True)
            gathered.append(lax.all_gather(item, "chan", axis=chan_axis, tiled=True))
        for layer in range(layers):
            sources.append(
                Whole(
                    {
                        "in": gathered[0][layer],
                        "conv": gathered[1][layer],
                        "out": gathered[2][layer],
                        "head": whole_head,
                    }
                )
            )

    order = jnp.arange(order_n, dtype=jnp.int32)
    meta = jnp.concatenate([seg_count.astype(jnp.int32), chan[None].astype(jnp.int32), order])

    grad_low = logit_grad.astype(bf16)
    grad_rows = jnp.pad(grad_low, ((0, 15), (0, class_pad - classes)))
    bias_row = jnp.pad(head_bias, (0, class_pad - classes))[None]

    x0 = jnp.transpose(clip_input[0], (1, 0, 2, 3))
    x0 = jnp.pad(x0, ((0, 0), (0, 0), (0, WPAD - wide_map), (0, 0))).reshape(geo.rows, wide)

    gate0 = kernel_gate(z, meta, sources[0], x0, prm[0])
    block0 = kernel_block(z, meta, sources[0], gate0["g"], x0, prm[0], thr[0])
    x1 = block0["x_next"]
    top = kernel_top(z, meta, sources[1], x1, prm[1], thr[1], grad_rows, bias_row)
    mid1 = kernel_conv_back(z, meta, sources[1], top["ag2"], top)
    join = kernel_join(
        z, meta, sources[1], sources[0], mid1["gg"], top, block0, prm[1], x1, top["d3"], top["pg"]
    )
    mid0 = kernel_conv_back(z, meta, sources[0], join["ag2"], {**gate0, **block0})
    low = kernel_bottom(z, meta, sources[0], mid0["gg"], gate0, prm[0], x0, join["e3"])

    logits = top["logits"][0:1, :classes]
    input_grad = low["x_grad"].reshape(high, seg, WPAD, -1)[:, :, :wide_map]
    input_grad = jnp.transpose(input_grad, (1, 0, 2, 3))[None]

    pooled_all = lax.all_gather(top["pooled"].astype(bf16), "clip", axis=0, tiled=True)
    grad_all = lax.all_gather(grad_low, "clip", axis=0, tiled=True)
    own_rows = head_master.shape[0]
    pooled_own = lax.dynamic_slice_in_dim(pooled_all, clip * own_rows, own_rows, 1)
    head_share = lax.dot_general(
        pooled_own, grad_all, (((0,), (0,)), ((), ())), preferred_element_type=f32
    )
    bias_grad = jnp.sum(grad_all.astype(f32), axis=0)

    def joined(item, tag=""):
        return jnp.concatenate([item["away" + tag], item["home" + tag]], axis=0)

    in_terms = jnp.stack([joined(low), joined(join, "_in")]).reshape(layers, wide, LANE)
    mid_terms = jnp.stack([joined(mid0), joined(mid1)]).reshape(layers, 8, 3, 3, 64, LANE)
    mid_terms = jnp.transpose(mid_terms, (0, 2, 3, 1, 4, 5)).reshape(layers, 3, 3, inner, LANE)
    out_terms = jnp.stack([joined(join), joined(top)]).reshape(layers, 8, 2, LANE, LANE)
    out_terms = jnp.transpose(out_terms, (0, 3, 1, 2, 4)).reshape(layers, LANE, wide)
    in_share = lax.psum_scatter(in_terms, "clip", scatter_dimension=1, tiled=True).astype(f32)
    mid_share = lax.psum_scatter(mid_terms, "clip", scatter_dimension=3, tiled=True).astype(f32)
    out_share = lax.psum_scatter(out_terms, "clip", scatter_dimension=2, tiled=True).astype(f32)

    third = jnp.stack([join["third_grad"], top["third_grad"]])
    third_own = lax.dynamic_slice_in_dim(third, chan * (wide // chan_n), wide // chan_n, 2)
    small = jnp.concatenate(
        [
            jnp.stack([low["small"], join["small"]]),
            jnp.stack([mid0["small"], mid1["small"]]),
            third_own.reshape(layers, -1, LANE),
        ],
        axis=1,
    )
    small = lax.psum(small, "clip")
    third_rows = (small.shape[1] - 22) // 2
    return (
        logits,
        input_grad,
        in_share,
        mid_share,
        out_share,
        head_share,
        small[:, 0],
        small[:, 1],
        small[:, 2:11].reshape(layers, 3, 3, LANE),
        small[:, 11:20].reshape(layers, 3, 3, LANE),
        small[:, 20],
        small[:, 21],
        small[:, 22 : 22 + third_rows].reshape(layers, -1),
        small[:, 22 + third_rows :].reshape(layers, -1),
        bias_grad,
    )


def solution(mesh):
    clip_n, chan_n = mesh.shape["clip"], mesh.shape["chan"]

    def program(*args):
        return local(*args, clip_n, chan_n)

    in_specs = (
        P("clip", None, None, None, None),
        P("clip"),
        P(None, "clip", "chan"),
        P(None, None, None, "clip", "chan"),
        P(None, "chan", "clip"),
        P("clip", None),
        P(None, "chan"),
        P(None, "chan"),
        P(None, None, None, "chan"),
        P(None, None, None, "chan"),
        P(None, "chan"),
        P(None, "chan"),
        P(None, "chan"),
        P(None, "chan"),
        P(),
        P("clip", None),
    )
    out_specs = (
        P("clip", None),
        P("clip", None, None, None, "chan"),
        P(None, "clip", "chan"),
        P(None, None, None, "clip", "chan"),
        P(None, "chan", "clip"),
        P("clip", None),
        P(None, "chan"),
        P(None, "chan"),
        P(None, None, None, "chan"),
        P(None, None, None, "chan"),
        P(None, "chan"),
        P(None, "chan"),
        P(None, "chan"),
        P(None, "chan"),
        P(),
    )
    return jax.shard_map(program, mesh=mesh, in_specs=in_specs, out_specs=out_specs, check_vma=False)
```

```python
import types

import jax
import jax.numpy as jnp
from jax import lax
from jax.experimental import pallas as pl
from jax.experimental.pallas import tpu as pltpu
from jax.sharding import PartitionSpec as P

EPS = 1e-05
LANE = 128
WPAD = 8
CHUNK = 256
bf16 = jnp.bfloat16
f32 = jnp.float32


def call(name, body, ins, outs, scratch, flops=0, nbytes=0, limit=60):
    in_names, out_names, scratch_names = list(ins), list(outs), list(scratch)

    def kernel(*refs):
        body(types.SimpleNamespace(**dict(zip(in_names + out_names + scratch_names, refs))))

    results = pl.pallas_call(
        kernel,
        name=name,
        out_shape=[jax.ShapeDtypeStruct(*outs[n]) for n in out_names],
        in_specs=[pl.BlockSpec(memory_space=ins[n][1]) for n in in_names],
        out_specs=[pl.BlockSpec(memory_space=pltpu.VMEM) for _ in out_names],
        scratch_shapes=[scratch[n] for n in scratch_names],
        compiler_params=pltpu.CompilerParams(vmem_limit_bytes=limit * 1024 * 1024),
        cost_estimate=pl.CostEstimate(flops=flops, bytes_accessed=nbytes, transcendentals=0),
    )(*[ins[n][0] for n in in_names])
    return dict(zip(out_names, results))


VM = pltpu.VMEM
SM = pltpu.SMEM
HB = pl.ANY
COUNT, OWN, ORDER = 0, 1, 2


def lanes(start, size=LANE):
    return pl.ds(pl.multiple_of(start, LANE), size)


def dot(a, b):
    return jnp.dot(a, b, preferred_element_type=f32)


def dot_nt(a, b):
    return lax.dot_general(a, b, (((1,), (1,)), ((), ())), preferred_element_type=f32)


def sigmoid(v):
    return 1.0 / (1.0 + jnp.exp(-v))


def rotate(v, k):
    if k == 0:
        return v
    groups = v.reshape(v.shape[0] // WPAD, WPAD, v.shape[1])
    return pltpu.roll(groups, (-k) % WPAD, axis=1).reshape(v.shape)


class Geometry:
    def __init__(self, seg, high, wide):
        self.seg, self.high, self.wide = seg, high, wide
        self.step = seg * WPAD
        self.rows = high * self.step

    def block(self, h):
        return slice(h * self.step, (h + 1) * self.step)


def fill_masks(r, geo):
    count = r.meta[COUNT]
    row = lax.broadcasted_iota(jnp.int32, (geo.step, LANE), 0)
    seg = row // WPAD
    col = row - seg * WPAD
    inside = col < geo.wide
    r.mask[0] = jnp.where(inside & (seg < count), 1.0, 0.0)
    r.mask[1] = jnp.where(inside & (seg + 1 < count), 1.0, 0.0)
    r.mask[2] = jnp.where(inside, 1.0, 0.0)
    r.mask[3] = jnp.where(col >= 2, 1.0, 0.0)
    r.mask[4] = jnp.where(col < geo.wide - 2, 1.0, 0.0)


MASKS = 5
SMALL_ROWS = 24


def pixel_count(r, geo):
    return r.meta[COUNT].astype(f32) * float(geo.high * geo.wide)


def column_sum(v):
    return jnp.sum(v, axis=0, keepdims=True)


def statistics(pre, cs, r, geo):
    n = pixel_count(r, geo)
    m = r.mask[0]
    total = jnp.zeros((geo.step, LANE), f32)
    for h in range(geo.high):
        total = total + pre[geo.block(h), cs] * m
    mean = column_sum(total) / n
    total = jnp.zeros((geo.step, LANE), f32)
    for h in range(geo.high):
        centred = pre[geo.block(h), cs] - mean
        total = total + centred * centred * m
    return mean, lax.rsqrt(column_sum(total) / n + EPS)


class Slots:
    def __init__(self, arrays, devices, parts, chan_n):
        self.arrays, self.devices, self.parts, self.chan_n = arrays, devices, parts, chan_n

    def operands(self):
        ins = {"slot_dev": (self.devices, SM)}
        for no, array in enumerate(self.arrays):
            ins[f"slots{no}"] = (array, HB)
        return ins

    def start(self, kind, r, dst, sem):
        base = 0
        bases = []
        for array in self.arrays:
            bases.append(base)
            base += array.shape[0]
        for no, row0, first, many in self.parts[kind]:
            ref = getattr(r, f"slots{no}")

            def body(s, carry, ref=ref, base=bases[no], row0=row0, first=first, many=many):
                clip = r.slot_dev[0, base + s]
                chan = r.slot_dev[1, base + s]

                def copy(src, to):
                    pltpu.make_async_copy(src, to, sem).start()

                if kind == "in":
                    rows = pl.ds(pl.multiple_of(clip * 256 + first, LANE), many)
                    copy(ref.at[s, pl.ds(row0, many)], dst.at[rows, lanes(chan * LANE)])
                elif kind in ("conv", "conv_t"):
                    rows = pl.ds(pl.multiple_of(clip * 64, 64), 64)
                    src = ref.at[s, pl.ds(row0, many * 192)].reshape(many, 3, 64, LANE)
                    if kind == "conv":
                        copy(src, dst.at[pl.ds(first, many), :, rows, lanes(chan * LANE)])
                    else:
                        for b in range(3):
                            copy(
                                src.at[:, b],
                                dst.at[pl.ds(first, many), rows, lanes(chan * LANE + b * 512)],
                            )
                elif kind == "out":
                    rows = pl.ds(pl.multiple_of(chan * LANE, LANE), LANE)
                    for half in range(2):
                        copy(
                            ref.at[s, pl.ds(row0 + half * LANE, LANE)],
                            dst.at[rows, lanes(clip * 256 + half * LANE)],
                        )
                else:
                    rows = pl.ds(pl.multiple_of(clip * 256 + chan * 64, 64), 64)
                    for half in range(2):
                        copy(ref.at[s, pl.ds(row0 + half * 64, 64)], dst.at[rows, lanes(half * LANE)])
                return carry

            lax.fori_loop(0, self.arrays[no].shape[0], body, 0)


class Whole:
    def __init__(self, arrays):
        self.arrays = arrays

    def operands(self):
        return {f"whole_{kind}": (array, HB) for kind, array in self.arrays.items()}

    def start(self, kind, r, dst, sem):
        if kind == "conv_t":
            for b in range(3):
                pltpu.make_async_copy(
                    r.whole_conv.at[:, b], dst.at[:, :, pl.ds(b * 512, 512)], sem
                ).start()
        else:
            pltpu.make_async_copy(getattr(r, f"whole_{kind}"), dst, sem).start()


def arrived(dst, sem):
    pltpu.make_async_copy(dst, dst, sem).wait()


def first_matmul(r, geo, x, weight, pre):
    def body(n, carry):
        cs = lanes(n * CHUNK, CHUNK)
        pre[:, cs] = dot(x[...], weight[:, cs])
        return carry

    lax.fori_loop(0, pre.shape[1] // CHUNK, body, 0)


def conv_matmul(r, geo, g, weight, pre):
    def body(n, carry):
        cs = lanes(n * CHUNK, CHUNK)
        for a in range(3):
            w = weight[a, :, :, cs].reshape(-1, CHUNK)
            part = dot(g[a * geo.step : a * geo.step + geo.rows, :], w)
            pre[:, cs] = part if a == 0 else pre[:, cs] + part
        return carry

    lax.fori_loop(0, pre.shape[1] // CHUNK, body, 0)


def clear_edges(ref, geo, edge):
    zero = jnp.zeros((edge * geo.step, ref.shape[-1]), ref.dtype)
    lead = ref.shape[:-2]
    if lead:
        for i in range(lead[0]):
            ref[i, : edge * geo.step, :] = zero
            ref[i, (geo.high + edge) * geo.step :, :] = zero
    else:
        ref[: edge * geo.step, :] = zero
        ref[(geo.high + edge) * geo.step :, :] = zero


def store_rotated(rot, value, h, r, geo):
    at = slice((h + 2) * geo.step, (h + 3) * geo.step)
    rot[2, at, :] = value
    rot[1, at, :] = rotate(value, -1)
    rot[3, at, :] = rotate(value, 1)
    rot[0, at, :] = rotate(value, -2) * r.mask[3]
    rot[4, at, :] = rotate(value, 2) * r.mask[4]


def gate_forward(r, geo, prm, pre, keep):
    clear_edges(r.rot, geo, 2)
    clear_edges(r.g, geo, 1)
    own = r.meta[OWN]
    width = pre.shape[1]

    def body(c, carry):
        cs = lanes(c * LANE)
        mean, rr = statistics(pre, cs, r, geo)
        gain, shift = prm[0:1, cs], prm[1:2, cs]
        keep.gr1[0:1, cs] = gain * rr
        inside = r.mask[2]
        for h in range(geo.high):
            at = geo.block(h)
            xhat = (pre[at, cs] - mean) * rr
            y = xhat * gain + shift
            s = sigmoid(y)
            act = y * s
            keep.xh1[at, cs] = xhat.astype(bf16)
            keep.d1[at, cs] = (s + act * (1.0 - s)).astype(bf16)
            act = act * inside
            r.act[at, :] = act
            later = jnp.concatenate([act[WPAD:], jnp.zeros((WPAD, LANE), f32)], axis=0)
            diff = (later - act) * r.mask[1]
            store_rotated(r.rot, diff, h, r, geo)

        @pl.when(c == own)
        def _():
            keep.diff[...] = r.rot[2, 2 * geo.step : (2 + geo.high) * geo.step, :]

        for h in range(geo.high):
            at = geo.block(h)
            logit = jnp.zeros((geo.step, LANE), f32)
            for a in range(3):
                for b in range(3):
                    near = r.rot[b + 1, (h + a + 1) * geo.step : (h + a + 2) * geo.step, :]
                    logit = logit + near * prm[2 + 3 * a + b : 3 + 3 * a + b, cs]
                    far = r.rot[2 * b, (h + 2 * a) * geo.step : (h + 2 * a + 1) * geo.step, :]
                    logit = logit + far * prm[11 + 3 * a + b : 12 + 3 * a + b, cs]
            q = sigmoid(logit)
            act = r.act[at, :]
            plus = 1.0 + q
            gated = act * plus
            keep.plus[at, cs] = plus.astype(bf16)
            keep.slope[at, cs] = (act * q * (1.0 - q)).astype(bf16)
            to = slice((h + 1) * geo.step, (h + 2) * geo.step)
            for b in range(3):
                r.g[to, lanes(b * width + c * LANE)] = rotate(gated, b - 1).astype(bf16)
        return carry

    lax.fori_loop(0, width // LANE, body, 0)


def middle_forward(r, geo, prm, pre, act2, keep, transposed):
    own = r.meta[OWN]

    def body(c, carry):
        cs = lanes(c * LANE)
        mean, rr = statistics(pre, cs, r, geo)
        gain, shift = prm[20:21, cs], prm[21:22, cs]
        keep.gr2[0:1, cs] = gain * rr
        for h in range(geo.high):
            at = geo.block(h)
            xhat = (pre[at, cs] - mean) * rr
            y = xhat * gain + shift
            s = sigmoid(y)
            act = y * s
            keep.xh2[at, cs] = xhat.astype(bf16)
            keep.d2[at, cs] = (s + act * (1.0 - s)).astype(bf16)
            act2[at, cs] = act.astype(bf16)

            @pl.when(c == own)
            def _():
                transposed[:, h * geo.step : (h + 1) * geo.step] = jnp.transpose(act).astype(bf16)

        return carry

    lax.fori_loop(0, pre.shape[1] // LANE, body, 0)


def third_forward(r, geo, thr, act2, weight, x, keep):
    def body(n, carry):
        ws = lanes(n * CHUNK, CHUNK)
        r.br[...] = dot(act2[...], weight[:, ws])
        for half in range(CHUNK // LANE):
            ls = slice(half * LANE, (half + 1) * LANE)
            cs = lanes(n * CHUNK + half * LANE)
            mean, rr = statistics(r.br, ls, r, geo)
            gain, shift = thr[0:1, cs], thr[1:2, cs]
            keep.gr3[0:1, cs] = gain * rr
            for h in range(geo.high):
                at = geo.block(h)
                xhat = (r.br[at, ls] - mean) * rr
                y = x[at, cs].astype(f32) + (xhat * gain + shift)
                s = sigmoid(y)
                out = y * s
                keep.xh3[at, cs] = xhat.astype(bf16)
                keep.d3[at, cs] = (s + out * (1.0 - s)).astype(bf16)
                keep.x_next[at, cs] = out.astype(bf16)
        return carry

    lax.fori_loop(0, x.shape[1] // CHUNK, body, 0)


def by_destination(r, parts, body):
    each = parts[0].shape[0]

    def step(j, carry):
        for p, ref in enumerate(parts):
            body(r.meta[ORDER + p * each + j], ref, j)
        return carry

    lax.fori_loop(0, each, step, 0)


def third_both(r, geo, thr, act2, act2_t, weight, x, pg, parts):
    n_pix = pixel_count(r, geo)
    r.ag2[...] = jnp.zeros_like(r.ag2)

    def body(n, ref, place):
        ws = lanes(n * CHUNK, CHUNK)
        r.br[...] = dot(act2[...], weight[:, ws])
        for half in range(CHUNK // LANE):
            ls = slice(half * LANE, (half + 1) * LANE)
            cs = lanes(n * CHUNK + half * LANE)
            mean, rr = statistics(r.br, ls, r, geo)
            gain, shift = thr[0:1, cs], thr[1:2, cs]
            grad = pg[0:1, cs]
            m = r.mask[0]
            pool = jnp.zeros((geo.step, LANE), f32)
            s1 = jnp.zeros((geo.step, LANE), f32)
            s2 = jnp.zeros((geo.step, LANE), f32)
            for h in range(geo.high):
                at = geo.block(h)
                xhat = (r.br[at, ls] - mean) * rr
                y = x[at, cs].astype(f32) + (xhat * gain + shift)
                s = sigmoid(y)
                out = y * s
                d = s + out * (1.0 - s)
                pool = pool + out * m
                e = d * (grad * m)
                s1 = s1 + e
                s2 = s2 + e * xhat
                r.br[at, ls] = xhat
                r.e[at, ls] = e
                r.d3[at, cs] = d.astype(bf16)
            shift_grad, gain_grad = column_sum(s1), column_sum(s2)
            r.pooled[0:1, cs] = column_sum(pool) / n_pix
            r.third_grad[0:1, cs] = gain_grad
            r.third_grad[1:2, cs] = shift_grad
            third_scale(r, geo, ls, gain * rr, shift_grad / n_pix, gain_grad / n_pix)
        third_products(r, geo, act2_t, weight, ws, ref, place)

    by_destination(r, parts, body)


def third_scale(r, geo, ls, scale, mean1, mean2):
    m = r.mask[0]
    for h in range(geo.high):
        at = geo.block(h)
        v = scale * (r.e[at, ls] - m * (mean1 + r.br[at, ls] * mean2))
        r.bg[at, ls] = v.astype(bf16)


def third_products(r, geo, act2_t, weight, ws, ref, place, row0=0):
    grad = dot(act2_t[...], r.bg[...]).astype(bf16)
    for half in range(CHUNK // LANE):
        rows = slice(row0 + half * LANE, row0 + (half + 1) * LANE)
        ref[place, rows, :] = grad[:, half * LANE : (half + 1) * LANE]
    r.ag2[...] += dot_nt(r.bg[...], weight[:, ws])


HEAD_ROWS = 16


def conv_backward(r, geo, weight_t, sem, parts, top):
    clear_edges(r.sg, geo, 1)
    r.sgt[...] = jnp.zeros_like(r.sgt)
    own = r.meta[OWN]
    n_pix = pixel_count(r, geo)
    width = r.ag2.shape[1]
    m = r.mask[0]

    def body(c, carry):
        cs = lanes(c * LANE)
        s1 = jnp.zeros((geo.step, LANE), f32)
        s2 = jnp.zeros((geo.step, LANE), f32)
        for h in range(geo.high):
            at = geo.block(h)
            e = r.ag2[at, cs] * r.d2[at, cs].astype(f32)
            r.e[at, :] = e
            e = e * m
            s1 = s1 + e
            s2 = s2 + e * r.xh2[at, cs].astype(f32)
        shift_grad, gain_grad = column_sum(s1), column_sum(s2)

        @pl.when(c == own)
        def _():
            r.small[0:1, :] = gain_grad
            r.small[1:2, :] = shift_grad

        scale, mean1, mean2 = r.gr2[0:1, cs], shift_grad / n_pix, gain_grad / n_pix
        for h in range(geo.high):
            at = geo.block(h)
            v = scale * (r.e[at, :] - m * (mean1 + r.xh2[at, cs].astype(f32) * mean2))
            to = slice((h + 1) * geo.step, (h + 2) * geo.step)
            for b in range(3):
                r.sg[to, lanes(b * width + c * LANE)] = rotate(v, 1 - b).astype(bf16)

            @pl.when(c == own)
            def _():
                turned = jnp.transpose(v).astype(bf16)
                for a in range(3):
                    if 0 <= h + a - 1 < geo.high:
                        place = (h + a - 1) * geo.step
                        r.sgt[a * LANE : (a + 1) * LANE, place : place + geo.step] = turned

        return carry

    lax.fori_loop(0, width // LANE, body, 0)

    def weight_grad(k, carry):
        gs = lanes(k * CHUNK, CHUNK)
        part = dot(r.sgt[...], r.g[geo.step : geo.step + geo.rows, gs])
        b = k // (width // CHUNK)
        first = (k - b * (width // CHUNK)) * CHUNK
        for a in range(3):
            for half in range(CHUNK // LANE):
                block = part[a * LANE : (a + 1) * LANE, half * LANE : (half + 1) * LANE]
                rows = pl.ds(pl.multiple_of(first + half * LANE, LANE), LANE)
                r.wg[3 * a + b, rows, :] = jnp.transpose(block)
        return carry

    lax.fori_loop(0, 3 * width // CHUNK, weight_grad, 0)

    def hand_out(n, ref, place):
        rows = pl.ds(pl.multiple_of(n * 64, 64), 64)
        for tap in range(9):
            ref[place, tap * 64 : (tap + 1) * 64, :] = r.wg[tap, rows, :].astype(bf16)
        if top:
            pieces = [r.pooled[0:1, lanes(n * CHUNK, CHUNK)], r.grad[0:1, :].astype(f32)]
            pieces = [v[:, i * LANE : (i + 1) * LANE] for v in pieces for i in range(2)]
            pieces.append(jnp.zeros((HEAD_ROWS - 4, LANE), f32))
            ref[place, 576 : 576 + HEAD_ROWS, :] = jnp.concatenate(pieces, axis=0).astype(bf16)

    by_destination(r, parts, hand_out)
    arrived(weight_t, sem)

    def input_grad(n, carry):
        cs = lanes(n * CHUNK, CHUNK)
        rows = pl.ds(pl.multiple_of(n * CHUNK, CHUNK), CHUNK)
        for a in range(3):
            lhs = r.sg[(2 - a) * geo.step : (2 - a) * geo.step + geo.rows, :]
            part = dot_nt(lhs, weight_t[a, rows, :])
            r.gg[:, cs] = part if a == 0 else r.gg[:, cs] + part
        return carry

    lax.fori_loop(0, width // CHUNK, input_grad, 0)


def gate_backward(r, geo, prm):
    clear_edges(r.rot, geo, 2)
    own = r.meta[OWN]
    n_pix = pixel_count(r, geo)
    width = r.gg.shape[1]

    def body(c, carry):
        cs = lanes(c * LANE)
        m = r.mask[0]
        inside = r.mask[2]
        for h in range(geo.high):
            at = geo.block(h)
            grad = r.gg[at, cs] * inside
            r.e[at, :] = grad * r.plus[at, cs].astype(f32)
            store_rotated(r.rot, grad * r.slope[at, cs].astype(f32), h, r, geo)
        s1 = jnp.zeros((geo.step, LANE), f32)
        s2 = jnp.zeros((geo.step, LANE), f32)
        for h in range(geo.high):
            at = geo.block(h)
            back = jnp.zeros((geo.step, LANE), f32)
            for a in range(3):
                for b in range(3):
                    near = r.rot[3 - b, (h + 3 - a) * geo.step : (h + 4 - a) * geo.step, :]
                    back = back + near * prm[2 + 3 * a + b : 3 + 3 * a + b, cs]
                    far = r.rot[4 - 2 * b, (h + 4 - 2 * a) * geo.step : (h + 5 - 2 * a) * geo.step, :]
                    back = back + far * prm[11 + 3 * a + b : 12 + 3 * a + b, cs]
            back = back * r.mask[1]
            earlier = jnp.concatenate([jnp.zeros((WPAD, LANE), f32), back[:-WPAD]], axis=0)
            e = (r.e[at, :] + (earlier - back)) * r.d1[at, cs].astype(f32)
            r.e[at, :] = e
            e = e * m
            s1 = s1 + e
            s2 = s2 + e * r.xh1[at, cs].astype(f32)
        shift_grad, gain_grad = column_sum(s1), column_sum(s2)
        scale, mean1, mean2 = r.gr1[0:1, cs], shift_grad / n_pix, gain_grad / n_pix
        for h in range(geo.high):
            at = geo.block(h)
            v = scale * (r.e[at, :] - m * (mean1 + r.xh1[at, cs].astype(f32) * mean2))
            r.fg[at, cs] = v.astype(bf16)

            @pl.when(c == own)
            def _():
                r.fgt[:, h * geo.step : (h + 1) * geo.step] = jnp.transpose(v).astype(bf16)

        @pl.when(c == own)
        def _():
            r.small[SMALL_ROWS - 4 :, :] = jnp.zeros((4, LANE), f32)
            r.small[0:1, :] = gain_grad
            r.small[1:2, :] = shift_grad
            for a in range(3):
                for b in range(3):
                    near = jnp.zeros((geo.step, LANE), f32)
                    far = jnp.zeros((geo.step, LANE), f32)
                    for h in range(geo.high):
                        diff = r.diff[geo.block(h), :]
                        near = near + diff * r.rot[3 - b, (h + 3 - a) * geo.step : (h + 4 - a) * geo.step, :]
                        far = far + diff * r.rot[4 - 2 * b, (h + 4 - 2 * a) * geo.step : (h + 5 - 2 * a) * geo.step, :]
                    r.small[2 + 3 * a + b : 3 + 3 * a + b, :] = column_sum(near)
                    r.small[11 + 3 * a + b : 12 + 3 * a + b, :] = column_sum(far)

        return carry

    lax.fori_loop(0, width // LANE, body, 0)


def first_products(r, geo, x, parts):
    def body(n, ref, place):
        part = dot(r.fgt[...], x[:, lanes(n * CHUNK, CHUNK)])
        for half in range(CHUNK // LANE):
            block = part[:, half * LANE : (half + 1) * LANE]
            ref[place, half * LANE : (half + 1) * LANE, :] = jnp.transpose(block).astype(bf16)

    by_destination(r, parts, body)


def third_backward(r, geo, weight_in, weight_out, act2_t, pg, parts):
    n_pix = pixel_count(r, geo)
    own = r.meta[OWN]
    r.ag2[...] = jnp.zeros_like(r.ag2)
    per_own = r.e3.shape[1] // CHUNK

    def body(n, ref, place):
        ws = lanes(n * CHUNK, CHUNK)
        rows = pl.ds(pl.multiple_of(n * CHUNK, CHUNK), CHUNK)
        r.br[...] = dot_nt(r.fg[...], weight_in[rows, :])
        m = r.mask[0]
        for half in range(CHUNK // LANE):
            ls = slice(half * LANE, (half + 1) * LANE)
            cs = lanes(n * CHUNK + half * LANE)
            grad = pg[0:1, cs]
            s1 = jnp.zeros((geo.step, LANE), f32)
            s2 = jnp.zeros((geo.step, LANE), f32)
            for h in range(geo.high):
                at = geo.block(h)
                out_grad = r.br[at, ls] + r.d3_next[at, cs].astype(f32) * (grad * m)
                e = out_grad * r.d3[at, cs].astype(f32)
                xhat = r.xh3[at, cs].astype(f32)
                r.ee[at, ls] = e
                r.br[at, ls] = xhat
                e = e * m
                s1 = s1 + e
                s2 = s2 + e * xhat
            shift_grad, gain_grad = column_sum(s1), column_sum(s2)
            r.third_grad[0:1, cs] = gain_grad
            r.third_grad[1:2, cs] = shift_grad
            scale, mean1, mean2 = r.gr3[0:1, cs], shift_grad / n_pix, gain_grad / n_pix
            for h in range(geo.high):
                at = geo.block(h)
                v = scale * (r.ee[at, ls] - m * (mean1 + r.br[at, ls] * mean2))
                r.bg[at, ls] = v.astype(bf16)
        owner = n // per_own

        @pl.when(owner == own)
        def _():
            r.e3[:, lanes((n - owner * per_own) * CHUNK, CHUNK)] = r.ee[...]

        third_products(r, geo, act2_t, weight_out, ws, ref, place, 256)

    by_destination(r, parts, body)


class Sizes:
    def __init__(self, geo, inner, wide, order_n):
        self.geo, self.inner, self.wide, self.order_n = geo, inner, wide, order_n

    def mask(self):
        return VM((MASKS, self.geo.step, LANE), f32)

    def rot(self):
        return VM((5, (self.geo.high + 4) * self.geo.step, LANE), f32)

    def narrow(self, dtype=bf16):
        return ((self.geo.rows, self.inner), dtype)

    def broad(self, dtype=bf16):
        return ((self.geo.rows, self.wide), dtype)

    def stacked(self):
        return ((self.geo.rows + 2 * self.geo.step, 3 * self.inner), bf16)

    def parts(self, rows):
        return {"away": ((self.order_n // 2, rows, LANE), bf16), "home": ((self.order_n // 2, rows, LANE), bf16)}


def gate_outs(z):
    return {
        "g": z.stacked(),
        "xh1": z.narrow(),
        "d1": z.narrow(),
        "plus": z.narrow(),
        "slope": z.narrow(),
        "diff": ((z.geo.rows, LANE), f32),
        "gr1": ((1, z.inner), f32),
    }


def gate_scratch(z):
    return {"rot": z.rot(), "act": VM((z.geo.rows, LANE), f32), "mask": z.mask()}


def middle_outs(z):
    return {
        "xh2": z.narrow(),
        "d2": z.narrow(),
        "gr2": ((1, z.inner), f32),
        "act2_t": ((LANE, z.geo.rows), bf16),
    }


def kernel_gate(z, meta, source, x, prm):
    geo = z.geo

    def body(r):
        source.start("in", r, r.w_in, r.sem)
        fill_masks(r, geo)
        arrived(r.w_in, r.sem)
        first_matmul(r, geo, r.x, r.w_in, r.pre)
        gate_forward(r, geo, r.prm, r.pre, r)

    return call(
        "gate_forward",
        body,
        {"meta": (meta, SM), **source.operands(), "x": (x, VM), "prm": (prm, VM)},
        gate_outs(z),
        {
            **gate_scratch(z),
            "w_in": VM((z.wide, z.inner), bf16),
            "pre": VM((geo.rows, z.inner), f32),
            "sem": pltpu.SemaphoreType.DMA,
        },
        flops=16_000_000_000,
        nbytes=16_000_000,
    )


def kernel_block(z, meta, source, g, x, prm, thr):
    geo = z.geo

    def body(r):
        source.start("conv", r, r.w_mid, r.sem)
        source.start("out", r, r.w_out, r.sem2)
        fill_masks(r, geo)
        arrived(r.w_mid, r.sem)
        conv_matmul(r, geo, r.g, r.w_mid, r.pre)
        middle_forward(r, geo, r.prm, r.pre, r.act2, r, r.act2_t)
        arrived(r.w_out, r.sem2)
        third_forward(r, geo, r.thr, r.act2, r.w_out, r.x, r)

    return call(
        "block_forward",
        body,
        {"meta": (meta, SM), **source.operands(), "g": (g, VM), "x": (x, VM), "prm": (prm, VM), "thr": (thr, VM)},
        {
            **middle_outs(z),
            "xh3": z.broad(),
            "d3": z.broad(),
            "x_next": z.broad(),
            "gr3": ((1, z.wide), f32),
        },
        {
            "mask": z.mask(),
            "w_mid": VM((3, 3, z.inner, z.inner), bf16),
            "w_out": VM((z.inner, z.wide), bf16),
            "pre": VM((geo.rows, z.inner), f32),
            "act2": VM((geo.rows, z.inner), bf16),
            "br": VM((geo.rows, CHUNK), f32),
            "sem": pltpu.SemaphoreType.DMA,
            "sem2": pltpu.SemaphoreType.DMA,
        },
        flops=16_000_000_000,
        nbytes=16_000_000,
    )


def kernel_top(z, meta, source, x, prm, thr, grad_low, bias):
    geo = z.geo

    def body(r):
        source.start("in", r, r.w_in, r.sem)
        source.start("conv", r, r.w_mid, r.sem2)
        source.start("out", r, r.w_out, r.sem3)
        source.start("head", r, r.w_head, r.sem4)
        fill_masks(r, geo)
        arrived(r.w_in, r.sem)
        first_matmul(r, geo, r.x, r.w_in, r.pre)
        gate_forward(r, geo, r.prm, r.pre, r)
        arrived(r.w_mid, r.sem2)
        conv_matmul(r, geo, r.g, r.w_mid, r.pre)
        middle_forward(r, geo, r.prm, r.pre, r.act2, r, r.act2_t)
        arrived(r.w_out, r.sem3)
        arrived(r.w_head, r.sem4)
        n_pix = pixel_count(r, geo)
        r.pg[...] = dot_nt(r.grad[...], r.w_head[...])[0:1] / n_pix
        third_both(r, geo, r.thr, r.act2, r.act2_t, r.w_out, r.x, r.pg, [r.away, r.home])
        low = jnp.broadcast_to(r.pooled[...].astype(bf16), (16, z.wide))
        r.logits[...] = dot(low, r.w_head[...])[0:8] + r.bias[...]

    return call(
        "top_both",
        body,
        {
            "meta": (meta, SM),
            **source.operands(),
            "x": (x, VM),
            "prm": (prm, VM),
            "thr": (thr, VM),
            "grad": (grad_low, VM),
            "bias": (bias, VM),
        },
        {
            **gate_outs(z),
            **middle_outs(z),
            "d3": z.broad(),
            "pooled": ((1, z.wide), f32),
            "pg": ((1, z.wide), f32),
            "logits": ((8, bias.shape[1]), f32),
            "third_grad": ((2, z.wide), f32),
            "ag2": z.narrow(f32),
            **z.parts(256),
        },
        {
            **gate_scratch(z),
            "w_in": VM((z.wide, z.inner), bf16),
            "w_mid": VM((3, 3, z.inner, z.inner), bf16),
            "w_out": VM((z.inner, z.wide), bf16),
            "w_head": VM((z.wide, bias.shape[1]), bf16),
            "pre": VM((geo.rows, z.inner), f32),
            "act2": VM((geo.rows, z.inner), bf16),
            "br": VM((geo.rows, CHUNK), f32),
            "e": VM((geo.rows, CHUNK), f32),
            "bg": VM((geo.rows, CHUNK), bf16),
            "sem": pltpu.SemaphoreType.DMA,
            "sem2": pltpu.SemaphoreType.DMA,
            "sem3": pltpu.SemaphoreType.DMA,
            "sem4": pltpu.SemaphoreType.DMA,
        },
        flops=40_000_000_000,
        nbytes=30_000_000,
    )


def kernel_conv_back(z, meta, source, ag2, kept, grad_low=None):
    geo = z.geo
    top = grad_low is not None
    extra = {"pooled": (kept["pooled"], VM), "grad": (grad_low, VM)} if top else {}

    def body(r):
        source.start("conv_t", r, r.w_t, r.sem)
        fill_masks(r, geo)
        conv_backward(r, geo, r.w_t, r.sem, [r.away, r.home], top)

    return call(
        "conv_backward",
        body,
        {
            "meta": (meta, SM),
            **source.operands(),
            "ag2": (ag2, VM),
            "xh2": (kept["xh2"], VM),
            "d2": (kept["d2"], VM),
            "gr2": (kept["gr2"], VM),
            "g": (kept["g"], VM),
            **extra,
        },
        {"gg": z.narrow(f32), "small": ((2, LANE), f32), **z.parts(576 + (HEAD_ROWS if top else 0))},
        {
            "mask": z.mask(),
            "w_t": VM((3, z.inner, 3 * z.inner), bf16),
            "sg": VM(*z.stacked()),
            "sgt": VM((3 * LANE, geo.rows), bf16),
            "wg": VM((9, z.inner, LANE), f32),
            "e": VM((geo.rows, LANE), f32),
            "sem": pltpu.SemaphoreType.DMA,
        },
        flops=20_000_000_000,
        nbytes=16_000_000,
    )


def gate_back_ins(kept, prm):
    ins = {name: (kept[name], VM) for name in ("xh1", "d1", "plus", "slope", "diff", "gr1")}
    ins["prm"] = (prm, VM)
    return ins


def gate_back_scratch(z):
    return {
        "mask": z.mask(),
        "rot": z.rot(),
        "e": VM((z.geo.rows, LANE), f32),
        "fg": VM(*z.narrow()),
        "fgt": VM((LANE, z.geo.rows), bf16),
        "w_in": VM((z.wide, z.inner), bf16),
        "sem": pltpu.SemaphoreType.DMA,
    }


def kernel_join(z, meta, source, source_below, gg, kept, below, prm, x, d3_next, pg):
    geo = z.geo
    both = {}
    for tag, item in (("a_", source), ("b_", source_below)):
        both.update({tag + name: value for name, value in item.operands().items()})

    def view(r, tag):
        picked = {k[2:]: v for k, v in vars(r).items() if k.startswith(tag)}
        return types.SimpleNamespace(**picked)

    def body(r):
        source.start("in", view(r, "a_"), r.w_in, r.sem)
        source_below.start("out", view(r, "b_"), r.w_out, r.sem2)
        fill_masks(r, geo)
        gate_backward(r, geo, r.prm)
        first_products(r, geo, r.x, [r.away, r.home])
        arrived(r.w_in, r.sem)
        arrived(r.w_out, r.sem2)
        third_backward(r, geo, r.w_in, r.w_out, r.act2_t, r.pg, [r.away, r.home])

    return call(
        "join_backward",
        body,
        {
            "meta": (meta, SM),
            **both,
            "gg": (gg, VM),
            **gate_back_ins(kept, prm),
            "x": (x, VM),
            "d3_next": (d3_next, VM),
            "pg": (pg, VM),
            "d3": (below["d3"], VM),
            "xh3": (below["xh3"], VM),
            "gr3": (below["gr3"], VM),
            "act2_t": (below["act2_t"], VM),
        },
        {
            "small": ((SMALL_ROWS, LANE), f32),
            "third_grad": ((2, z.wide), f32),
            "ag2": z.narrow(f32),
            "e3": ((geo.rows, z.wide // 4), f32),
            **z.parts(512),
        },
        {
            **gate_back_scratch(z),
            "w_out": VM((z.inner, z.wide), bf16),
            "br": VM((geo.rows, CHUNK), f32),
            "ee": VM((geo.rows, CHUNK), f32),
            "bg": VM((geo.rows, CHUNK), bf16),
            "sem2": pltpu.SemaphoreType.DMA,
        },
        flops=20_000_000_000,
        nbytes=30_000_000,
    )


def kernel_bottom(z, meta, source, gg, kept, prm, x, e3, smalls):
    geo = z.geo
    quarter = e3.shape[1]

    def body(r):
        source.start("in", r, r.w_in, r.sem)
        fill_masks(r, geo)
        gate_backward(r, geo, r.prm)
        first_products(r, geo, r.x, [r.away, r.home])
        arrived(r.w_in, r.sem)
        own = r.meta[OWN]
        both = jnp.concatenate([r.small[...], r.smalls[...]], axis=0).astype(bf16)
        for ref in (r.away, r.home):
            for place in range(ref.shape[0]):
                ref[place, 256:, :] = both
        for n in range(quarter // CHUNK):
            cs = slice(n * CHUNK, (n + 1) * CHUNK)
            rows = pl.ds(pl.multiple_of(own * quarter + n * CHUNK, CHUNK), CHUNK)
            r.x_grad[:, cs] = (dot_nt(r.fg[...], r.w_in[rows, :]) + r.e3[:, cs]).astype(bf16)

    return call(
        "bottom_backward",
        body,
        {
            "meta": (meta, SM),
            **source.operands(),
            "gg": (gg, VM),
            **gate_back_ins(kept, prm),
            "x": (x, VM),
            "e3": (e3, VM),
            "smalls": (smalls, VM),
        },
        {"x_grad": ((geo.rows, quarter), bf16), **z.parts(256 + SMALL_ROWS + smalls.shape[0])},
        {**gate_back_scratch(z), "small": VM((SMALL_ROWS, LANE), f32)},
        flops=10_000_000_000,
        nbytes=16_000_000,
    )


def fold(recv, home, stack_rows=0):
    slots, rows, _ = home.shape
    added = rows - stack_rows

    def body(r):
        for k in range(slots):
            out = getattr(r, f"s{k}")
            out[:added] = (r.recv[k, :added].astype(f32) + r.home[k, :added].astype(f32)).astype(bf16)
            if stack_rows:
                out[added:rows] = r.home[k, added:]
                out[rows:] = r.recv[k, added:]

    outs = {f"s{k}": ((rows + stack_rows, LANE), bf16) for k in range(slots)}
    done = call("fold", body, {"recv": (recv, VM), "home": (home, VM)}, outs, {}, nbytes=4_000_000)
    return [done[f"s{k}"] for k in range(slots)]


class Grid:
    def __init__(self, clip_n, chan_n):
        self.clip_n, self.chan_n = clip_n, chan_n
        self.z_n = clip_n // 2

    def across_x(self, value):
        return lax.ppermute(value, "clip", [(i, i ^ 1) for i in range(self.clip_n)])

    def along_z(self, value, k):
        return lax.ppermute(value, "clip", [(i, (i + 2 * k) % self.clip_n) for i in range(self.clip_n)])

    def across_y(self, value):
        return lax.ppermute(value, "chan", [(i, i ^ 2) for i in range(self.chan_n)])

    def across_core(self, value):
        return lax.ppermute(value, "chan", [(i, i ^ 1) for i in range(self.chan_n)])

    def scatter(self, away, home, stack_rows=0):
        shares = fold(self.across_x(away), home, stack_rows)
        return [shares[0]] + [self.along_z(shares[k], k) for k in range(1, self.z_n)]

    def gather(self, own, cut):
        clip, chan = lax.axis_index("clip"), lax.axis_index("chan")
        column = jnp.stack([own] + [self.along_z(own, k) for k in range(1, self.z_n)])
        over_x, over_y = self.across_x(column), self.across_y(column)
        low = self.across_y(over_x[:, :cut])
        high = self.across_x(over_y[:, cut:])
        arrays = [column, over_x, over_y, low, high]
        arrays = arrays + [self.across_core(item) for item in arrays]
        z, x = clip // 2, clip % 2
        column_z = (z + self.z_n - jnp.arange(self.z_n, dtype=jnp.int32)) % self.z_n
        clips, chans = [], []
        for core in (0, 1):
            for dx, dy in ((0, 0), (1, 0), (0, 2), (1, 2), (1, 2)):
                clips.append(column_z * 2 + (x ^ dx))
                chans.append(jnp.full((self.z_n,), 1, jnp.int32) * (chan ^ dy ^ core))
        devices = jnp.stack([jnp.concatenate(clips), jnp.concatenate(chans)]).astype(jnp.int32)
        whole = [0, 1, 2, 5, 6, 7]
        return arrays, devices, whole, [3, 8], [4, 9]


def four(shares):
    a, b, c, d = [v.astype(f32) for v in shares]
    return (a + c) + (b + d)


def local(
    clip_input,
    seg_count,
    proj_in_master,
    conv_master,
    proj_out_master,
    head_master,
    gain_first,
    shift_first,
    taps_near,
    taps_far,
    gain_second,
    shift_second,
    gain_third,
    shift_third,
    head_bias,
    logit_grad,
    clip_n,
    chan_n,
):
    clip = lax.axis_index("clip")
    chan = lax.axis_index("chan")
    _, seg, high_map, wide_map, wide = clip_input.shape
    layers = proj_in_master.shape[0]
    inner = proj_in_master.shape[2] * chan_n
    classes = head_master.shape[1]
    class_pad = -(-classes // LANE) * LANE
    geo = Geometry(seg, high_map, wide_map)
    order_n = wide // CHUNK
    z = Sizes(geo, inner, wide, order_n)

    direct = clip_n == 8 and chan_n == 4 and proj_in_master.shape[1] == 256
    grid = Grid(clip_n, chan_n)

    own_small = jnp.concatenate(
        [
            gain_first[:, None],
            shift_first[:, None],
            taps_near.reshape(layers, 9, -1),
            taps_far.reshape(layers, 9, -1),
            gain_second[:, None],
            shift_second[:, None],
            gain_third.reshape(layers, -1, LANE),
            shift_third.reshape(layers, -1, LANE),
        ],
        axis=1,
    )
    if direct:
        empty = jnp.zeros((chan_n,) + own_small.shape, f32)
        all_small = lax.dynamic_update_slice_in_dim(empty, own_small[None], chan, 0)
        all_small = all_small + grid.across_y(all_small)
        all_small = all_small + grid.across_core(all_small)
    else:
        all_small = lax.all_gather(own_small, "chan", axis=0, tiled=False)
    prm = jnp.transpose(all_small[:, :, :22], (1, 2, 0, 3)).reshape(layers, 22, inner)
    thr = jnp.transpose(all_small[:, :, 22:].reshape(chan_n, layers, 2, -1), (1, 2, 0, 3)).reshape(
        layers, 2, wide
    )

    head_low = jnp.pad(head_master.astype(bf16), ((0, 0), (0, class_pad - classes)))
    if direct:
        own_head = lax.dynamic_slice_in_dim(head_low, chan * 64, 64, 0)
        own_head = jnp.transpose(own_head.reshape(64, 2, LANE), (1, 0, 2)).reshape(128, LANE)
        in_low = [proj_in_master[layer].astype(bf16) for layer in range(layers)]
        mid_low = [conv_master[layer].astype(bf16).reshape(-1, LANE) for layer in range(layers)]
        out_low = [proj_out_master[layer].astype(bf16).reshape(LANE, 2, LANE) for layer in range(layers)]
        out_low = [jnp.transpose(item, (1, 0, 2)).reshape(256, LANE) for item in out_low]
        arrays, devices, full, low, high = grid.gather(in_low[0], 128)
        parts = {"in": [(i, 0, 0, 256) for i in full]}
        parts["in"] += [(i, 0, 0, 128) for i in low] + [(i, 0, 128, 128) for i in high]
        in_source = Slots(arrays, devices, parts, chan_n)
        arrays, devices, full, low, high = grid.gather(jnp.concatenate([mid_low[0], out_low[0]]), 384)
        parts = {
            "conv": [(i, 0, 0, 3) for i in full] + [(i, 0, 0, 2) for i in low] + [(i, 0, 2, 1) for i in high],
            "out": [(i, 576, 0, 2) for i in full] + [(i, 192, 0, 2) for i in high],
        }
        parts["conv_t"] = parts["conv"]
        rest_source = Slots(arrays, devices, parts, chan_n)
        packed = jnp.concatenate([in_low[1], mid_low[1], out_low[1], own_head], axis=0)
        packed = lax.all_gather(packed, ("clip", "chan"), axis=0, tiled=False)
        numbers = jnp.arange(clip_n * chan_n, dtype=jnp.int32)
        devices = jnp.stack([numbers // chan_n, numbers % chan_n])
        parts = {
            "in": [(0, 0, 0, 256)],
            "conv": [(0, 256, 0, 3)],
            "conv_t": [(0, 256, 0, 3)],
            "out": [(0, 832, 0, 2)],
            "head": [(0, 1088, 0, 2)],
        }
        top_source = Slots([packed], devices, parts, chan_n)
    else:
        whole_head = lax.all_gather(head_low, "clip", axis=0, tiled=True)
        gathered = []
        for master, clip_axis, chan_axis in ((proj_in_master, 1, 2), (conv_master, 3, 4), (proj_out_master, 2, 1)):
            item = lax.all_gather(master.astype(bf16), "clip", axis=clip_axis, tiled=True)
            gathered.append(lax.all_gather(item, "chan", axis=chan_axis, tiled=True))
        in_source = rest_source = Whole(
            {"in": gathered[0][0], "conv": gathered[1][0], "out": gathered[2][0], "head": whole_head}
        )
        top_source = Whole(
            {"in": gathered[0][1], "conv": gathered[1][1], "out": gathered[2][1], "head": whole_head}
        )

    order = jnp.arange(order_n, dtype=jnp.int32)
    if direct:
        z_to = (clip // 2 + jnp.arange(4, dtype=jnp.int32)) % 4
        order = jnp.concatenate([z_to * 2 + ((clip % 2) ^ 1), z_to * 2 + clip % 2]).astype(jnp.int32)
    meta = jnp.concatenate([seg_count.astype(jnp.int32), chan[None].astype(jnp.int32), order])

    grad_low = logit_grad.astype(bf16)
    grad_rows = jnp.pad(grad_low, ((0, 15), (0, class_pad - classes)))
    bias_row = jnp.pad(head_bias, (0, class_pad - classes))[None]

    x0 = jnp.transpose(clip_input[0], (1, 0, 2, 3))
    x0 = jnp.pad(x0, ((0, 0), (0, 0), (0, WPAD - wide_map), (0, 0))).reshape(geo.rows, wide)

    gate0 = kernel_gate(z, meta, in_source, x0, prm[0])
    block0 = kernel_block(z, meta, rest_source, gate0["g"], x0, prm[0], thr[0])
    x1 = block0["x_next"]
    top = kernel_top(z, meta, top_source, x1, prm[1], thr[1], grad_rows, bias_row)
    mid1 = kernel_conv_back(z, meta, top_source, top["ag2"], top, grad_rows)
    join = kernel_join(
        z, meta, top_source, rest_source, mid1["gg"], top, block0, prm[1], x1, top["d3"], top["pg"]
    )
    mid0 = kernel_conv_back(z, meta, rest_source, join["ag2"], {**gate0, **block0})
    third = jnp.stack([join["third_grad"], top["third_grad"]])
    third = lax.dynamic_slice_in_dim(third, chan * (wide // chan_n), wide // chan_n, 2)
    third_rows = wide // chan_n // LANE
    smalls = [join["small"], mid0["small"], mid1["small"], third.reshape(-1, LANE)]
    smalls = jnp.concatenate(smalls, axis=0)
    smalls = jnp.pad(smalls, ((0, -smalls.shape[0] % 16 + 8), (0, 0)))
    low = kernel_bottom(z, meta, in_source, mid0["gg"], gate0, prm[0], x0, join["e3"], smalls)

    logits = top["logits"][0:1, :classes]
    input_grad = low["x_grad"].reshape(high_map, seg, WPAD, -1)[:, :, :wide_map]
    input_grad = jnp.transpose(input_grad, (1, 0, 2, 3))[None]

    if direct:
        out1 = four(grid.scatter(top["away"], top["home"]))
        mid1_shares = grid.scatter(mid1["away"], mid1["home"], HEAD_ROWS)
        joined = four(grid.scatter(join["away"], join["home"]))
        mid0_sum = four(grid.scatter(mid0["away"], mid0["home"]))
        last = four(grid.scatter(low["away"], low["home"]))
        in_share = jnp.stack([last[:256], joined[:256]])
        mid_share = jnp.stack([mid0_sum, four([v[:576] for v in mid1_shares])])
        mid_share = mid_share.reshape(conv_master.shape)
        out_share = jnp.stack([joined[256:], out1]).reshape(layers, 2, LANE, LANE)
        out_share = jnp.transpose(out_share, (0, 2, 1, 3)).reshape(proj_out_master.shape)
        small = last[256:]
        heads = jnp.stack([v[576:].reshape(2, HEAD_ROWS, LANE)[:, :4] for v in mid1_shares])
        heads = heads.reshape(8, 4, LANE)
        pooled_all, grad_all = heads[:, :2].reshape(8, 256), heads[:, 2:].reshape(8, 256)[:, :classes]
        head_share = lax.dot_general(
            pooled_all, grad_all, (((0,), (0,)), ((), ())), preferred_element_type=f32
        )
        g = grad_all.astype(f32)
        g = g[0::2] + g[1::2]
        bias_grad = (g[0] + g[2]) + (g[1] + g[3])
    else:
        pooled_all = lax.all_gather(top["pooled"].astype(bf16), "clip", axis=0, tiled=True)
        grad_all = lax.all_gather(grad_low, "clip", axis=0, tiled=True)
        own_rows = head_master.shape[0]
        pooled_own = lax.dynamic_slice_in_dim(pooled_all, clip * own_rows, own_rows, 1)
        head_share = lax.dot_general(
            pooled_own, grad_all, (((0,), (0,)), ((), ())), preferred_element_type=f32
        )
        bias_grad = jnp.sum(grad_all.astype(f32), axis=0)

        def joined(item, first, rows):
            return jnp.concatenate([item["away"], item["home"]], axis=0)[:, first : first + rows]

        in_terms = jnp.stack([joined(low, 0, 256), joined(join, 0, 256)]).reshape(layers, wide, LANE)
        mid_terms = jnp.stack([joined(mid0, 0, 576), joined(mid1, 0, 576)])
        mid_terms = mid_terms.reshape(layers, order_n, 3, 3, 64, LANE)
        mid_terms = jnp.transpose(mid_terms, (0, 2, 3, 1, 4, 5)).reshape(layers, 3, 3, inner, LANE)
        out_terms = jnp.stack([joined(join, 256, 256), joined(top, 0, 256)])
        out_terms = out_terms.reshape(layers, order_n, 2, LANE, LANE)
        out_terms = jnp.transpose(out_terms, (0, 3, 1, 2, 4)).reshape(layers, LANE, wide)
        in_share = lax.psum_scatter(in_terms, "clip", scatter_dimension=1, tiled=True).astype(f32)
        mid_share = lax.psum_scatter(mid_terms, "clip", scatter_dimension=3, tiled=True).astype(f32)
        out_share = lax.psum_scatter(out_terms, "clip", scatter_dimension=2, tiled=True).astype(f32)
        small = lax.psum(low["home"][0, 256:].astype(f32), "clip")
    firsts = small[: 2 * SMALL_ROWS].reshape(2, SMALL_ROWS, LANE)
    seconds = small[2 * SMALL_ROWS : 2 * SMALL_ROWS + 4].reshape(2, 2, LANE)
    thirds = small[2 * SMALL_ROWS + 4 : 2 * SMALL_ROWS + 4 + 4 * third_rows].reshape(2, 2, -1)
    return (
        logits,
        input_grad,
        in_share,
        mid_share,
        out_share,
        head_share,
        firsts[:, 0],
        firsts[:, 1],
        firsts[:, 2:11].reshape(taps_near.shape),
        firsts[:, 11:20].reshape(taps_far.shape),
        seconds[:, 0],
        seconds[:, 1],
        thirds[:, 0],
        thirds[:, 1],
        bias_grad,
    )


def solution(mesh):
    clip_n, chan_n = mesh.shape["clip"], mesh.shape["chan"]

    def program(*args):
        return local(*args, clip_n, chan_n)

    in_specs = (
        P("clip", None, None, None, None),
        P("clip"),
        P(None, "clip", "chan"),
        P(None, None, None, "clip", "chan"),
        P(None, "chan", "clip"),
        P("clip", None),
        P(None, "chan"),
        P(None, "chan"),
        P(None, None, None, "chan"),
        P(None, None, None, "chan"),
        P(None, "chan"),
        P(None, "chan"),
        P(None, "chan"),
        P(None, "chan"),
        P(),
        P("clip", None),
    )
    out_specs = (
        P("clip", None),
        P("clip", None, None, None, "chan"),
        P(None, "clip", "chan"),
        P(None, None, None, "clip", "chan"),
        P(None, "chan", "clip"),
        P("clip", None),
        P(None, "chan"),
        P(None, "chan"),
        P(None, None, None, "chan"),
        P(None, None, None, "chan"),
        P(None, "chan"),
        P(None, "chan"),
        P(None, "chan"),
        P(None, "chan"),
        P(),
    )
    return jax.shard_map(program, mesh=mesh, in_specs=in_specs, out_specs=out_specs, check_vma=False)
```

```python
import types

import jax
import jax.numpy as jnp
from jax import lax
from jax.experimental import pallas as pl
from jax.experimental.pallas import tpu as pltpu
from jax.sharding import PartitionSpec as P

EPS = 1e-05
LANE = 128
CHUNK = 256
SMALL_ROWS = 24
HEAD_ROWS = 16
HEAD_PART = 48
SLOT = 32
MASKS = 3
CLIP, CHAN = "clip", "chan"
bf16 = jnp.bfloat16
f32 = jnp.float32


VM = pltpu.VMEM
SM = pltpu.SMEM
HB = pl.ANY
LATE = object()
SLICED = object()
ORDERED = object()
COUNT, OWN, ORDER = 0, 1, 2
Space = types.SimpleNamespace


def _bytes(shape, dtype):
    size = jnp.dtype(dtype).itemsize
    for extent in shape:
        size *= extent
    return size


def _flat(items):
    flat, groups = {}, {}
    for name, item in items.items():
        if isinstance(item, list):
            groups[name] = [name + str(i) for i in range(len(item))]
            flat.update(zip(groups[name], item))
        else:
            flat[name] = item
    return flat, groups


def call(name, body, ins, outs, scratch, flops=0, nbytes=0, after=(), kept=(), direct=False, limit=60):
    ins, in_groups = _flat(dict(ins, unread=[(item, HB) for item in after]))
    outs, out_groups = _flat(outs)
    in_names, out_names = list(ins), list(outs)

    def kind(space):
        return [n for n in in_names if ins[n][1] is space]

    sliced, late, ordered = kind(SLICED), kind(LATE), kind(ORDERED)
    early = [n for n in out_names if _bytes(*outs[n]) > 65536 and n not in kept and not direct]
    part = {n: ins[n][2] for n in late if len(ins[n]) > 2}
    extra = dict(scratch)
    sems = {}
    for n in sliced + late + ordered:
        shape = ins[n][0].shape
        extra[n] = VM(shape[1:] if n in part else shape, ins[n][0].dtype)
        count = {id(SLICED): shape[-1] // LANE, id(ORDERED): shape[-1] // CHUNK}.get(id(ins[n][1]), 1)
        sems[n] = pltpu.SemaphoreType.DMA((count,))
    for n in early:
        extra[n] = VM(*outs[n])
        sems[n] = pltpu.SemaphoreType.DMA((1,))
    extra_names, sem_names = list(extra), list(sems)

    def kernel(*refs):
        outer = dict(zip(in_names + out_names, refs))
        refs = refs[len(outer) :]
        inner = dict(zip(extra_names, refs))
        sem = dict(zip(sem_names, refs[len(inner) :]))
        every = {**outer, **inner}
        r = Space(**every)
        for group, names in {**in_groups, **out_groups}.items():
            setattr(r, group, [every[n] for n in names])

        def slice_copy(n, c, size):
            cs = lanes(c * size, size)
            return pltpu.make_async_copy(outer[n].at[:, cs], inner[n].at[:, cs], sem[n].at[c])

        def whole_copy(n):
            ref = outer[n].at[part[n]] if n in part else outer[n]
            return pltpu.make_async_copy(ref, inner[n], sem[n].at[0])

        def start_rest():
            if ordered:
                each = ins[ordered[0]][0].shape[1] // CHUNK // 2
                for j in range(each):
                    for p in range(2):
                        for n in ordered:
                            slice_copy(n, r.meta[ORDER + p * each + j], CHUNK).start()
            for n in late:
                whole_copy(n).start()

        def ready_lanes(c):
            for n in sliced:
                slice_copy(n, c, LANE).wait()

        def ready_chunk(chunk):
            for n in ordered:
                slice_copy(n, chunk, CHUNK).wait()

        def ready(n):
            whole_copy(n).wait()

        def push(n, *index):
            if n not in early:
                return
            src, dst = (inner[n].at[index], outer[n].at[index]) if index else (inner[n], outer[n])
            pltpu.make_async_copy(src, dst, sem[n].at[0]).start()

        r.ready, r.ready_lanes, r.ready_chunk, r.push = ready, ready_lanes, ready_chunk, push
        r.start_rest = start_rest
        for c in range(ins[sliced[0]][0].shape[1] // LANE if sliced else 0):
            for n in sliced:
                slice_copy(n, c, LANE).start()
        if not ordered:
            start_rest()
        body(r)
        for n in early:
            pltpu.make_async_copy(inner[n], outer[n], sem[n].at[0]).wait()

    own = (LATE, SLICED, ORDERED)
    results = pl.pallas_call(
        kernel,
        name=name,
        out_shape=[jax.ShapeDtypeStruct(*outs[n]) for n in out_names],
        in_specs=[pl.BlockSpec(memory_space=HB if ins[n][1] in own else ins[n][1]) for n in in_names],
        out_specs=[pl.BlockSpec(memory_space=HB if n in early else VM) for n in out_names],
        scratch_shapes=[extra[n] for n in extra_names] + [sems[n] for n in sem_names],
        compiler_params=pltpu.CompilerParams(vmem_limit_bytes=limit * 1024 * 1024),
        cost_estimate=pl.CostEstimate(flops=flops, bytes_accessed=nbytes, transcendentals=0),
    )(*[ins[n][0] for n in in_names])
    done = dict(zip(out_names, results))
    for group, names in out_groups.items():
        done[group] = [done[n] for n in names]
    return Space(**done)


def lanes(start, size=LANE):
    return pl.ds(pl.multiple_of(start, LANE), size)


def rows_at(start, size, unit):
    return pl.ds(pl.multiple_of(start, unit), size)


def dot(a, b):
    return jnp.dot(a, b, preferred_element_type=f32)


def dot_nt(a, b):
    return lax.dot_general(a, b, (((1,), (1,)), ((), ())), preferred_element_type=f32)


def dot_tn(a, b):
    return lax.dot_general(a, b, (((0,), (0,)), ((), ())), preferred_element_type=f32)


class Geometry:
    def __init__(self, seg, high, wide):
        self.seg, self.high, self.wide = seg, high, wide
        self.step = seg * wide
        self.rows = high * self.step

    def slab(self, h, w, first=0):
        start = first + (h * self.wide + w) * self.seg
        return slice(start, start + self.seg)

    def slabs(self):
        for h in range(self.high):
            for w in range(self.wide):
                yield self.slab(h, w), h, w


def fill_masks(r, geo):
    count = r.meta[COUNT]
    seg = lax.broadcasted_iota(jnp.int32, (geo.seg, LANE), 0)
    r.mask[0] = jnp.where(seg < count, 1.0, 0.0)
    r.mask[1] = jnp.where(seg + 1 < count, 1.0, 0.0)
    r.mask[2] = jnp.where(seg + 1 < count, 0.5, 0.0)


def pixel_count(r, geo):
    return r.meta[COUNT].astype(f32) * float(geo.high * geo.wide)


def column_sum(v):
    return jnp.sum(v, axis=0, keepdims=True)


def zeros8():
    return jnp.zeros((8, LANE), f32)


def eights(v):
    return jnp.sum(v.reshape(v.shape[0] // 8, 8, LANE), axis=0)


def statistics(pre, cs, r, geo):
    n = pixel_count(r, geo)
    pilot = pre[0:1, cs]
    s1, s2 = zeros8(), zeros8()
    m = r.mask[0]
    for at, _, _ in geo.slabs():
        v = (pre[at, cs] - pilot) * m
        s1 = s1 + eights(v)
        s2 = s2 + eights(v * v)
    shift = column_sum(s1) / n
    var = jnp.maximum(column_sum(s2) / n - shift * shift, 0.0)
    return pilot + shift, lax.rsqrt(var + EPS)


def norm_back(n, gain, shift, s1, total, c):
    gain_grad = (c * total - shift * s1) / gain
    k1 = gain_grad / (n * gain)
    return gain_grad, s1 / n - shift * k1, c * k1


IN, CONV, CONV_T, OUT, HEAD, IN_OWN, CONV_OWN, IN_ROWS, CONV_ROWS = range(9)


class Slots:
    def __init__(self, name, arrays, devices, parts, chan_n):
        self.name, self.arrays, self.devices, self.parts, self.chan_n = name, arrays, devices, parts, chan_n

    def operands(self):
        return {self.name: [(array, HB) for array in self.arrays], self.name + "_": (self.devices, SM)}

    def start(self, kind, r, dst, sem):
        refs, devices = getattr(r, self.name), getattr(r, self.name + "_")
        own = r.meta[OWN]
        for no, row0, first, many in self.parts[kind]:
            ref = refs[no]
            base = sum(array.shape[0] for array in self.arrays[:no])

            def body(s, carry, ref=ref, base=base, row0=row0, first=first, many=many):
                clip, chan = devices[0, base + s], devices[1, base + s]

                def copy(src, to):
                    pltpu.make_async_copy(src, to, sem).start()

                if kind in (IN, IN_OWN, IN_ROWS):
                    start = clip * 256 + first - (own * 512 if kind == IN_ROWS else 0)
                    cs = slice(None) if kind == IN_OWN else lanes(chan * LANE)
                    copy(ref.at[s, pl.ds(row0, many)], dst.at[rows_at(start, many, LANE), cs])
                elif kind in (CONV, CONV_OWN, CONV_T, CONV_ROWS):
                    rows = rows_at(clip * 64 - (own * LANE if kind == CONV_ROWS else 0), 64, 64)
                    src = ref.at[s, pl.ds(row0, many * 192)].reshape(many, 3, 64, LANE)
                    taps = pl.ds(first, many)
                    if kind == CONV:
                        copy(src, dst.at[taps, :, rows, lanes(chan * LANE)])
                    elif kind == CONV_OWN:
                        copy(src, dst.at[taps, :, rows, :])
                    else:
                        for b in range(3):
                            copy(src.at[:, b], dst.at[taps, rows, lanes(chan * LANE + b * 512)])
                elif kind == OUT:
                    for half in range(first, first + many):
                        src = ref.at[s, pl.ds(row0 + (half - first) * LANE, LANE)]
                        copy(src, dst.at[rows_at(chan * LANE, LANE, LANE), lanes(clip * 256 + half * LANE)])
                else:
                    rows = rows_at(chan * HEAD_PART, HEAD_PART, 16)
                    for half in range(2):
                        src = ref.at[s, pl.ds(row0 + half * HEAD_PART, HEAD_PART)]
                        copy(src, dst.at[rows, lanes(clip * 256 + half * LANE)])
                return carry

            lax.fori_loop(0, self.arrays[no].shape[0], body, 0)

    def wait_head(self, dst, sem):
        rows = self.chan_n * HEAD_PART
        dst[rows:, :] = jnp.zeros((dst.shape[0] - rows, dst.shape[1]), dst.dtype)
        arrived(dst.at[:rows], sem)


class Whole:
    def __init__(self, name, arrays):
        self.name, self.arrays = name, arrays

    def operands(self):
        return {self.name: [(array, HB) for array in self.arrays.values()]}

    def start(self, kind, r, dst, sem):
        stored = {CONV_T: CONV}.get(kind, kind)
        ref = getattr(r, self.name)[list(self.arrays).index(stored)]
        if kind in (CONV_T, CONV_ROWS):
            for b in range(3):
                pltpu.make_async_copy(ref.at[:, b], dst.at[:, :, pl.ds(b * 512, 512)], sem).start()
        else:
            pltpu.make_async_copy(ref, dst, sem).start()

    def wait_head(self, dst, sem):
        arrived(dst, sem)


def arrived(dst, sem):
    pltpu.make_async_copy(dst, dst, sem).wait()


def first_matmul(r, geo, x, weight, pre):
    pre[...] = dot(x[...], weight[...])


def conv_matmul(r, geo, g, weight, pre):
    total = None
    for a in range(3):
        w = weight[a].reshape(-1, pre.shape[1])
        part = dot(g[a * geo.step : a * geo.step + geo.rows, :], w)
        total = part if total is None else total + part
    pre[...] = total


def clear_border(ref, geo, width, left, right):
    zero = jnp.zeros((geo.step, ref.shape[1]), ref.dtype)
    ref[: geo.step, :] = zero
    ref[geo.rows + geo.step :, :] = zero
    side = jnp.zeros((geo.seg, width), ref.dtype)
    for h in range(geo.high):
        ref[geo.slab(h, 0, geo.step), left * width : (left + 1) * width] = side
        ref[geo.slab(h, geo.wide - 1, geo.step), right * width : (right + 1) * width] = side


def store_shifted(ref, value, h, w, c, width, geo, sign):
    value = value.astype(bf16)
    for b in range(3):
        to = w - sign * (b - 1)
        if 0 <= to < geo.wide:
            ref[geo.slab(h, to, geo.step), lanes(b * width + c * LANE)] = value


def taps_sum(field, prm, cs, h, w, geo, sign):
    total = None
    for a in range(3):
        for b in range(3):
            for first, reach in ((2, 1), (11, 2)):
                dh, dw = h + sign * reach * (a - 1), w + sign * reach * (b - 1)
                if not (0 <= dh < geo.high and 0 <= dw < geo.wide):
                    continue
                term = field[geo.slab(dh, dw), :] * prm[first + 3 * a + b : first + 1 + 3 * a + b, cs]
                total = term if total is None else total + term
    return total


def silu_parts(half):
    t = jnp.tanh(half)
    out = half * t + half
    return out, (1.0 + out) + t * (1.0 - out)


def gate_forward(r, geo, prm, pre):
    width = pre.shape[1]
    whole = width > LANE
    own = r.meta[OWN] if whole else 0
    if whole:
        clear_border(r.g, geo, width, 0, 2)

    def body(c, carry):
        cs = lanes(c * LANE)
        mean, rr = statistics(pre, cs, r, geo)
        gain, shift = prm[0:1, cs], prm[1:2, cs]
        scale = gain * rr
        r.gr1[0:1, cs] = scale
        mul = 0.5 * scale
        add = 0.5 * shift - mean * mul
        next_valid = r.mask[1]
        for at, _, _ in geo.slabs():
            half = pre[at, cs] * mul + add
            act, slope = silu_parts(half)
            r.h1[at, cs] = half.astype(bf16)
            r.d1[at, cs] = slope.astype(bf16)
            r.act[at, :] = act
            r.field[at, :] = (pltpu.roll(act, geo.seg - 1, axis=0) - act) * next_valid

        @pl.when(c == own)
        def _():
            r.diff[...] = r.field[...]

        for at, h, w in geo.slabs():
            t = jnp.tanh(taps_sum(r.field, prm, cs, h, w, geo, 1))
            act = r.act[at, :]
            plus = 1.5 + 0.5 * t
            r.plus[at, cs] = plus.astype(bf16)
            r.slope[at, cs] = (act - act * (t * t)).astype(bf16)
            if whole:
                store_shifted(r.g, act * plus, h, w, c, width, geo, 1)
            else:
                r.gated[at, :] = (act * plus).astype(bf16)
        for name in ("h1", "d1", "plus", "slope"):
            r.push(name, slice(None), cs)
        for b in range(3 if whole else 0):
            r.push("g", slice(None), lanes(b * width + c * LANE))
        return carry

    lax.fori_loop(0, width // LANE, body, 0)


def own_masked(r, geo, cs):
    m = r.mask[0]
    for at, _, _ in geo.slabs():
        r.act2_own[at, :] = (r.act2[at, cs].astype(f32) * m).astype(bf16)


def middle_forward(r, geo, prm, pre, act2):
    own = r.meta[OWN]

    def body(c, carry):
        cs = lanes(c * LANE)
        mean, rr = statistics(pre, cs, r, geo)
        gain, shift = prm[20:21, cs], prm[21:22, cs]
        scale = gain * rr
        r.gr2[0:1, cs] = scale
        mul = 0.5 * scale
        add = 0.5 * shift - mean * mul
        for at, _, _ in geo.slabs():
            half = pre[at, cs] * mul + add
            act, slope = silu_parts(half)
            r.h2[at, cs] = half.astype(bf16)
            r.d2[at, cs] = slope.astype(bf16)
            act2[at, cs] = act.astype(bf16)

        @pl.when(c == own)
        def _():
            own_masked(r, geo, cs)

        r.push("h2", slice(None), cs)
        r.push("d2", slice(None), cs)
        return carry

    lax.fori_loop(0, pre.shape[1] // LANE, body, 0)


def in_pairs(count, pick, load, work):
    load(pick(0, 0), 0)

    def step(j, carry):
        load(pick(j, 1), 1)
        work(pick(j, 0), 0, j, 0)
        load(pick(jnp.minimum(j + 1, count - 1), 0), 0)
        work(pick(j, 1), 1, j, 1)
        return carry

    lax.fori_loop(0, count, step, 0)


def third_forward(r, geo, thr, act2, weight, x):
    buffers = [r.br0, r.br1]

    def load(n, slot):
        buffers[slot][...] = dot(act2[...], weight[:, lanes(n * CHUNK, CHUNK)])

    def work(n, slot, j, p):
        br = buffers[slot]
        for half in range(CHUNK // LANE):
            ls = slice(half * LANE, (half + 1) * LANE)
            cs = lanes(n * CHUNK + half * LANE)
            mean, rr = statistics(br, ls, r, geo)
            gain, shift = thr[0:1, cs], thr[1:2, cs]
            mul = gain * rr
            add = shift - mean * mul
            r.gr3[0:1, cs] = mul
            for at, _, _ in geo.slabs():
                y = br[at, ls] * mul + add
                out, slope = silu_parts(0.5 * (x[at, cs].astype(f32) + y))
                r.y3[at, cs] = y.astype(bf16)
                r.d3[at, cs] = slope.astype(bf16)
                r.x_next[at, cs] = out.astype(bf16)
        cs = lanes(n * CHUNK, CHUNK)
        for name in ("y3", "d3", "x_next"):
            r.push(name, slice(None), cs)

    in_pairs(x.shape[1] // CHUNK // 2, lambda j, p: 2 * j + p, load, work)


def third_both(r, geo, thr, act2, weight, x, pg, parts):
    n_pix = pixel_count(r, geo)
    buffers = [r.br0, r.br1]
    each = parts[0].shape[0]

    def load(n, slot):
        buffers[slot][...] = dot(act2[...], weight[:, lanes(n * CHUNK, CHUNK)])

    def work(n, slot, j, p):
        br = buffers[slot]
        for half in range(CHUNK // LANE):
            ls = slice(half * LANE, (half + 1) * LANE)
            cs = lanes(n * CHUNK + half * LANE)
            mean, rr = statistics(br, ls, r, geo)
            gain, shift = thr[0:1, cs], thr[1:2, cs]
            mul = gain * rr
            add = shift - mean * mul
            m = r.mask[0]
            grad = (0.5 * pg[0:1, cs]) * m
            pool, s1, s2 = zeros8(), zeros8(), zeros8()
            for at, _, _ in geo.slabs():
                y = br[at, ls] * mul + add
                out, slope = silu_parts(0.5 * (x[at, cs].astype(f32) + y))
                pool = pool + eights(out * m)
                e = slope * grad
                s1 = s1 + eights(e)
                s2 = s2 + eights(e * y)
                br[at, ls] = y
                r.e[at, ls] = e
                r.d3[at, cs] = slope.astype(bf16)
            shift_grad = column_sum(s1)
            gain_grad, k0, k1 = norm_back(n_pix, gain, shift, shift_grad, column_sum(s2), 1.0)
            r.pooled[0:1, cs] = column_sum(pool) / n_pix
            r.third[0:1, cs] = gain_grad
            r.third[1:2, cs] = shift_grad
            k0, k1 = mul * k0, mul * k1
            for at, _, _ in geo.slabs():
                v = mul * r.e[at, ls] - (k0 + br[at, ls] * k1)
                r.bg[at, cs] = v.astype(bf16)
        r.push("d3", slice(None), lanes(n * CHUNK, CHUNK))

    in_pairs(each, lambda j, p: r.meta[ORDER + p * each + j], load, work)


def by_destination(r, parts, body):
    each = parts[0].shape[0]

    def step(j, carry):
        for p, ref in enumerate(parts):
            body(r.meta[ORDER + p * each + j], ref, j)
        return carry

    lax.fori_loop(0, each, step, 0)


def third_products(r, geo, act2_own, weight, parts, row0=0):
    r.wide[...] = dot_tn(act2_own[...], r.bg[...]).astype(bf16)

    def body(n, ref, place):
        for half in range(CHUNK // LANE):
            rows = slice(row0 + half * LANE, row0 + (half + 1) * LANE)
            ref[place, rows, :] = r.wide[:, lanes(n * CHUNK + half * LANE)]

    by_destination(r, parts, body)
    if row0 == 256:
        r.push("away")
        r.push("home")
    r.ag2[...] = dot_nt(r.bg[...], weight[...]).astype(bf16)
    r.push("ag2")


def conv_backward(r, geo, prm, wait, weight_t, sem, parts, top):
    own = r.meta[OWN]
    n_pix = pixel_count(r, geo)
    width = r.ag2.shape[1]
    clear_border(r.sg, geo, width, 2, 0)
    r.sgo[...] = jnp.zeros_like(r.sgo)

    def body(c, carry):
        cs = lanes(c * LANE)
        wait(c)
        s1, s2 = zeros8(), zeros8()
        m = r.mask[0]
        for at, _, _ in geo.slabs():
            e = (r.ag2[at, cs].astype(f32) * r.d2[at, cs].astype(f32)) * m
            r.e[at, 0:LANE] = e
            s1 = s1 + eights(e)
            s2 = s2 + eights(e * r.h2[at, cs].astype(f32))
        gain, shift, scale = prm[20:21, cs], prm[21:22, cs], r.gr2[0:1, cs]
        shift_grad = 0.5 * column_sum(s1)
        gain_grad, k0, k1 = norm_back(n_pix, gain, shift, shift_grad, 0.5 * column_sum(s2), 2.0)
        k0, k1, scale = scale * k0, scale * k1, 0.5 * scale
        for at, h, w in geo.slabs():
            v = scale * r.e[at, 0:LANE] - m * (k0 + r.h2[at, cs].astype(f32) * k1)
            store_shifted(r.sg, v, h, w, c, width, geo, -1)

        @pl.when(c == own)
        def _():
            r.small2[0:1, :] = gain_grad
            r.small2[1:2, :] = shift_grad
            centre = lanes(width + c * LANE)
            for a in range(3):
                for h in range(geo.high):
                    if 0 <= h - a + 1 < geo.high:
                        to = slice(h * geo.step, (h + 1) * geo.step)
                        start = (h - a + 2) * geo.step
                        r.sgo[to, a * LANE : (a + 1) * LANE] = r.sg[start : start + geo.step, centre]

        return carry

    lax.fori_loop(0, width // LANE, body, 0)
    if not top:
        r.ready("g")
    part = dot_tn(r.sgo[...], r.g[geo.step : geo.step + geo.rows, :])
    for a in range(3):
        for k in range(3 * width // LANE):
            block = part[a * LANE : (a + 1) * LANE, k * LANE : (k + 1) * LANE]
            b, first = k // (width // LANE), k % (width // LANE) * LANE
            r.wg[3 * a + b, first : first + LANE, :] = jnp.transpose(block).astype(bf16)

    def hand_out(n, ref, place):
        rows = rows_at(n * 64, 64, 64)
        for tap in range(9):
            ref[place, tap * 64 : (tap + 1) * 64, :] = r.wg[tap, rows, :]
        if top:
            pieces = [r.pooled[0:1, lanes(n * CHUNK, CHUNK)], r.grad[0:1, :].astype(f32)]
            pieces = [v[:, i * LANE : (i + 1) * LANE] for v in pieces for i in range(2)]
            pieces.append(jnp.zeros((HEAD_ROWS - 4, LANE), f32))
            ref[place, 832 : 832 + HEAD_ROWS, :] = jnp.concatenate(pieces, axis=0).astype(bf16)

    by_destination(r, parts, hand_out)
    r.push("away")
    r.push("home")
    arrived(weight_t, sem)
    total = None
    for a in range(3):
        lhs = r.sg[(2 - a) * geo.step : (2 - a) * geo.step + geo.rows, :]
        part = dot_nt(lhs, weight_t[a])
        total = part if total is None else total + part
    r.gg[...] = total.astype(bf16)
    r.push("gg")


def gate_backward(r, geo, prm):
    n_pix = pixel_count(r, geo)
    width = r.gg.shape[1]
    own = r.meta[OWN] if width > LANE else 0

    def body(c, carry):
        cs = lanes(c * LANE)
        r.ready_lanes(c)
        for at, _, _ in geo.slabs():
            grad = r.gg[at, cs].astype(f32)
            r.e[at, :] = grad * r.plus[at, cs].astype(f32)
            r.field[at, :] = grad * r.slope[at, cs].astype(f32)
        s1, s2 = zeros8(), zeros8()
        half_next, m = r.mask[2], r.mask[0]
        for at, h, w in geo.slabs():
            back = taps_sum(r.field, prm, cs, h, w, geo, -1) * half_next
            e = (r.e[at, :] + (pltpu.roll(back, 1, axis=0) - back)) * r.d1[at, cs].astype(f32)
            r.e[at, :] = e
            s1 = s1 + eights(e)
            s2 = s2 + eights(e * r.h1[at, cs].astype(f32))
        gain, shift, scale = prm[0:1, cs], prm[1:2, cs], r.gr1[0:1, cs]
        shift_grad = 0.5 * column_sum(s1)
        gain_grad, k0, k1 = norm_back(n_pix, gain, shift, shift_grad, 0.5 * column_sum(s2), 2.0)
        k0, k1, scale = scale * k0, scale * k1, 0.5 * scale
        for at, _, _ in geo.slabs():
            v = scale * r.e[at, :] - m * (k0 + r.h1[at, cs].astype(f32) * k1)
            r.fg[at, cs] = v.astype(bf16)

        @pl.when(c == own)
        def _():
            r.ready("diff")
            r.small[SMALL_ROWS - 4 :, :] = jnp.zeros((4, LANE), f32)
            r.small[0:1, :] = gain_grad
            r.small[1:2, :] = shift_grad
            for a in range(3):
                for b in range(3):
                    for first, reach in ((2, 1), (11, 2)):
                        total = zeros8()
                        for at, h, w in geo.slabs():
                            dh, dw = h - reach * (a - 1), w - reach * (b - 1)
                            if 0 <= dh < geo.high and 0 <= dw < geo.wide:
                                total = total + eights(r.diff[at, :] * r.field[geo.slab(dh, dw), :])
                        row = first + 3 * a + b
                        r.small[row : row + 1, :] = 0.25 * column_sum(total)

        return carry

    lax.fori_loop(0, width // LANE, body, 0)


def first_products(r, geo, x, parts):
    own = r.meta[OWN] if r.fg.shape[1] > LANE else 0
    r.wide[...] = dot_tn(r.fg[:, lanes(own * LANE)], x[...]).astype(bf16)

    def body(n, ref, place):
        for half in range(CHUNK // LANE):
            block = r.wide[:, lanes(n * CHUNK + half * LANE)]
            ref[place, half * LANE : (half + 1) * LANE, :] = jnp.transpose(block)

    by_destination(r, parts, body)


def third_backward(r, geo, thr, weight_in, pg, each):
    n_pix = pixel_count(r, geo)
    own = r.meta[OWN]
    per_own = r.e3.shape[1] // CHUNK
    buffers = [r.br0, r.br1]

    def load(n, slot):
        rows = rows_at(n * CHUNK, CHUNK, CHUNK)
        buffers[slot][...] = dot_nt(r.fg[...], weight_in[rows, :])

    def work(n, slot, j, p):
        br = buffers[slot]
        r.ready_chunk(n)
        for half in range(CHUNK // LANE):
            ls = slice(half * LANE, (half + 1) * LANE)
            cs = lanes(n * CHUNK + half * LANE)
            grad = (0.5 * pg[0:1, cs]) * r.mask[0]
            s1, s2 = zeros8(), zeros8()
            for at, _, _ in geo.slabs():
                out_grad = br[at, ls] + r.d3_next[at, cs].astype(f32) * grad
                e = out_grad * r.d3[at, cs].astype(f32)
                br[at, ls] = e
                s1 = s1 + eights(e)
                s2 = s2 + eights(e * r.y3[at, cs].astype(f32))
            gain, shift, scale = thr[0:1, cs], thr[1:2, cs], r.gr3[0:1, cs]
            shift_grad = 0.5 * column_sum(s1)
            gain_grad, k0, k1 = norm_back(n_pix, gain, shift, shift_grad, 0.5 * column_sum(s2), 1.0)
            r.third[0:1, cs] = gain_grad
            r.third[1:2, cs] = shift_grad
            k0, k1, scale = scale * k0, scale * k1, 0.5 * scale
            for at, _, _ in geo.slabs():
                v = scale * br[at, ls] - (k0 + r.y3[at, cs].astype(f32) * k1)
                r.bg[at, cs] = v.astype(bf16)
        owner = n // per_own

        @pl.when(owner == own)
        def _():
            r.e3[:, lanes((n - owner * per_own) * CHUNK, CHUNK)] = br[...].astype(bf16)

    in_pairs(each, lambda j, p: r.meta[ORDER + p * each + j], load, work)


class Sizes:
    def __init__(self, geo, inner, wide, order_n):
        self.geo, self.inner, self.wide, self.order_n = geo, inner, wide, order_n
        self.mask = VM((MASKS, geo.seg, LANE), f32)
        self.field = VM((geo.rows, LANE), f32)
        self.pair = VM((geo.rows, CHUNK), f32)

    def narrow(self, dtype=bf16):
        return ((self.geo.rows, self.inner), dtype)

    def slim(self, dtype=bf16):
        return ((self.geo.rows, LANE), dtype)

    def broad(self, dtype=bf16):
        return ((self.geo.rows, self.wide), dtype)

    def stacked(self):
        return ((self.geo.rows + 2 * self.geo.step, 3 * self.inner), bf16)

    def parts(self, rows):
        shape = ((self.order_n // 2, rows, LANE), bf16)
        return dict(away=shape, home=shape)

    def middle(self):
        return dict(h2=self.narrow(), d2=self.narrow(), gr2=((1, self.inner), f32), act2_own=self.slim())

    def gate(self, width):
        saved = ((self.geo.rows, width), bf16)
        return dict(h1=saved, d1=saved, plus=saved, slope=saved, diff=self.slim(f32), gr1=((1, width), f32))

    def conv_back_scratch(self, width):
        return dict(
            w_t=VM((3, width, 3 * self.inner), bf16),
            sg=VM(*self.stacked()),
            sgo=VM((self.geo.rows, 3 * LANE), bf16),
            wg=VM((9, self.inner, LANE), bf16),
        )

    def gate_back_scratch(self):
        return dict(mask=self.mask, field=self.field, e=self.field, wide=VM((LANE, self.wide), bf16))


def dma(count):
    return pltpu.SemaphoreType.DMA((count,))


def own_rows_of(prm, layer):
    return prm.at[pl.ds(layer * SLOT, SMALL_ROWS)]


def kernel_gate_own(z, meta, source, x, own_small, after=()):
    geo = z.geo

    def body(r):
        source.start(IN_OWN, r, r.w_in, r.sem.at[0])
        fill_masks(r, geo)
        r.ready("x")
        arrived(r.w_in, r.sem.at[0])
        first_matmul(r, geo, r.x, r.w_in, r.pre)
        gate_forward(r, geo, own_rows_of(r.prm, 0), r.pre)
        r.push("diff")
        r.push("gated")

    return call(
        "gate_own",
        body,
        dict(source.operands(), meta=(meta, SM), x=(x, LATE), prm=(own_small, VM)),
        dict(z.gate(LANE), gated=z.slim()),
        dict(
            field=z.field, act=z.field, mask=z.mask, pre=z.field,
            w_in=VM((z.wide, LANE), bf16), sem=dma(1),
        ),
        flops=4_000_000_000,
        nbytes=6_000_000,
        after=after,
    )


EXTRA = 16


def kernel_conv_own(z, meta, source, gated, chans, own_small, after=()):
    geo = z.geo

    def body(r):
        source.start(CONV_OWN, r, r.w_mid, r.sem.at[0])
        fill_masks(r, geo)
        clear_border(r.g, geo, z.inner, 0, 2)
        for i in range(len(gated)):
            r.ready("gated" + str(i))
            c = r.chans[i]
            for at, h, w in geo.slabs():
                store_shifted(r.g, r.gated[i][at, :], h, w, c, z.inner, geo, 1)
        r.push("g")
        arrived(r.w_mid, r.sem.at[0])
        conv_matmul(r, geo, r.g, r.w_mid, r.pre)
        cs = slice(0, LANE)
        mean, rr = statistics(r.pre, cs, r, geo)
        prm = own_rows_of(r.prm, 0)
        scale = prm[20:21, cs] * rr
        mul = 0.5 * scale
        add = 0.5 * prm[21:22, cs] - mean * mul
        for at, _, _ in geo.slabs():
            r.half[at, :] = (r.pre[at, cs] * mul + add).astype(bf16)
        near = scale.astype(bf16).astype(f32)
        rows = jnp.concatenate([near, scale - near, jnp.zeros((EXTRA - 2, LANE), f32)], axis=0)
        r.half[geo.rows :, :] = rows.astype(bf16)
        r.push("half")

    return call(
        "conv_own",
        body,
        dict(
            source.operands(), meta=(meta, SM), chans=(chans, SM), prm=(own_small, VM),
            gated=[(item, LATE) for item in gated],
        ),
        dict(g=z.stacked(), half=((geo.rows + EXTRA, LANE), bf16)),
        dict(mask=z.mask, pre=z.field, w_mid=VM((3, 3, z.inner, LANE), bf16), sem=dma(1)),
        flops=6_000_000_000,
        nbytes=6_000_000,
        after=after,
    )


def kernel_third(z, meta, source, halves, chans, x, thr, after=()):
    geo = z.geo

    def body(r):
        source.start(OUT, r, r.w_out, r.sem.at[0])
        fill_masks(r, geo)
        own = r.meta[OWN]
        for i in range(len(halves)):
            r.ready("halves" + str(i))
            c = r.chans[i]
            cs = lanes(c * LANE)
            for at, _, _ in geo.slabs():
                half = r.halves[i][at, :]
                act, slope = silu_parts(half.astype(f32))
                r.h2[at, cs] = half
                r.d2[at, cs] = slope.astype(bf16)
                r.act2[at, cs] = act.astype(bf16)
            tail = r.halves[i][geo.rows :, :].astype(f32)
            r.gr2[0:1, cs] = tail[0:1] + tail[1:2]

            @pl.when(c == own)
            def _():
                own_masked(r, geo, cs)

        for name in ("h2", "d2", "act2_own"):
            r.push(name)
        r.ready("x")
        arrived(r.w_out, r.sem.at[0])
        third_forward(r, geo, r.thr, r.act2, r.w_out, r.x)

    return call(
        "third_forward",
        body,
        dict(
            source.operands(), meta=(meta, SM), chans=(chans, SM), thr=(thr, VM),
            halves=[(item, LATE) for item in halves], x=(x, LATE),
        ),
        dict(
            z.middle(), y3=z.broad(), d3=z.broad(), x_next=z.broad(), gr3=((1, z.wide), f32),
        ),
        dict(
            mask=z.mask, w_out=VM((z.inner, z.wide), bf16), act2=VM(*z.narrow()), br0=z.pair, br1=z.pair,
            sem=dma(1),
        ),
        flops=12_000_000_000,
        nbytes=16_000_000,
        after=after,
    )


def kernel_top(z, meta, source, x, prm, thr, grad_low, bias, after=()):
    geo = z.geo

    def body(r):
        source.start(IN, r, r.w_in, r.sem.at[0])
        source.start(CONV, r, r.w_mid, r.sem.at[1])
        source.start(OUT, r, r.w_out, r.sem.at[2])
        source.start(HEAD, r, r.w_head, r.sem.at[3])
        source.start(CONV_T, r, r.w_t, r.sem.at[4])
        fill_masks(r, geo)
        r.ready("x")
        arrived(r.w_in, r.sem.at[0])
        first_matmul(r, geo, r.x, r.w_in, r.pre)
        gate_forward(r, geo, r.prm, r.pre)
        r.push("diff")
        arrived(r.w_mid, r.sem.at[1])
        conv_matmul(r, geo, r.g, r.w_mid, r.pre)
        middle_forward(r, geo, r.prm, r.pre, r.act2)
        arrived(r.w_out, r.sem.at[2])
        source.wait_head(r.w_head, r.sem.at[3])
        r.pg[...] = dot(r.grad[...], r.w_head[...])[0:1] / pixel_count(r, geo)
        third_both(r, geo, r.thr, r.act2, r.w_out, r.x, r.pg, [r.away, r.home])
        low = jnp.broadcast_to(r.pooled[...].astype(bf16), (16, z.wide))
        r.logits[...] = dot_nt(low, r.w_head[...])[0:8] + r.bias[...]
        r.pooled_out[...] = r.pooled[...]
        third_products(r, geo, r.act2_own, r.w_out, [r.away, r.home], 576)
        conv_backward(r, geo, r.prm, lambda c: None, r.w_t, r.sem.at[4], [r.away, r.home], True)

    row = ((1, z.wide), f32)
    return call(
        "top_both",
        body,
        dict(
            source.operands(), meta=(meta, SM), x=(x, LATE), prm=(prm, VM), thr=(thr, VM),
            grad=(grad_low, VM), bias=(bias, VM),
        ),
        dict(
            z.gate(z.inner), **z.parts(832 + HEAD_ROWS), g=z.stacked(), d3=z.broad(), pg=row, pooled_out=row,
            logits=((8, bias.shape[1]), f32), third=((2, z.wide), f32), gg=z.narrow(), small2=((2, LANE), f32),
        ),
        dict(
            z.conv_back_scratch(z.inner),
            **{name: VM(*value) for name, value in z.middle().items()},
            field=z.field, act=z.field, mask=z.mask, br0=z.pair, br1=z.pair, e=z.pair,
            pooled=VM(*row), ag2=VM(*z.narrow()), pre=VM(*z.narrow(f32)), act2=VM(*z.narrow()),
            w_in=VM((z.wide, z.inner), bf16), w_mid=VM((3, 3, z.inner, z.inner), bf16),
            w_out=VM((z.inner, z.wide), bf16), w_head=VM((bias.shape[1], z.wide), bf16),
            bg=VM(*z.broad()), wide=VM((LANE, z.wide), bf16), sem=dma(5),
        ),
        flops=60_000_000_000,
        nbytes=30_000_000,
        after=after,
    )


def gate_back_ins(kept, prm):
    ins = {name: (getattr(kept, name), SLICED) for name in ("plus", "slope", "h1", "d1")}
    return dict(ins, diff=(kept.diff, LATE), gr1=(kept.gr1, VM), prm=(prm, VM))


def kernel_join(z, meta, source, source_below, kept, below, prm, thr, x, after=()):
    geo = z.geo

    def body(r):
        source.start(IN, r, r.w_in, r.sem.at[0])
        r.start_rest()
        source_below.start(OUT, r, r.w_out, r.sem.at[1])
        fill_masks(r, geo)
        gate_backward(r, geo, r.prm)
        arrived(r.w_in, r.sem.at[0])
        third_backward(r, geo, r.thr, r.w_in, r.pg, z.order_n // 2)
        r.push("e3")
        r.ready("x")
        first_products(r, geo, r.x, [r.away, r.home])
        arrived(r.w_out, r.sem.at[1])
        third_products(r, geo, r.act2_own, r.w_out, [r.away, r.home], 256)

    return call(
        "join_backward",
        body,
        dict(
            {**source.operands(), **source_below.operands()},
            **gate_back_ins(kept, prm), meta=(meta, SM), gg=(kept.gg, SLICED), thr=(thr, VM), pg=(kept.pg, VM),
            d3_next=(kept.d3, ORDERED), d3=(below.d3, ORDERED), y3=(below.y3, ORDERED), gr3=(below.gr3, VM),
            x=(x, LATE), act2_own=(below.act2_own, VM),
        ),
        dict(
            z.parts(512), small=((SMALL_ROWS, LANE), f32), third=((2, z.wide), f32), ag2=z.narrow(),
            e3=((geo.rows, z.wide // 4), bf16),
        ),
        dict(
            z.gate_back_scratch(), fg=VM(*z.narrow()), w_in=VM((z.wide, z.inner), bf16),
            w_out=VM((z.inner, z.wide), bf16), br0=z.pair, br1=z.pair, bg=VM(*z.broad()), sem=dma(2),
        ),
        flops=20_000_000_000,
        nbytes=30_000_000,
        after=after,
    )


def kernel_conv_back(z, meta, source, ag2, kept, g, prm, after=()):
    geo = z.geo

    def body(r):
        source.start(CONV_ROWS, r, r.w_t, r.sem.at[0])
        fill_masks(r, geo)
        conv_backward(r, geo, r.prm, r.ready_lanes, r.w_t, r.sem.at[0], [r.away, r.home], False)

    return call(
        "conv_backward",
        body,
        dict(
            source.operands(), meta=(meta, SM), ag2=(ag2, SLICED), d2=(kept.d2, SLICED), h2=(kept.h2, SLICED),
            gr2=(kept.gr2, VM), prm=(prm, VM), g=(g, LATE),
        ),
        dict(z.parts(576), gg=z.slim(), small2=((2, LANE), f32)),
        dict(z.conv_back_scratch(LANE), mask=z.mask, e=z.field, sem=dma(1)),
        flops=12_000_000_000,
        nbytes=16_000_000,
        after=after,
    )


def kernel_bottom(z, meta, gg, kept, own_small, x, smalls, after=()):
    geo = z.geo

    def body(r):
        fill_masks(r, geo)
        gate_backward(r, geo, own_rows_of(r.prm, 0))
        r.push("fg")
        both = jnp.concatenate([r.small[...], r.smalls[...]], axis=0).astype(bf16)
        for ref in (r.away, r.home):
            for place in range(ref.shape[0]):
                ref[place, 256:, :] = both
        r.ready("x")
        first_products(r, geo, r.x, [r.away, r.home])
        r.push("away")
        r.push("home")

    return call(
        "bottom_backward",
        body,
        dict(
            gate_back_ins(kept, own_small), meta=(meta, SM), gg=(gg, SLICED), x=(x, LATE), smalls=(smalls, VM),
        ),
        dict(z.parts(256 + SMALL_ROWS + smalls.shape[0]), fg=z.slim()),
        dict(z.gate_back_scratch(), small=VM((SMALL_ROWS, LANE), f32)),
        flops=4_000_000_000,
        nbytes=10_000_000,
        after=after,
    )


def kernel_input_grad(z, meta, source, fgs, chans, e3, after=()):
    geo = z.geo
    quarter = e3.shape[1]

    def body(r):
        source.start(IN_ROWS, r, r.w_in, r.sem.at[0])
        for i in range(len(fgs)):
            r.ready("fgs" + str(i))
            r.fg[:, lanes(r.chans[i] * LANE)] = r.fgs[i][...]
        r.ready("e3")
        arrived(r.w_in, r.sem.at[0])
        r.x_grad[...] = (dot_nt(r.fg[...], r.w_in[...]) + 0.5 * r.e3[...].astype(f32)).astype(bf16)
        r.push("x_grad")

    return call(
        "input_grad",
        body,
        dict(
            source.operands(), meta=(meta, SM), chans=(chans, SM), fgs=[(item, LATE) for item in fgs],
            e3=(e3, LATE),
        ),
        dict(x_grad=((geo.rows, quarter), bf16)),
        dict(w_in=VM((quarter, z.inner), bf16), fg=VM(*z.narrow()), sem=dma(1)),
        flops=1_000_000_000,
        nbytes=8_000_000,
        after=after,
    )


def fold(recv, home, stack_rows=0, after=()):
    slots, rows, _ = home.shape
    added = rows - stack_rows

    def body(r):
        for k, out in enumerate(r.s):
            out[:added] = (r.recv[k, :added].astype(f32) + r.home[k, :added].astype(f32)).astype(bf16)
            if stack_rows:
                out[added:rows] = r.home[k, added:]
                out[rows:] = r.recv[k, added:]
            r.push("s" + str(k))

    outs = dict(s=[((rows + stack_rows, LANE), bf16)] * slots)
    return call("fold", body, dict(recv=(recv, VM), home=(home, VM)), outs, {}, nbytes=4_000_000, after=after).s


def copies(sources, outs, plan, picks=None, after=()):
    ins = dict(a=[(item, HB) for item in sources])
    if picks is not None:
        ins["picks"] = (picks, SM)

    def body(r):
        started = []
        for i, (src, src_at, dst, dst_at) in enumerate(plan):
            if isinstance(src_at, tuple) and src_at[0] is Ellipsis:
                src_at = (r.picks[src_at[1]],)
            started.append(pltpu.make_async_copy(r.a[src].at[src_at], r.o[dst].at[dst_at], r.sem.at[i]))
            started[-1].start()
        for item, (_, _, dst, dst_at) in zip(started, plan):
            item.wait()
            r.push("o" + str(dst), *(dst_at if isinstance(dst_at, tuple) else (dst_at,)))

    outs = dict(o=[(shape, sources[0].dtype) for shape in outs])
    return call("copies", body, ins, outs, dict(sem=dma(len(plan))), nbytes=2_000_000, after=after).o


class Grid:
    FULL, LOW, HIGH = (0, 1, 2, 5, 6, 7), (3, 8), (4, 9)

    def __init__(self, clip_n, chan_n):
        self.clip_n, self.chan_n = clip_n, chan_n
        self.z_n = clip_n // 2
        self.clip, self.chan = lax.axis_index(CLIP).astype(jnp.int32), lax.axis_index(CHAN).astype(jnp.int32)

    def across_x(self, value):
        return lax.ppermute(value, CLIP, [(i, i ^ 1) for i in range(self.clip_n)])

    def along_z(self, value, k):
        return lax.ppermute(value, CLIP, [(i, (i + 2 * k) % self.clip_n) for i in range(self.clip_n)])

    def across(self, value, flip):
        return lax.ppermute(value, CHAN, [(i, i ^ flip) for i in range(self.chan_n)])

    def column(self, own):
        return [own] + [self.along_z(own, k) for k in range(1, self.z_n)]

    def stack(self, column, cuts, after=()):
        plan = [(k, rows, i, k) for i, rows in enumerate(cuts) for k in range(self.z_n)]
        shapes = [(self.z_n, rows.stop - rows.start, LANE) for rows in cuts]
        return copies(column, shapes, plan, after=after)

    def corner(self, plane, cut, after=()):
        rows = plane[0].shape[1]
        whole = slice(None)
        plan = [(0, (whole, slice(0, cut)), 0, whole), (1, (whole, slice(cut, rows)), 1, whole)]
        shapes = [(self.z_n, cut, LANE), (self.z_n, rows - cut, LANE)]
        low, high = copies(plane[1:], shapes, plan, after=after)
        arrays = list(plane) + [self.across(low, 2), self.across_x(high)]
        return arrays + [self.across(item, 1) for item in arrays]

    def column_z(self):
        return (self.clip // 2 + self.z_n - jnp.arange(self.z_n, dtype=jnp.int32)) % self.z_n

    def places(self, corners):
        x = self.clip % 2
        clips = [self.column_z() * 2 + (x ^ dx) for dx, _ in corners]
        chans = [jnp.full((self.z_n,), 1, jnp.int32) * (self.chan ^ flip) for _, flip in corners]
        return jnp.stack([jnp.concatenate(clips), jnp.concatenate(chans)]).astype(jnp.int32)

    def all_chans(self, own):
        over_y = self.across(own, 2)
        return [own, over_y, self.across(own, 1), self.across(over_y, 1)]

    def send_z(self, shares):
        return [shares[0]] + [self.along_z(shares[k], k) for k in range(1, self.z_n)]


FLIPS = (0, 2, 1, 3)


def pack(layer, names, masters, groups, head=None, chan=None, after=()):
    ins = {n: (masters[n], LATE, layer) for n in names}
    rows = dict(first=256, conv=576, out=256, head=2 * HEAD_PART)
    scratch = {}
    if head is not None:
        ins.update(head=(head, VM), chan=(chan, SM))
        scratch.update(padded=VM((4 * HEAD_PART, head.shape[1]), f32))

    def body(r):
        for to, group in zip(r.p, groups):
            row = 0
            for n in group:
                if n in ins and n in names:
                    r.ready(n)
                if n == "head":
                    r.padded[...] = jnp.zeros_like(r.padded)
                    r.padded[: head.shape[0], :] = r.head[...]
                    own = r.padded[rows_at(r.chan[0] * HEAD_PART, HEAD_PART, 16), :].astype(bf16)
                    for half in range(2):
                        at = row + half * HEAD_PART
                        to[at : at + HEAD_PART] = own[:, half * LANE : (half + 1) * LANE]
                elif n == "first":
                    to[row : row + 256] = r.first[...].astype(bf16)
                elif n == "conv":
                    for tap in range(9):
                        to[row + tap * 64 : row + tap * 64 + 64] = r.conv[tap // 3, tap % 3].astype(bf16)
                else:
                    for half in range(2):
                        block = r.out[:, half * LANE : (half + 1) * LANE].astype(bf16)
                        to[row + half * LANE : row + (half + 1) * LANE] = block
                row += rows[n]
        for i in range(len(groups)):
            r.push("p" + str(i))

    outs = dict(p=[((sum(rows[n] for n in group), LANE), bf16) for group in groups])
    return call("pack", body, ins, outs, scratch, nbytes=2_000_000, after=after).p


def pack_small(items):
    layers = items[0].shape[0]
    items = [jnp.transpose(item, (1, 2, 0, 3)) if item.ndim == 4 else item for item in items]

    def body(r):
        r.s[...] = jnp.zeros_like(r.s)
        for layer in range(layers):
            row = layer * SLOT
            for ref in r.i:
                if len(ref.shape) == 4:
                    for tap in range(9):
                        r.s[row : row + 1] = 0.5 * ref[tap // 3, tap % 3, layer : layer + 1, :]
                        row += 1
                else:
                    for k in range(ref.shape[1] // LANE):
                        r.s[row : row + 1] = ref[layer : layer + 1, k * LANE : (k + 1) * LANE]
                        row += 1

    ins = dict(i=[(item, VM) for item in items])
    return call("pack_small", body, ins, dict(s=((layers * SLOT, LANE), f32)), {}, nbytes=200_000).s


def spread_small(chans, slots, layers, inner, wide, per):
    def body(r):
        for i, ref in enumerate(r.s):
            chan = r.chans[i]
            for layer in range(layers):
                first = layer * SLOT
                r.prm[layer, :, lanes(chan * LANE)] = ref[first : first + SMALL_ROWS, :]
                for k in range(2):
                    for n in range(per):
                        at = first + 22 + k * per + n
                        r.thr[layer, k : k + 1, lanes((chan * per + n) * LANE)] = ref[at : at + 1, :]

    ins = dict(chans=(chans, SM), s=[(item, VM) for item in slots])
    outs = dict(prm=((layers, SMALL_ROWS, inner), f32), thr=((layers, 2, wide), f32))
    done = call("spread_small", body, ins, outs, {}, nbytes=200_000, direct=True)
    return done.prm, done.thr


def four(refs, rows):
    a, b, c, d = [ref[rows].astype(f32) for ref in refs]
    return (a + c) + (b + d)


def finish_upper(shares1, shares2, layers, classes, after=()):
    def body(r):
        for half in range(2):
            cs = slice(half * LANE, (half + 1) * LANE)
            r.out_grad[layers - 1, :, cs] = four(r.one, slice(576 + half * LANE, 576 + (half + 1) * LANE))
            r.out_grad[0, :, cs] = four(r.two, slice(256 + half * LANE, 256 + (half + 1) * LANE))
        pooled, grads, total = [], [], []
        for ref in r.one:
            own, other = ref[832:848].astype(f32), ref[848:864].astype(f32)
            for v in (own, other):
                pooled.append(jnp.concatenate([v[0:1], v[1:2]], axis=1))
                grads.append(jnp.concatenate([v[2:3], v[3:4]], axis=1))
            total.append(grads[-2] + grads[-1])
        pooled = jnp.concatenate(pooled, axis=0).astype(bf16)
        grads = jnp.concatenate(grads, axis=0).astype(bf16)
        r.head_grad[...] = dot_tn(grads, pooled)[:classes]
        r.bias_grad[...] = (total[0] + total[2]) + (total[1] + total[3])

    outs = dict(
        out_grad=((layers, LANE, 256), f32), head_grad=((classes, 256), f32), bias_grad=((1, 256), f32)
    )
    ins = dict(one=[(item, VM) for item in shares1], two=[(item, VM) for item in shares2])
    return call("finish_upper", body, ins, outs, {}, nbytes=4_000_000, after=after, direct=True)


def finish_lower(shares, layers, smalls, after=()):
    def body(r):
        for layer, refs in ((0, r.three), (layers - 1, r.one)):
            for tap in range(9):
                r.conv_grad[layer, tap // 3, tap % 3] = four(refs, slice(tap * 64, (tap + 1) * 64))
        r.push("conv_grad")
        r.in_grad[0] = four(r.last, slice(0, 256))
        r.in_grad[layers - 1] = four(r.two, slice(0, 256))
        r.push("in_grad")
        r.sum[...] = four(r.last, slice(256, r.last[0].shape[0]))
        for out, (rows, shape) in zip(r.small, smalls):
            for layer, row in enumerate(rows):
                if len(shape) == 4:
                    for tap in range(9):
                        out[tap // 3, tap % 3, layer : layer + 1] = r.sum[row + tap : row + tap + 1, :]
                else:
                    for k in range(shape[1] // LANE):
                        out[layer : layer + 1, k * LANE : (k + 1) * LANE] = r.sum[row + k : row + k + 1, :]

    one, two, three, last = [[(item, VM) for item in group] for group in shares]
    shapes = [(3, 3, shape[0], LANE) if len(shape) == 4 else shape for _, shape in smalls]
    outs = dict(
        in_grad=((layers, 256, LANE), f32), conv_grad=((layers, 3, 3, 64, LANE), f32),
        small=[(shape, f32) for shape in shapes],
    )
    scratch = dict(sum=VM((shares[3][0].shape[0] - 256, LANE), f32))
    ins = dict(one=one, two=two, three=three, last=last)
    done = call("finish_lower", body, ins, outs, scratch, nbytes=4_000_000, after=after)
    small = [jnp.transpose(item, (2, 0, 1, 3)) if item.ndim == 4 else item for item in done.small]
    return done.in_grad, done.conv_grad, small


def local(
    clip_input,
    seg_count,
    proj_in_master,
    conv_master,
    proj_out_master,
    head_master,
    gain_first,
    shift_first,
    taps_near,
    taps_far,
    gain_second,
    shift_second,
    gain_third,
    shift_third,
    head_bias,
    logit_grad,
    clip_n,
    chan_n,
):
    grid = Grid(clip_n, chan_n)
    clip, chan = grid.clip, grid.chan
    _, seg, high_map, wide_map, wide = clip_input.shape
    layers = proj_in_master.shape[0]
    inner = proj_in_master.shape[2] * chan_n
    classes = head_master.shape[1]
    class_pad = -(-classes // LANE) * LANE
    geo = Geometry(seg, high_map, wide_map)
    order_n = wide // CHUNK
    z = Sizes(geo, inner, wide, order_n)
    third_rows = wide // chan_n // LANE
    direct = clip_n == 8 and chan_n == 4 and proj_in_master.shape[1] == 256

    grad_low = logit_grad.astype(bf16)
    grad_rows = jnp.pad(grad_low, ((0, 15), (0, class_pad - classes)))
    bias_row = jnp.pad(head_bias, (0, class_pad - classes))[None]
    order = jnp.arange(order_n, dtype=jnp.int32)
    chans = jnp.arange(chan_n, dtype=jnp.int32)
    if direct:
        z_to = (clip // 2 + jnp.arange(4, dtype=jnp.int32)) % 4
        order = jnp.concatenate([z_to * 2 + ((clip % 2) ^ 1), z_to * 2 + clip % 2]).astype(jnp.int32)
        chans = jnp.stack([chan ^ flip for flip in FLIPS])
    meta = jnp.concatenate([seg_count.astype(jnp.int32), chan[None], order])
    x0 = jnp.transpose(clip_input[0], (1, 2, 0, 3)).reshape(geo.rows, wide)
    own_small = pack_small(
        [
            gain_first,
            shift_first,
            taps_near,
            taps_far,
            gain_second,
            shift_second,
            gain_third,
            shift_third,
        ]
    )

    def gather_chan(own):
        if direct:
            return grid.all_chans(own)
        every = lax.all_gather(own, CHAN, axis=0, tiled=False)
        return [every[i] for i in range(chan_n)]

    if direct:
        masters = dict(first=proj_in_master, conv=conv_master, out=proj_out_master)
        names = list(masters)
        first1, rest1 = pack(
            1, names, masters, [names[:1], names[1:] + ["head"]], head_master.T, chan[None]
        )
        by_core = lax.all_gather(rest1, (CLIP, CHAN), axis=0, tiled=False)
        own_a, own_out = pack(0, names, masters, [names[:2], names[2:]], after=[rest1])
        column_a = grid.column(own_a)
        prm, thr = spread_small(chans, gather_chan(own_small), layers, inner, wide, third_rows)
        in_a, conv_a = grid.stack(column_a, [slice(0, 256), slice(256, 832)], after=[prm])
        in_x = grid.across_x(in_a)
        conv_x = grid.across_x(conv_a)
        (own_e,) = copies(
            [own_out, first1], [(512, LANE)], [(0, slice(None), 0, slice(0, 256)), (1, slice(None), 0, slice(256, 512))],
            after=[in_a],
        )
        column_e = grid.column(own_e)

        near = grid.places([(0, 0), (1, 0)])
        in_source = Slots("wa", [in_a, in_x], near, {IN_OWN: [(0, 0, 0, 256), (1, 0, 0, 256)]}, chan_n)
        mid_source = Slots("wb", [conv_a, conv_x], near, {CONV_OWN: [(0, 0, 0, 3), (1, 0, 0, 3)]}, chan_n)
        gate0 = kernel_gate_own(z, meta, in_source, x0, own_small)
        gated = gather_chan(gate0.gated)
        conv0 = kernel_conv_own(z, meta, mid_source, gated, chans, own_small)
        halves = gather_chan(conv0.half)

        (stack_e,) = grid.stack(column_e, [slice(0, 512)], after=[gate0.gr1])
        plane_e = [stack_e, grid.across_x(stack_e), grid.across(stack_e, 2)]
        arrays_e = grid.corner(plane_e, 256, after=[conv0.half])
        corners = [(0, 0), (1, 0), (0, 2), (1, 2), (1, 2)]
        corners = corners + [(dx, flip ^ 1) for dx, flip in corners]
        places = grid.places(corners)
        full, low_part, high_part = grid.FULL, grid.LOW, grid.HIGH
        out_source = Slots("wc", arrays_e, places, {OUT: [(i, 0, 0, 2) for i in full + low_part]}, chan_n)
        third0 = kernel_third(z, meta, out_source, halves, chans, x0, thr[0])

        numbers = jnp.arange(clip_n * chan_n, dtype=jnp.int32)
        numbers = jnp.stack([numbers // chan_n, numbers % chan_n])
        last = len(arrays_e)
        parts = {
            IN: [(i, 256, 0, 256) for i in full] + [(i, 0, 0, 256) for i in high_part],
            CONV: [(last, 0, 0, 3)],
            OUT: [(last, 576, 0, 2)],
            HEAD: [(last, 832, 0, 2)],
        }
        parts[CONV_T] = parts[CONV]
        top_source = Slots("wd", arrays_e + [by_core], jnp.concatenate([places, numbers], axis=1), parts, chan_n)

        picks = jnp.stack([(clip // 2 - (chan ^ flip) + 4) % 4 for flip in FLIPS]).astype(jnp.int32)
        plan = []
        for i in range(4):
            for k in range(2):
                plan.append((k, (..., i), i, (k, slice(0, 256))))
                plan.append((2 + k, (..., i), i, (k, slice(256, 832))))
        sent = copies([in_a, in_x, conv_a, conv_x], [(2, 832, LANE)] * 4, plan, picks, after=[third0.gr3])
        rows_a = sent[:1] + [grid.across(item, flip) for item, flip in zip(sent[1:], FLIPS[1:])]
        x_own = clip % 2
        pair = jnp.stack([2 * chan + x_own, 2 * chan + (x_own ^ 1)])
        four_chans = jnp.repeat(chans, 2)
        four_clips = jnp.concatenate([pair] * 4)
        parts = {IN_ROWS: [(i, 0, 0, 256) for i in range(4)], CONV_ROWS: [(i, 256, 0, 3) for i in range(4)]}
        rows_source = Slots("we", rows_a, jnp.stack([four_clips, four_chans]).astype(jnp.int32), parts, chan_n)
    else:
        prm, thr = spread_small(chans, gather_chan(own_small), layers, inner, wide, third_rows)
        head_low = jnp.pad(head_master.astype(bf16), ((0, 0), (0, class_pad - classes)))
        head_low = lax.all_gather(head_low.T, CLIP, axis=1, tiled=True)
        gathered, own_cols = [], []
        for master, clip_axis, chan_axis in ((proj_in_master, 1, 2), (conv_master, 3, 4), (proj_out_master, 2, 1)):
            own_cols.append(lax.all_gather(master.astype(bf16), CLIP, axis=clip_axis, tiled=True))
            gathered.append(lax.all_gather(own_cols[-1], CHAN, axis=chan_axis, tiled=True))
        in_source = Whole("wa", {IN_OWN: own_cols[0][0]})
        mid_source = Whole("wb", {CONV_OWN: own_cols[1][0]})
        out_source = Whole("wc", {OUT: gathered[2][0]})
        top_source = Whole("wd", {IN: gathered[0][1], CONV: gathered[1][1], OUT: gathered[2][1], HEAD: head_low})
        wide_own, inner_own = wide // chan_n, inner // chan_n
        in_rows = lax.dynamic_slice_in_dim(gathered[0][0], chan * wide_own, wide_own, 0)
        conv_rows = lax.dynamic_slice_in_dim(gathered[1][0], chan * inner_own, inner_own, 2)
        rows_source = Whole("we", {IN_ROWS: in_rows, CONV_ROWS: conv_rows})
        gate0 = kernel_gate_own(z, meta, in_source, x0, own_small)
        conv0 = kernel_conv_own(z, meta, mid_source, gather_chan(gate0.gated), chans, own_small)
        third0 = kernel_third(z, meta, out_source, gather_chan(conv0.half), chans, x0, thr[0])

    x1 = third0.x_next
    top = kernel_top(z, meta, top_source, x1, prm[1], thr[1], grad_rows, bias_row)
    join = kernel_join(z, meta, top_source, out_source, top, third0, prm[1], thr[0], x1)
    after_mid, after_low = [], []
    if direct:
        folded1 = fold(grid.across_x(top.away), top.home, HEAD_ROWS, after=[join.third])
        shares1 = grid.send_z(folded1)
        after_mid = folded1[:1]
    mid0 = kernel_conv_back(z, meta, rows_source, join.ag2, third0, conv0.g, prm[0], after=after_mid)
    if direct:
        folded2 = fold(grid.across_x(join.away), join.home, after=[mid0.small2])
        shares2 = grid.send_z(folded2)
        after_low = folded2[:1] + shares1[1:]
    third = jnp.stack([join.third, top.third])
    third = lax.dynamic_slice_in_dim(third, chan * (wide // chan_n), wide // chan_n, 2)
    smalls = jnp.concatenate([join.small, mid0.small2, top.small2, third.reshape(-1, LANE)], axis=0)
    smalls = jnp.pad(smalls, ((0, -smalls.shape[0] % 16 + 8), (0, 0)))
    low = kernel_bottom(z, meta, mid0.gg, gate0, own_small, x0, smalls, after=after_low)

    at = 2 * SMALL_ROWS
    small_places = [
        ((0, SMALL_ROWS), gain_first.shape),
        ((1, SMALL_ROWS + 1), shift_first.shape),
        ((2, SMALL_ROWS + 2), taps_near.shape),
        ((11, SMALL_ROWS + 11), taps_far.shape),
        ((at, at + 2), gain_second.shape),
        ((at + 1, at + 3), shift_second.shape),
        ((at + 4, at + 4 + 2 * third_rows), gain_third.shape),
        ((at + 4 + third_rows, at + 4 + 3 * third_rows), shift_third.shape),
    ]
    if direct:
        upper = finish_upper(shares1, shares2, layers, classes, after=[low.fg])
        folded3 = fold(grid.across_x(mid0.away), mid0.home, after=[upper.bias_grad])
        shares3 = grid.send_z(folded3)
        folded4 = fold(grid.across_x(low.away), low.home)
        shares4 = grid.send_z(folded4)
        in_share, mid_share, small_grads = finish_lower(
            [shares1, shares2, shares3, shares4], layers, small_places
        )
        out_share = upper.out_grad
        head_share, bias_grad = upper.head_grad.T, upper.bias_grad[0, :classes]
    else:
        pooled_all = lax.all_gather(top.pooled_out.astype(bf16), CLIP, axis=0, tiled=True)
        grad_all = lax.all_gather(grad_low, CLIP, axis=0, tiled=True)
        own_rows = head_master.shape[0]
        pooled_own = lax.dynamic_slice_in_dim(pooled_all, clip * own_rows, own_rows, 1)
        head_share = dot_tn(pooled_own, grad_all)
        bias_grad = jnp.sum(grad_all.astype(f32), axis=0)

        def joined(item, first, rows):
            return jnp.concatenate([item.away, item.home], axis=0)[:, first : first + rows]

        in_terms = jnp.stack([joined(low, 0, 256), joined(join, 0, 256)]).reshape(layers, wide, LANE)
        mid_terms = jnp.stack([joined(mid0, 0, 576), joined(top, 0, 576)])
        mid_terms = mid_terms.reshape(layers, order_n, 3, 3, 64, LANE)
        mid_terms = jnp.transpose(mid_terms, (0, 2, 3, 1, 4, 5)).reshape(layers, 3, 3, inner, LANE)
        out_terms = jnp.stack([joined(join, 256, 256), joined(top, 576, 256)])
        out_terms = out_terms.reshape(layers, order_n, 2, LANE, LANE)
        out_terms = jnp.transpose(out_terms, (0, 3, 1, 2, 4)).reshape(layers, LANE, wide)
        in_share = lax.psum_scatter(in_terms, CLIP, scatter_dimension=1, tiled=True).astype(f32)
        mid_share = lax.psum_scatter(mid_terms, CLIP, scatter_dimension=3, tiled=True).astype(f32)
        out_share = lax.psum_scatter(out_terms, CLIP, scatter_dimension=2, tiled=True).astype(f32)
        small = lax.psum(low.home[0, 256:].astype(f32), CLIP)
        small_grads = []
        for rows, shape in small_places:
            count = 9 if len(shape) == 4 else shape[1] // LANE
            small_grads.append(jnp.stack([small[row : row + count] for row in rows]).reshape(shape))

    x_grad = kernel_input_grad(z, meta, rows_source, gather_chan(low.fg), chans, join.e3).x_grad
    input_grad = x_grad.reshape(high_map, wide_map, seg, -1)
    input_grad = jnp.transpose(input_grad, (2, 0, 1, 3))[None]
    return (
        top.logits[0:1, :classes],
        input_grad,
        in_share,
        mid_share,
        out_share,
        head_share,
        *small_grads,
        bias_grad,
    )


def solution(mesh):
    clip_n, chan_n = mesh.shape[CLIP], mesh.shape[CHAN]

    def program(*args):
        return local(*args, clip_n, chan_n)

    by_clip, by_chan = P(CLIP, None), P(None, CHAN)
    weights = (P(None, CLIP, CHAN), P(None, None, None, CLIP, CHAN), P(None, CHAN, CLIP), by_clip)
    taps = P(None, None, None, CHAN)
    small = (by_chan, by_chan, taps, taps, by_chan, by_chan, by_chan, by_chan, P())
    in_specs = (P(CLIP, None, None, None, None), P(CLIP)) + weights + small + (by_clip,)
    out_specs = (by_clip, P(CLIP, None, None, None, CHAN)) + weights + small
    return jax.shard_map(program, mesh=mesh, in_specs=in_specs, out_specs=out_specs, check_vma=False)
```

```python
import types

import jax
import jax.numpy as jnp
from jax import lax
from jax.experimental import pallas as pl
from jax.experimental.pallas import tpu as pltpu
from jax.sharding import PartitionSpec as P

EPS = 1e-05
LANE = 128
CHUNK = 256
SMALL_ROWS = 24
HEAD_ROWS = 16
HEAD_PART = 48
SLOT = 32
SMALL_PART = 8
DIGITS = "01"
MASKS = 3
CLIP, CHAN = "clip", "chan"
bf16 = jnp.bfloat16
f32 = jnp.float32


VM = pltpu.VMEM
SM = pltpu.SMEM
HB = pl.ANY
LATE = object()
SLICED = object()
ORDERED = object()
COUNT, OWN, CLIP_AT, ORDER = 0, 1, 2, 3
Space = types.SimpleNamespace


def _bytes(shape, dtype):
    size = jnp.dtype(dtype).itemsize
    for extent in shape:
        size *= extent
    return size


def _flat(items):
    flat, groups = {}, {}
    for name, item in items.items():
        if isinstance(item, list):
            groups[name] = [name + str(i) for i in range(len(item))]
            flat.update(zip(groups[name], item))
        else:
            flat[name] = item
    return flat, groups


def call(name, body, ins, outs, scratch, flops=0, nbytes=0, after=(), kept=(), direct=False, limit=60):
    ins, in_groups = _flat(dict(ins, unread=[(item, HB) for item in after]))
    outs, out_groups = _flat(outs)
    in_names, out_names = list(ins), list(outs)

    def kind(space):
        return [n for n in in_names if ins[n][1] is space]

    sliced, late, ordered = kind(SLICED), kind(LATE), kind(ORDERED)
    early = [n for n in out_names if _bytes(*outs[n]) > 65536 and n not in kept and not direct]
    part = {n: ins[n][2] for n in late if len(ins[n]) > 2}
    extra = dict(scratch)
    sems = {}
    for n in sliced + late + ordered:
        shape = ins[n][0].shape
        extra[n] = VM(shape[1:] if n in part else shape, ins[n][0].dtype)
        count = {id(SLICED): shape[-1] // LANE, id(ORDERED): shape[-1] // CHUNK}.get(id(ins[n][1]), 1)
        sems[n] = pltpu.SemaphoreType.DMA((count,))
    for n in early:
        extra[n] = VM(*outs[n])
        sems[n] = pltpu.SemaphoreType.DMA((1,))
    extra_names, sem_names = list(extra), list(sems)

    def kernel(*refs):
        outer = dict(zip(in_names + out_names, refs))
        refs = refs[len(outer) :]
        inner = dict(zip(extra_names, refs))
        sem = dict(zip(sem_names, refs[len(inner) :]))
        every = {**outer, **inner}
        r = Space(**every)
        for group, names in {**in_groups, **out_groups}.items():
            setattr(r, group, [every[n] for n in names])

        def slice_copy(n, c, size):
            cs = lanes(c * size, size)
            return pltpu.make_async_copy(outer[n].at[:, cs], inner[n].at[:, cs], sem[n].at[c])

        def whole_copy(n):
            ref = outer[n].at[part[n]] if n in part else outer[n]
            return pltpu.make_async_copy(ref, inner[n], sem[n].at[0])

        def start_rest():
            if ordered:
                each = ins[ordered[0]][0].shape[1] // CHUNK // 2
                for j in range(each):
                    for p in range(2):
                        for n in ordered:
                            slice_copy(n, r.meta[ORDER + p * each + j], CHUNK).start()
            for n in late:
                whole_copy(n).start()

        def ready_lanes(c):
            for n in sliced:
                slice_copy(n, c, LANE).wait()

        def ready_chunk(chunk):
            for n in ordered:
                slice_copy(n, chunk, CHUNK).wait()

        def ready(n):
            whole_copy(n).wait()

        def push(n, *index):
            if n not in early:
                return
            src, dst = (inner[n].at[index], outer[n].at[index]) if index else (inner[n], outer[n])
            pltpu.make_async_copy(src, dst, sem[n].at[0]).start()

        r.ready, r.ready_lanes, r.ready_chunk, r.push = ready, ready_lanes, ready_chunk, push
        r.start_rest = start_rest
        for c in range(ins[sliced[0]][0].shape[1] // LANE if sliced else 0):
            for n in sliced:
                slice_copy(n, c, LANE).start()
        if not ordered:
            start_rest()
        body(r)
        for n in early:
            pltpu.make_async_copy(inner[n], outer[n], sem[n].at[0]).wait()

    own = (LATE, SLICED, ORDERED)
    results = pl.pallas_call(
        kernel,
        name=name,
        out_shape=[jax.ShapeDtypeStruct(*outs[n]) for n in out_names],
        in_specs=[pl.BlockSpec(memory_space=HB if ins[n][1] in own else ins[n][1]) for n in in_names],
        out_specs=[pl.BlockSpec(memory_space=HB if n in early else VM) for n in out_names],
        scratch_shapes=[extra[n] for n in extra_names] + [sems[n] for n in sem_names],
        compiler_params=pltpu.CompilerParams(vmem_limit_bytes=limit * 1024 * 1024),
        cost_estimate=pl.CostEstimate(flops=flops, bytes_accessed=nbytes, transcendentals=0),
    )(*[ins[n][0] for n in in_names])
    done = dict(zip(out_names, results))
    for group, names in out_groups.items():
        done[group] = [done[n] for n in names]
    return Space(**done)


def lanes(start, size=LANE):
    return pl.ds(pl.multiple_of(start, LANE), size)


def rows_at(start, size, unit):
    return pl.ds(pl.multiple_of(start, unit), size)


def dot(a, b):
    return jnp.dot(a, b, preferred_element_type=f32)


def dot_nt(a, b):
    return lax.dot_general(a, b, (((1,), (1,)), ((), ())), preferred_element_type=f32)


def dot_tn(a, b):
    return lax.dot_general(a, b, (((0,), (0,)), ((), ())), preferred_element_type=f32)


class Geometry:
    def __init__(self, seg, high, wide):
        self.seg, self.high, self.wide = seg, high, wide
        self.step = seg * wide
        self.rows = high * self.step

    def slab(self, h, w, first=0):
        start = first + (h * self.wide + w) * self.seg
        return slice(start, start + self.seg)

    def slabs(self):
        for h in range(self.high):
            for w in range(self.wide):
                yield self.slab(h, w), h, w


def fill_masks(r, geo):
    count = r.meta[COUNT]
    seg = lax.broadcasted_iota(jnp.int32, (geo.seg, LANE), 0)
    r.mask[0] = jnp.where(seg < count, 1.0, 0.0)
    r.mask[1] = jnp.where(seg + 1 < count, 1.0, 0.0)
    r.mask[2] = jnp.where(seg + 1 < count, 0.5, 0.0)


def pixel_count(r, geo):
    return r.meta[COUNT].astype(f32) * float(geo.high * geo.wide)


def column_sum(v):
    return jnp.sum(v, axis=0, keepdims=True)


def zeros8():
    return jnp.zeros((8, LANE), f32)


def eights(v):
    return jnp.sum(v.reshape(v.shape[0] // 8, 8, LANE), axis=0)


def statistics(pre, cs, r, geo):
    n = pixel_count(r, geo)
    pilot = pre[0:1, cs]
    s1, s2 = zeros8(), zeros8()
    m = r.mask[0]
    for at, _, _ in geo.slabs():
        v = (pre[at, cs] - pilot) * m
        s1 = s1 + eights(v)
        s2 = s2 + eights(v * v)
    shift = column_sum(s1) / n
    var = jnp.maximum(column_sum(s2) / n - shift * shift, 0.0)
    return pilot + shift, lax.rsqrt(var + EPS)


def norm_back(n, gain, shift, s1, total, c):
    gain_grad = (c * total - shift * s1) / gain
    k1 = gain_grad / (n * gain)
    return gain_grad, s1 / n - shift * k1, c * k1


IN, CONV, CONV_T, OUT, HEAD, IN_OWN, CONV_OWN, IN_ROWS, CONV_ROWS = range(9)


class Slots:
    def __init__(self, name, arrays, rules, parts, chan_n):
        self.name, self.arrays, self.rules, self.parts, self.chan_n = name, arrays, rules, parts, chan_n

    def operands(self):
        return {self.name: [(array, HB) for array in self.arrays]}

    def start(self, kind, r, dst, sem):
        refs = getattr(r, self.name)
        own = r.meta[OWN]
        for no, row0, first, many in self.parts[kind]:
            ref = refs[no]

            def body(s, carry, ref=ref, rule=self.rules[no], row0=row0, first=first, many=many):
                clip, chan = rule(s, r.meta[CLIP_AT], own)

                def copy(src, to):
                    pltpu.make_async_copy(src, to, sem).start()

                if kind in (IN, IN_OWN, IN_ROWS):
                    start = clip * 256 + first - (own * 512 if kind == IN_ROWS else 0)
                    cs = slice(None) if kind == IN_OWN else lanes(chan * LANE)
                    copy(ref.at[s, pl.ds(row0, many)], dst.at[rows_at(start, many, LANE), cs])
                elif kind in (CONV, CONV_OWN, CONV_T, CONV_ROWS):
                    rows = rows_at(clip * 64 - (own * LANE if kind == CONV_ROWS else 0), 64, 64)
                    whole = first % 3 == 0 and many % 3 == 0
                    for a, b, src in self.taps(ref.at[s], row0, first, many, whole):
                        if kind == CONV:
                            copy(src, dst.at[a, b, rows, lanes(chan * LANE)])
                        elif kind == CONV_OWN:
                            copy(src, dst.at[a, b, rows, :])
                        elif whole:
                            for b in range(3):
                                copy(src.at[:, b], dst.at[a, rows, lanes(chan * LANE + b * 512)])
                        else:
                            copy(src, dst.at[a, rows, lanes(chan * LANE + b * 512)])
                elif kind == OUT:
                    for half in range(first, first + many):
                        src = ref.at[s, pl.ds(row0 + (half - first) * LANE, LANE)]
                        copy(src, dst.at[rows_at(chan * LANE, LANE, LANE), lanes(clip * 256 + half * LANE)])
                else:
                    rows = rows_at(chan * HEAD_PART, HEAD_PART, 16)
                    for half in range(2):
                        src = ref.at[s, pl.ds(row0 + half * HEAD_PART, HEAD_PART)]
                        copy(src, dst.at[rows, lanes(clip * 256 + half * LANE)])
                return carry

            lax.fori_loop(0, self.arrays[no].shape[0], body, 0)

    @staticmethod
    def taps(ref, row0, first, many, whole):
        if whole:
            block = ref.at[pl.ds(row0, many * 64)].reshape(many // 3, 3, 64, LANE)
            return [(pl.ds(first // 3, many // 3), slice(None), block)]
        each = range(first, first + many)
        return [(tap // 3, tap % 3, ref.at[pl.ds(row0 + (tap - first) * 64, 64)]) for tap in each]

    def wait_head(self, dst, sem):
        rows = self.chan_n * HEAD_PART
        dst[rows:, :] = jnp.zeros((dst.shape[0] - rows, dst.shape[1]), dst.dtype)
        arrived(dst.at[:rows], sem)


def along_column(dx, flip):
    return lambda s, clip, chan: ((clip // 2 - s) % 4 * 2 + ((clip % 2) ^ dx), chan ^ flip)


def in_order(chan_n):
    return lambda s, clip, chan: (s // chan_n, s % chan_n)


def own_pair(flip):
    return lambda s, clip, chan: (2 * chan + ((clip % 2) ^ s), chan ^ flip)


class Whole:
    def __init__(self, name, arrays):
        self.name, self.arrays = name, arrays

    def operands(self):
        return {self.name: [(array, HB) for array in self.arrays.values()]}

    def start(self, kind, r, dst, sem):
        stored = {CONV_T: CONV}.get(kind, kind)
        ref = getattr(r, self.name)[list(self.arrays).index(stored)]
        if kind in (CONV_T, CONV_ROWS):
            for b in range(3):
                pltpu.make_async_copy(ref.at[:, b], dst.at[:, :, pl.ds(b * 512, 512)], sem).start()
        else:
            pltpu.make_async_copy(ref, dst, sem).start()

    def wait_head(self, dst, sem):
        arrived(dst, sem)


def arrived(dst, sem):
    pltpu.make_async_copy(dst, dst, sem).wait()


def first_matmul(r, geo, x, weight, pre):
    pre[...] = dot(x[...], weight[...])


def conv_matmul(r, geo, g, weight, pre):
    total = None
    for a in range(3):
        w = weight[a].reshape(-1, pre.shape[1])
        part = dot(g[a * geo.step : a * geo.step + geo.rows, :], w)
        total = part if total is None else total + part
    pre[...] = total


def clear_border(ref, geo, width, left, right):
    zero = jnp.zeros((geo.step, ref.shape[1]), ref.dtype)
    ref[: geo.step, :] = zero
    ref[geo.rows + geo.step :, :] = zero
    side = jnp.zeros((geo.seg, width), ref.dtype)
    for h in range(geo.high):
        ref[geo.slab(h, 0, geo.step), left * width : (left + 1) * width] = side
        ref[geo.slab(h, geo.wide - 1, geo.step), right * width : (right + 1) * width] = side


def store_shifted(ref, value, h, w, c, width, geo, sign):
    value = value.astype(bf16)
    for b in range(3):
        to = w - sign * (b - 1)
        if 0 <= to < geo.wide:
            ref[geo.slab(h, to, geo.step), lanes(b * width + c * LANE)] = value


def taps_sum(field, prm, cs, h, w, geo, sign):
    total = None
    for a in range(3):
        for b in range(3):
            for first, reach in ((2, 1), (11, 2)):
                dh, dw = h + sign * reach * (a - 1), w + sign * reach * (b - 1)
                if not (0 <= dh < geo.high and 0 <= dw < geo.wide):
                    continue
                term = field[geo.slab(dh, dw), :] * prm[first + 3 * a + b : first + 1 + 3 * a + b, cs]
                total = term if total is None else total + term
    return total


def silu_parts(half):
    t = jnp.tanh(half)
    out = half * t + half
    return out, (1.0 + out) + t * (1.0 - out)


def gate_forward(r, geo, prm, pre):
    width = pre.shape[1]
    whole = width > LANE
    own = r.meta[OWN] if whole else 0
    if whole:
        clear_border(r.g, geo, width, 0, 2)

    def body(c, carry):
        cs = lanes(c * LANE)
        mean, rr = statistics(pre, cs, r, geo)
        gain, shift = prm[0:1, cs], prm[1:2, cs]
        scale = gain * rr
        r.gr1[0:1, cs] = scale
        mul = 0.5 * scale
        add = 0.5 * shift - mean * mul
        next_valid = r.mask[1]
        for at, _, _ in geo.slabs():
            half = pre[at, cs] * mul + add
            act, slope = silu_parts(half)
            r.h1[at, cs] = half.astype(bf16)
            r.d1[at, cs] = slope.astype(bf16)
            r.act[at, :] = act
            r.field[at, :] = (pltpu.roll(act, geo.seg - 1, axis=0) - act) * next_valid

        @pl.when(c == own)
        def _():
            r.diff[...] = r.field[...]

        for at, h, w in geo.slabs():
            t = jnp.tanh(taps_sum(r.field, prm, cs, h, w, geo, 1))
            act = r.act[at, :]
            plus = 1.5 + 0.5 * t
            r.plus[at, cs] = plus.astype(bf16)
            r.slope[at, cs] = (act - act * (t * t)).astype(bf16)
            if whole:
                store_shifted(r.g, act * plus, h, w, c, width, geo, 1)
            else:
                r.gated[at, :] = (act * plus).astype(bf16)
        for name in ("h1", "d1", "plus", "slope"):
            r.push(name, slice(None), cs)
        for b in range(3 if whole else 0):
            r.push("g", slice(None), lanes(b * width + c * LANE))
        return carry

    lax.fori_loop(0, width // LANE, body, 0)


def own_masked(r, geo, cs):
    m = r.mask[0]
    for at, _, _ in geo.slabs():
        r.act2_own[at, :] = (r.act2[at, cs].astype(f32) * m).astype(bf16)


def middle_forward(r, geo, prm, pre, act2):
    own = r.meta[OWN]

    def body(c, carry):
        cs = lanes(c * LANE)
        mean, rr = statistics(pre, cs, r, geo)
        gain, shift = prm[20:21, cs], prm[21:22, cs]
        scale = gain * rr
        r.gr2[0:1, cs] = scale
        mul = 0.5 * scale
        add = 0.5 * shift - mean * mul
        for at, _, _ in geo.slabs():
            half = pre[at, cs] * mul + add
            act, slope = silu_parts(half)
            r.h2[at, cs] = half.astype(bf16)
            r.d2[at, cs] = slope.astype(bf16)
            act2[at, cs] = act.astype(bf16)

        @pl.when(c == own)
        def _():
            own_masked(r, geo, cs)

        r.push("h2", slice(None), cs)
        r.push("d2", slice(None), cs)
        return carry

    lax.fori_loop(0, pre.shape[1] // LANE, body, 0)


def in_pairs(count, pick, load, work):
    load(pick(0, 0), 0)

    def step(j, carry):
        load(pick(j, 1), 1)
        work(pick(j, 0), 0, j, 0)
        load(pick(jnp.minimum(j + 1, count - 1), 0), 0)
        work(pick(j, 1), 1, j, 1)
        return carry

    lax.fori_loop(0, count, step, 0)


def third_forward(r, geo, thr, act2, weight, x):
    buffers = [r.br0, r.br1]

    def load(n, slot):
        buffers[slot][...] = dot(act2[...], weight[:, lanes(n * CHUNK, CHUNK)])

    def work(n, slot, j, p):
        br = buffers[slot]
        for half in range(CHUNK // LANE):
            ls = slice(half * LANE, (half + 1) * LANE)
            cs = lanes(n * CHUNK + half * LANE)
            mean, rr = statistics(br, ls, r, geo)
            gain, shift = thr[0:1, cs], thr[1:2, cs]
            mul = gain * rr
            add = shift - mean * mul
            r.gr3[0:1, cs] = mul
            for at, _, _ in geo.slabs():
                y = br[at, ls] * mul + add
                out, slope = silu_parts(0.5 * (x[at, cs].astype(f32) + y))
                r.y3[at, cs] = y.astype(bf16)
                r.d3[at, cs] = slope.astype(bf16)
                r.x_next[at, cs] = out.astype(bf16)
        cs = lanes(n * CHUNK, CHUNK)
        for name in ("y3", "d3", "x_next"):
            r.push(name, slice(None), cs)

    in_pairs(x.shape[1] // CHUNK // 2, lambda j, p: 2 * j + p, load, work)


def third_both(r, geo, thr, act2, weight, x, pg, parts):
    n_pix = pixel_count(r, geo)
    buffers = [r.br0, r.br1]
    each = parts[0].shape[0]

    def load(n, slot):
        buffers[slot][...] = dot(act2[...], weight[:, lanes(n * CHUNK, CHUNK)])

    def work(n, slot, j, p):
        br = buffers[slot]
        for half in range(CHUNK // LANE):
            ls = slice(half * LANE, (half + 1) * LANE)
            cs = lanes(n * CHUNK + half * LANE)
            mean, rr = statistics(br, ls, r, geo)
            gain, shift = thr[0:1, cs], thr[1:2, cs]
            mul = gain * rr
            add = shift - mean * mul
            m = r.mask[0]
            grad = (0.5 * pg[0:1, cs]) * m
            pool, s1, s2 = zeros8(), zeros8(), zeros8()
            for at, _, _ in geo.slabs():
                y = br[at, ls] * mul + add
                out, slope = silu_parts(0.5 * (x[at, cs].astype(f32) + y))
                pool = pool + eights(out * m)
                e = slope * grad
                s1 = s1 + eights(e)
                s2 = s2 + eights(e * y)
                br[at, ls] = y
                r.e[at, ls] = e
                r.d3[at, cs] = slope.astype(bf16)
            shift_grad = column_sum(s1)
            gain_grad, k0, k1 = norm_back(n_pix, gain, shift, shift_grad, column_sum(s2), 1.0)
            r.pooled[0:1, cs] = column_sum(pool) / n_pix
            r.third[0:1, cs] = gain_grad
            r.third[1:2, cs] = shift_grad
            k0, k1 = mul * k0, mul * k1
            for at, _, _ in geo.slabs():
                v = mul * r.e[at, ls] - (k0 + br[at, ls] * k1)
                r.bg[at, cs] = v.astype(bf16)
        r.push("d3", slice(None), lanes(n * CHUNK, CHUNK))

    in_pairs(each, lambda j, p: r.meta[ORDER + p * each + j], load, work)


def by_destination(r, parts, body):
    each = parts[0].shape[0]

    def step(j, carry):
        for p, ref in enumerate(parts):
            body(r.meta[ORDER + p * each + j], ref, j)
        return carry

    lax.fori_loop(0, each, step, 0)


def third_products(r, geo, act2_own, weight, parts, row0=0):
    r.wide[...] = dot_tn(act2_own[...], r.bg[...]).astype(bf16)

    def body(n, ref, place):
        for half in range(CHUNK // LANE):
            rows = slice(row0 + half * LANE, row0 + (half + 1) * LANE)
            ref[place, rows, :] = r.wide[:, lanes(n * CHUNK + half * LANE)]

    by_destination(r, parts, body)
    if row0 == 256:
        r.push("away")
        r.push("home")
    r.ag2[...] = dot_nt(r.bg[...], weight[...]).astype(bf16)
    r.push("ag2")


def conv_backward(r, geo, prm, wait, weight_t, sem, parts, top):
    own = r.meta[OWN]
    n_pix = pixel_count(r, geo)
    width = r.ag2.shape[1]
    clear_border(r.sg, geo, width, 2, 0)
    r.sgo[...] = jnp.zeros_like(r.sgo)

    def body(c, carry):
        cs = lanes(c * LANE)
        wait(c)
        s1, s2 = zeros8(), zeros8()
        m = r.mask[0]
        for at, _, _ in geo.slabs():
            e = (r.ag2[at, cs].astype(f32) * r.d2[at, cs].astype(f32)) * m
            r.e[at, 0:LANE] = e
            s1 = s1 + eights(e)
            s2 = s2 + eights(e * r.h2[at, cs].astype(f32))
        gain, shift, scale = prm[20:21, cs], prm[21:22, cs], r.gr2[0:1, cs]
        shift_grad = 0.5 * column_sum(s1)
        gain_grad, k0, k1 = norm_back(n_pix, gain, shift, shift_grad, 0.5 * column_sum(s2), 2.0)
        k0, k1, scale = scale * k0, scale * k1, 0.5 * scale
        for at, h, w in geo.slabs():
            v = scale * r.e[at, 0:LANE] - m * (k0 + r.h2[at, cs].astype(f32) * k1)
            store_shifted(r.sg, v, h, w, c, width, geo, -1)

        @pl.when(c == own)
        def _():
            r.small2[0:1, :] = gain_grad
            r.small2[1:2, :] = shift_grad
            centre = lanes(width + c * LANE)
            for a in range(3):
                for h in range(geo.high):
                    if 0 <= h - a + 1 < geo.high:
                        to = slice(h * geo.step, (h + 1) * geo.step)
                        start = (h - a + 2) * geo.step
                        r.sgo[to, a * LANE : (a + 1) * LANE] = r.sg[start : start + geo.step, centre]

        return carry

    lax.fori_loop(0, width // LANE, body, 0)
    if not top:
        r.ready("g")
    part = dot_tn(r.sgo[...], r.g[geo.step : geo.step + geo.rows, :])
    for a in range(3):
        for k in range(3 * width // LANE):
            block = part[a * LANE : (a + 1) * LANE, k * LANE : (k + 1) * LANE]
            b, first = k // (width // LANE), k % (width // LANE) * LANE
            r.wg[3 * a + b, first : first + LANE, :] = jnp.transpose(block).astype(bf16)

    def hand_out(n, ref, place):
        rows = rows_at(n * 64, 64, 64)
        for tap in range(9):
            ref[place, tap * 64 : (tap + 1) * 64, :] = r.wg[tap, rows, :]
        if top:
            pieces = [r.pooled[0:1, lanes(n * CHUNK, CHUNK)], r.grad[0:1, :].astype(f32)]
            pieces = [v[:, i * LANE : (i + 1) * LANE] for v in pieces for i in range(2)]
            pieces.append(jnp.zeros((HEAD_ROWS - 4, LANE), f32))
            ref[place, 832 : 832 + HEAD_ROWS, :] = jnp.concatenate(pieces, axis=0).astype(bf16)

    by_destination(r, parts, hand_out)
    r.push("away")
    r.push("home")
    arrived(weight_t, sem)
    total = None
    for a in range(3):
        lhs = r.sg[(2 - a) * geo.step : (2 - a) * geo.step + geo.rows, :]
        part = dot_nt(lhs, weight_t[a])
        total = part if total is None else total + part
    r.gg[...] = total.astype(bf16)
    r.push("gg")


def gate_backward(r, geo, prm):
    n_pix = pixel_count(r, geo)
    width = r.gg.shape[1]
    own = r.meta[OWN] if width > LANE else 0

    def body(c, carry):
        cs = lanes(c * LANE)
        r.ready_lanes(c)
        for at, _, _ in geo.slabs():
            grad = r.gg[at, cs].astype(f32)
            r.e[at, :] = grad * r.plus[at, cs].astype(f32)
            r.field[at, :] = grad * r.slope[at, cs].astype(f32)
        s1, s2 = zeros8(), zeros8()
        half_next, m = r.mask[2], r.mask[0]
        for at, h, w in geo.slabs():
            back = taps_sum(r.field, prm, cs, h, w, geo, -1) * half_next
            e = (r.e[at, :] + (pltpu.roll(back, 1, axis=0) - back)) * r.d1[at, cs].astype(f32)
            r.e[at, :] = e
            s1 = s1 + eights(e)
            s2 = s2 + eights(e * r.h1[at, cs].astype(f32))
        gain, shift, scale = prm[0:1, cs], prm[1:2, cs], r.gr1[0:1, cs]
        shift_grad = 0.5 * column_sum(s1)
        gain_grad, k0, k1 = norm_back(n_pix, gain, shift, shift_grad, 0.5 * column_sum(s2), 2.0)
        k0, k1, scale = scale * k0, scale * k1, 0.5 * scale
        for at, _, _ in geo.slabs():
            v = scale * r.e[at, :] - m * (k0 + r.h1[at, cs].astype(f32) * k1)
            r.fg[at, cs] = v.astype(bf16)

        @pl.when(c == own)
        def _():
            r.ready("diff")
            r.small[SMALL_ROWS - 4 :, :] = jnp.zeros((4, LANE), f32)
            r.small[0:1, :] = gain_grad
            r.small[1:2, :] = shift_grad
            for a in range(3):
                for b in range(3):
                    for first, reach in ((2, 1), (11, 2)):
                        total = zeros8()
                        for at, h, w in geo.slabs():
                            dh, dw = h - reach * (a - 1), w - reach * (b - 1)
                            if 0 <= dh < geo.high and 0 <= dw < geo.wide:
                                total = total + eights(r.diff[at, :] * r.field[geo.slab(dh, dw), :])
                        row = first + 3 * a + b
                        r.small[row : row + 1, :] = 0.25 * column_sum(total)

        return carry

    lax.fori_loop(0, width // LANE, body, 0)


def first_products(r, geo, x, parts):
    own = r.meta[OWN] if r.fg.shape[1] > LANE else 0
    r.wide[...] = dot_tn(r.fg[:, lanes(own * LANE)], x[...]).astype(bf16)

    def body(n, ref, place):
        for half in range(CHUNK // LANE):
            block = r.wide[:, lanes(n * CHUNK + half * LANE)]
            ref[place, half * LANE : (half + 1) * LANE, :] = jnp.transpose(block)

    by_destination(r, parts, body)


def third_backward(r, geo, thr, weight_in, pg, each):
    n_pix = pixel_count(r, geo)
    own = r.meta[OWN]
    per_own = r.e3.shape[1] // CHUNK
    buffers = [r.br0, r.br1]

    def load(n, slot):
        rows = rows_at(n * CHUNK, CHUNK, CHUNK)
        buffers[slot][...] = dot_nt(r.fg[...], weight_in[rows, :])

    def work(n, slot, j, p):
        br = buffers[slot]
        r.ready_chunk(n)
        for half in range(CHUNK // LANE):
            ls = slice(half * LANE, (half + 1) * LANE)
            cs = lanes(n * CHUNK + half * LANE)
            grad = (0.5 * pg[0:1, cs]) * r.mask[0]
            s1, s2 = zeros8(), zeros8()
            for at, _, _ in geo.slabs():
                out_grad = br[at, ls] + r.d3_next[at, cs].astype(f32) * grad
                e = out_grad * r.d3[at, cs].astype(f32)
                br[at, ls] = e
                s1 = s1 + eights(e)
                s2 = s2 + eights(e * r.y3[at, cs].astype(f32))
            gain, shift, scale = thr[0:1, cs], thr[1:2, cs], r.gr3[0:1, cs]
            shift_grad = 0.5 * column_sum(s1)
            gain_grad, k0, k1 = norm_back(n_pix, gain, shift, shift_grad, 0.5 * column_sum(s2), 1.0)
            r.third[0:1, cs] = gain_grad
            r.third[1:2, cs] = shift_grad
            k0, k1, scale = scale * k0, scale * k1, 0.5 * scale
            for at, _, _ in geo.slabs():
                v = scale * br[at, ls] - (k0 + r.y3[at, cs].astype(f32) * k1)
                r.bg[at, cs] = v.astype(bf16)
        owner = n // per_own

        @pl.when(owner == own)
        def _():
            r.e3[:, lanes((n - owner * per_own) * CHUNK, CHUNK)] = br[...].astype(bf16)

    in_pairs(each, lambda j, p: r.meta[ORDER + p * each + j], load, work)


class Sizes:
    def __init__(self, geo, inner, wide, order_n):
        self.geo, self.inner, self.wide, self.order_n = geo, inner, wide, order_n
        self.mask = VM((MASKS, geo.seg, LANE), f32)
        self.field = VM((geo.rows, LANE), f32)
        self.pair = VM((geo.rows, CHUNK), f32)

    def narrow(self, dtype=bf16):
        return ((self.geo.rows, self.inner), dtype)

    def slim(self, dtype=bf16):
        return ((self.geo.rows, LANE), dtype)

    def broad(self, dtype=bf16):
        return ((self.geo.rows, self.wide), dtype)

    def stacked(self):
        return ((self.geo.rows + 2 * self.geo.step, 3 * self.inner), bf16)

    def parts(self, rows):
        shape = ((self.order_n // 2, rows, LANE), bf16)
        return dict(away=shape, home=shape)

    def middle(self):
        return dict(h2=self.narrow(), d2=self.narrow(), gr2=((1, self.inner), f32), act2_own=self.slim())

    def gate(self, width):
        saved = ((self.geo.rows, width), bf16)
        return dict(h1=saved, d1=saved, plus=saved, slope=saved, diff=self.slim(f32), gr1=((1, width), f32))

    def conv_back_scratch(self, width):
        return dict(
            w_t=VM((3, width, 3 * self.inner), bf16),
            sg=VM(*self.stacked()),
            sgo=VM((self.geo.rows, 3 * LANE), bf16),
            wg=VM((9, self.inner, LANE), bf16),
        )

    def gate_back_scratch(self):
        return dict(mask=self.mask, field=self.field, e=self.field, wide=VM((LANE, self.wide), bf16))


def dma(count):
    return pltpu.SemaphoreType.DMA((count,))


def own_rows_of(prm, layer):
    return prm.at[pl.ds(layer * SLOT, SMALL_ROWS)]


def kernel_gate_own(z, meta, source, x, own_small, after=()):
    geo = z.geo

    def body(r):
        source.start(IN_OWN, r, r.w_in, r.sem.at[0])
        fill_masks(r, geo)
        r.ready("x")
        arrived(r.w_in, r.sem.at[0])
        first_matmul(r, geo, r.x, r.w_in, r.pre)
        gate_forward(r, geo, own_rows_of(r.prm, 0), r.pre)
        r.push("diff")
        r.push("gated")

    return call(
        "gate_own",
        body,
        dict(source.operands(), meta=(meta, SM), x=(x, LATE), prm=(own_small, VM)),
        dict(z.gate(LANE), gated=z.slim()),
        dict(
            field=z.field, act=z.field, mask=z.mask, pre=z.field,
            w_in=VM((z.wide, LANE), bf16), sem=dma(1),
        ),
        flops=4_000_000_000,
        nbytes=6_000_000,
        after=after,
    )


EXTRA = 16


def kernel_conv_own(z, meta, source, gated, chans, own_small, after=()):
    geo = z.geo

    def body(r):
        source.start(CONV_OWN, r, r.w_mid, r.sem.at[0])
        fill_masks(r, geo)
        clear_border(r.g, geo, z.inner, 0, 2)
        for i in range(len(gated)):
            r.ready("gated" + str(i))
            c = chans(i, r.meta[OWN])
            for at, h, w in geo.slabs():
                store_shifted(r.g, r.gated[i][at, :], h, w, c, z.inner, geo, 1)
        r.push("g")
        arrived(r.w_mid, r.sem.at[0])
        conv_matmul(r, geo, r.g, r.w_mid, r.pre)
        cs = slice(0, LANE)
        mean, rr = statistics(r.pre, cs, r, geo)
        prm = own_rows_of(r.prm, 0)
        scale = prm[20:21, cs] * rr
        mul = 0.5 * scale
        add = 0.5 * prm[21:22, cs] - mean * mul
        for at, _, _ in geo.slabs():
            r.half[at, :] = (r.pre[at, cs] * mul + add).astype(bf16)
        near = scale.astype(bf16).astype(f32)
        rows = jnp.concatenate([near, scale - near, jnp.zeros((EXTRA - 2, LANE), f32)], axis=0)
        r.half[geo.rows :, :] = rows.astype(bf16)
        r.push("half")

    return call(
        "conv_own",
        body,
        dict(
            source.operands(), meta=(meta, SM), prm=(own_small, VM),
            gated=[(item, LATE) for item in gated],
        ),
        dict(g=z.stacked(), half=((geo.rows + EXTRA, LANE), bf16)),
        dict(mask=z.mask, pre=z.field, w_mid=VM((3, 3, z.inner, LANE), bf16), sem=dma(1)),
        flops=6_000_000_000,
        nbytes=6_000_000,
        after=after,
    )


def kernel_third(z, meta, source, halves, chans, x, thr, after=()):
    geo = z.geo

    def body(r):
        source.start(OUT, r, r.w_out, r.sem.at[0])
        fill_masks(r, geo)
        own = r.meta[OWN]
        for i in range(len(halves)):
            r.ready("halves" + str(i))
            c = chans(i, r.meta[OWN])
            cs = lanes(c * LANE)
            for at, _, _ in geo.slabs():
                half = r.halves[i][at, :]
                act, slope = silu_parts(half.astype(f32))
                r.h2[at, cs] = half
                r.d2[at, cs] = slope.astype(bf16)
                r.act2[at, cs] = act.astype(bf16)
            tail = r.halves[i][geo.rows :, :].astype(f32)
            r.gr2[0:1, cs] = tail[0:1] + tail[1:2]

            @pl.when(c == own)
            def _():
                own_masked(r, geo, cs)

        for name in ("h2", "d2", "act2_own"):
            r.push(name)
        r.ready("x")
        arrived(r.w_out, r.sem.at[0])
        third_forward(r, geo, r.thr, r.act2, r.w_out, r.x)

    return call(
        "third_forward",
        body,
        dict(
            source.operands(), meta=(meta, SM), thr=(thr, VM),
            halves=[(item, LATE) for item in halves], x=(x, LATE),
        ),
        dict(
            z.middle(), y3=z.broad(), d3=z.broad(), x_next=z.broad(), gr3=((1, z.wide), f32),
        ),
        dict(
            mask=z.mask, w_out=VM((z.inner, z.wide), bf16), act2=VM(*z.narrow()), br0=z.pair, br1=z.pair,
            sem=dma(1),
        ),
        flops=12_000_000_000,
        nbytes=16_000_000,
        after=after,
    )


def kernel_top(z, meta, source, x, prm, thr, grad_low, bias, after=()):
    geo = z.geo

    def body(r):
        source.start(IN, r, r.w_in, r.sem.at[0])
        source.start(CONV, r, r.w_mid, r.sem.at[1])
        source.start(OUT, r, r.w_out, r.sem.at[2])
        source.start(HEAD, r, r.w_head, r.sem.at[3])
        source.start(CONV_T, r, r.w_t, r.sem.at[4])
        fill_masks(r, geo)
        r.ready("x")
        arrived(r.w_in, r.sem.at[0])
        first_matmul(r, geo, r.x, r.w_in, r.pre)
        gate_forward(r, geo, r.prm, r.pre)
        r.push("diff")
        arrived(r.w_mid, r.sem.at[1])
        conv_matmul(r, geo, r.g, r.w_mid, r.pre)
        middle_forward(r, geo, r.prm, r.pre, r.act2)
        arrived(r.w_out, r.sem.at[2])
        source.wait_head(r.w_head, r.sem.at[3])
        r.pg[...] = dot(r.grad[...], r.w_head[...])[0:1] / pixel_count(r, geo)
        third_both(r, geo, r.thr, r.act2, r.w_out, r.x, r.pg, [r.away, r.home])
        low = jnp.broadcast_to(r.pooled[...].astype(bf16), (16, z.wide))
        r.logits[...] = dot_nt(low, r.w_head[...])[0:8] + r.bias[...]
        r.pooled_out[...] = r.pooled[...]
        third_products(r, geo, r.act2_own, r.w_out, [r.away, r.home], 576)
        conv_backward(r, geo, r.prm, lambda c: None, r.w_t, r.sem.at[4], [r.away, r.home], True)

    row = ((1, z.wide), f32)
    return call(
        "top_both",
        body,
        dict(
            source.operands(), meta=(meta, SM), x=(x, LATE), prm=(prm, VM), thr=(thr, VM),
            grad=(grad_low, VM), bias=(bias, VM),
        ),
        dict(
            z.gate(z.inner), **z.parts(832 + HEAD_ROWS), g=z.stacked(), d3=z.broad(), pg=row, pooled_out=row,
            logits=((8, bias.shape[1]), f32), third=((2, z.wide), f32), gg=z.narrow(), small2=((2, LANE), f32),
        ),
        dict(
            z.conv_back_scratch(z.inner),
            **{name: VM(*value) for name, value in z.middle().items()},
            field=z.field, act=z.field, mask=z.mask, br0=z.pair, br1=z.pair, e=z.pair,
            pooled=VM(*row), ag2=VM(*z.narrow()), pre=VM(*z.narrow(f32)), act2=VM(*z.narrow()),
            w_in=VM((z.wide, z.inner), bf16), w_mid=VM((3, 3, z.inner, z.inner), bf16),
            w_out=VM((z.inner, z.wide), bf16), w_head=VM((bias.shape[1], z.wide), bf16),
            bg=VM(*z.broad()), wide=VM((LANE, z.wide), bf16), sem=dma(5),
        ),
        flops=60_000_000_000,
        nbytes=30_000_000,
        after=after,
    )


def gate_back_ins(kept, prm):
    ins = {name: (getattr(kept, name), SLICED) for name in ("plus", "slope", "h1", "d1")}
    return dict(ins, diff=(kept.diff, LATE), gr1=(kept.gr1, VM), prm=(prm, VM))


def kernel_join(z, meta, source, source_below, kept, below, prm, thr, x, after=()):
    geo = z.geo

    def body(r):
        source.start(IN, r, r.w_in, r.sem.at[0])
        r.start_rest()
        source_below.start(OUT, r, r.w_out, r.sem.at[1])
        fill_masks(r, geo)
        gate_backward(r, geo, r.prm)
        arrived(r.w_in, r.sem.at[0])
        third_backward(r, geo, r.thr, r.w_in, r.pg, z.order_n // 2)
        r.push("e3")
        r.ready("x")
        first_products(r, geo, r.x, [r.away, r.home])
        arrived(r.w_out, r.sem.at[1])
        third_products(r, geo, r.act2_own, r.w_out, [r.away, r.home], 256)

    return call(
        "join_backward",
        body,
        dict(
            {**source.operands(), **source_below.operands()},
            **gate_back_ins(kept, prm), meta=(meta, SM), gg=(kept.gg, SLICED), thr=(thr, VM), pg=(kept.pg, VM),
            d3_next=(kept.d3, ORDERED), d3=(below.d3, ORDERED), y3=(below.y3, ORDERED), gr3=(below.gr3, VM),
            x=(x, LATE), act2_own=(below.act2_own, VM),
        ),
        dict(
            z.parts(512), small=((SMALL_ROWS, LANE), f32), third=((2, z.wide), f32), ag2=z.narrow(),
            e3=((geo.rows, z.wide // 4), bf16),
        ),
        dict(
            z.gate_back_scratch(), fg=VM(*z.narrow()), w_in=VM((z.wide, z.inner), bf16),
            w_out=VM((z.inner, z.wide), bf16), br0=z.pair, br1=z.pair, bg=VM(*z.broad()), sem=dma(2),
        ),
        flops=20_000_000_000,
        nbytes=30_000_000,
        after=after,
    )


def kernel_conv_back(z, meta, source, ag2, kept, g, prm, after=()):
    geo = z.geo

    def body(r):
        source.start(CONV_ROWS, r, r.w_t, r.sem.at[0])
        fill_masks(r, geo)
        conv_backward(r, geo, r.prm, r.ready_lanes, r.w_t, r.sem.at[0], [r.away, r.home], False)

    return call(
        "conv_backward",
        body,
        dict(
            source.operands(), meta=(meta, SM), ag2=(ag2, SLICED), d2=(kept.d2, SLICED), h2=(kept.h2, SLICED),
            gr2=(kept.gr2, VM), prm=(prm, VM), g=(g, LATE),
        ),
        dict(z.parts(576), gg=z.slim(), small2=((2, LANE), f32)),
        dict(z.conv_back_scratch(LANE), mask=z.mask, e=z.field, sem=dma(1)),
        flops=12_000_000_000,
        nbytes=16_000_000,
        after=after,
    )


def kernel_bottom(z, meta, gg, kept, own_small, x, seconds, join_small, thirds, after=()):
    geo = z.geo
    per = thirds[0].shape[1] // 4 // LANE
    total = -(-(2 * SMALL_ROWS + 4 + 4 * per) // 16) * 16

    def body(r):
        fill_masks(r, geo)
        gate_backward(r, geo, own_rows_of(r.prm, 0))
        r.push("fg")
        pieces = [r.small[...], r.join_small[...]] + [ref[...] for ref in r.seconds]
        for ref in r.thirds:
            own = r.meta[OWN] * per * LANE
            for k in range(2):
                pieces += [ref[k : k + 1, lanes(own + n * LANE)] for n in range(per)]
        filled = 2 * SMALL_ROWS + 4 + 4 * per
        pieces.append(jnp.zeros((total - filled, LANE), f32))
        both = jnp.concatenate(pieces, axis=0).astype(bf16)
        for ref in (r.away, r.home):
            for place in range(ref.shape[0]):
                ref[place, 256:, :] = both
        r.ready("x")
        first_products(r, geo, r.x, [r.away, r.home])
        r.push("away")
        r.push("home")

    return call(
        "bottom_backward",
        body,
        dict(
            gate_back_ins(kept, own_small), meta=(meta, SM), gg=(gg, SLICED), x=(x, LATE),
            join_small=(join_small, VM), seconds=[(item, VM) for item in seconds],
            thirds=[(item, VM) for item in thirds],
        ),
        dict(z.parts(256 + total), fg=z.slim()),
        dict(z.gate_back_scratch(), small=VM((SMALL_ROWS, LANE), f32)),
        flops=4_000_000_000,
        nbytes=10_000_000,
        after=after,
    )


def kernel_input_grad(z, meta, source, fgs, chans, e3, after=()):
    geo = z.geo
    quarter = e3.shape[1]

    def body(r):
        source.start(IN_ROWS, r, r.w_in, r.sem.at[0])
        for i in range(len(fgs)):
            r.ready("fgs" + str(i))
            r.fg[:, lanes(chans(i, r.meta[OWN]) * LANE)] = r.fgs[i][...]
        r.ready("e3")
        arrived(r.w_in, r.sem.at[0])
        r.x_grad[...] = (dot_nt(r.fg[...], r.w_in[...]) + 0.5 * r.e3[...].astype(f32)).astype(bf16)
        r.push("x_grad")

    return call(
        "input_grad",
        body,
        dict(
            source.operands(), meta=(meta, SM), fgs=[(item, LATE) for item in fgs],
            e3=(e3, LATE),
        ),
        dict(x_grad=((geo.rows, quarter), bf16)),
        dict(w_in=VM((quarter, z.inner), bf16), fg=VM(*z.narrow()), sem=dma(1)),
        flops=1_000_000_000,
        nbytes=8_000_000,
        after=after,
    )


def fold(pairs, stack_rows=0, after=()):
    slots = pairs[0][1].shape[0]
    rows = [home.shape[1] for _, home in pairs]
    total = sum(rows) + stack_rows

    def body(r):
        for k, out in enumerate(r.s):
            row = 0
            for i in range(len(pairs)):
                n = i * slots + k
                for name in ("x", "h"):
                    r.ready(name + str(n))
                added = rows[i] - (stack_rows if i == 0 else 0)
                out[row : row + added] = (r.x[n][:added].astype(f32) + r.h[n][:added].astype(f32)).astype(bf16)
                row += added
                if i == 0 and stack_rows:
                    out[row : row + stack_rows] = r.h[n][added:]
                    out[row + stack_rows : row + 2 * stack_rows] = r.x[n][added:]
                    row += 2 * stack_rows
            r.push("s" + str(k))

    outs = dict(s=[((total, LANE), bf16)] * slots)
    ins = dict(
        x=[(recv, LATE, k) for recv, _ in pairs for k in range(slots)],
        h=[(home, LATE, k) for _, home in pairs for k in range(slots)],
    )
    return call("fold", body, ins, outs, {}, after=after).s


def copies(sources, outs, plan, meta=None, after=()):
    ins = dict(a=[(item, HB) for item in sources])
    if meta is not None:
        ins.update(meta=(meta, SM))

    def body(r):
        started = []
        for i, (src, src_at, dst, dst_at) in enumerate(plan):
            if isinstance(src_at, tuple) and src_at[0] is Ellipsis:
                src_at = ((r.meta[CLIP_AT] // 2 - (r.meta[OWN] ^ src_at[1])) % 4,)
            started.append(pltpu.make_async_copy(r.a[src].at[src_at], r.o[dst].at[dst_at], r.sem.at[i]))
            started[-1].start()
        for item, (_, _, dst, dst_at) in zip(started, plan):
            item.wait()
            r.push("o" + str(dst), *(dst_at if isinstance(dst_at, tuple) else (dst_at,)))

    outs = dict(o=[(shape, sources[0].dtype) for shape in outs])
    return call("copies", body, ins, outs, dict(sem=dma(len(plan))), nbytes=2_000_000, after=after).o


class Grid:
    FULL, LOW, HIGH = (0, 1, 2, 5, 6, 7), (3, 8), (4, 9)

    def __init__(self, clip_n, chan_n):
        self.clip_n, self.chan_n = clip_n, chan_n
        self.z_n = clip_n // 2
        self.clip, self.chan = lax.axis_index(CLIP).astype(jnp.int32), lax.axis_index(CHAN).astype(jnp.int32)

    def across_x(self, value):
        return lax.ppermute(value, CLIP, [(i, i ^ 1) for i in range(self.clip_n)])

    def along_z(self, value, k):
        return lax.ppermute(value, CLIP, [(i, (i + 2 * k) % self.clip_n) for i in range(self.clip_n)])

    def across(self, value, flip):
        return lax.ppermute(value, CHAN, [(i, i ^ flip) for i in range(self.chan_n)])

    def column(self, own):
        return [own] + [self.along_z(own, k) for k in range(1, self.z_n)]

    def stack(self, column, cuts, after=()):
        plan = [(k, rows, i, k) for i, rows in enumerate(cuts) for k in range(self.z_n)]
        shapes = [(self.z_n, rows.stop - rows.start, LANE) for rows in cuts]
        return copies(column, shapes, plan, after=after)

    def corner(self, plane, cut, after=()):
        rows = plane[0].shape[1]
        whole = slice(None)
        plan = [(0, (whole, slice(0, cut)), 0, whole), (1, (whole, slice(cut, rows)), 1, whole)]
        shapes = [(self.z_n, cut, LANE), (self.z_n, rows - cut, LANE)]
        low, high = copies(plane[1:], shapes, plan, after=after)
        turned = [self.across(low, 2), self.across_x(high)]
        arrays = list(plane) + turned
        return arrays + [self.across(item, 1) for item in arrays]

    def all_chans(self, own, first=None):
        over_y = self.across(own, 2)
        if first is not None:
            over_y, _ = lax.optimization_barrier((over_y, first))
        return [own, over_y, self.across(own, 1), self.across(over_y, 1)]

    def send_z(self, shares):
        return [shares[0]] + [self.along_z(shares[k], k) for k in range(1, self.z_n)]


FLIPS = (0, 2, 1, 3)


def pack(names, masters, head=None, small=None, meta=None, after=()):
    ins = {n: (masters[n.rstrip(DIGITS)], LATE, layer) for n, layer in names.items()}
    rows = dict(first=256, conv=576, out=256, out1=256, head=2 * HEAD_PART, small=2 * SMALL_PART)
    scratch = {}
    if head is not None:
        ins.update(head=(head, VM), small=(small, VM), meta=(meta, SM))
        scratch.update(padded=VM((4 * HEAD_PART, head.shape[1]), f32))

    def body(r):
        row = 0
        for n in ins:
            if n in names:
                r.ready(n)
            if n == "first":
                r.p[row : row + 256] = r.first[...].astype(bf16)
            elif n == "conv":
                for tap in range(9):
                    r.p[row + tap * 64 : row + tap * 64 + 64] = r.conv[tap // 3, tap % 3].astype(bf16)
            elif n.startswith("out"):
                for half in range(2):
                    block = getattr(r, n)[:, half * LANE : (half + 1) * LANE].astype(bf16)
                    r.p[row + half * LANE : row + (half + 1) * LANE] = block
            elif n == "head":
                r.padded[...] = jnp.zeros_like(r.padded)
                r.padded[: head.shape[0], :] = r.head[...]
                own = r.padded[rows_at(r.meta[OWN] * HEAD_PART, HEAD_PART, 16), :].astype(bf16)
                for half in range(2):
                    at = row + half * HEAD_PART
                    r.p[at : at + HEAD_PART] = own[:, half * LANE : (half + 1) * LANE]
            elif n == "small":
                part = r.small[rows_at(r.meta[CLIP_AT] * SMALL_PART, SMALL_PART, 8), :]
                near = part.astype(bf16).astype(f32)
                r.p[row : row + 2 * SMALL_PART] = jnp.concatenate([near, part - near], axis=0).astype(bf16)
            row += rows.get(n, 0)
        r.push("p")

    outs = dict(p=((sum(rows.get(n, 0) for n in ins), LANE), bf16))
    return call("pack", body, ins, outs, scratch, nbytes=2_000_000, after=after).p


def pack_small(items):
    layers = items[0].shape[0]
    items = [jnp.transpose(item, (1, 2, 0, 3)) if item.ndim == 4 else item for item in items]

    def body(r):
        r.s[...] = jnp.zeros_like(r.s)
        for layer in range(layers):
            row = layer * SLOT
            for ref in r.i:
                if len(ref.shape) == 4:
                    for tap in range(9):
                        r.s[row : row + 1] = 0.5 * ref[tap // 3, tap % 3, layer : layer + 1, :]
                        row += 1
                else:
                    for k in range(ref.shape[1] // LANE):
                        r.s[row : row + 1] = ref[layer : layer + 1, k * LANE : (k + 1) * LANE]
                        row += 1

    ins = dict(i=[(item, VM) for item in items])
    return call("pack_small", body, ins, dict(s=((layers * SLOT, LANE), f32)), {}, nbytes=200_000).s


def spread_small(meta, chans, slots, layers, inner, wide, per):
    def body(r):
        for i, ref in enumerate(r.s):
            chan = chans(i, r.meta[OWN])
            for layer in range(layers):
                first = layer * SLOT
                r.prm[layer, :, lanes(chan * LANE)] = ref[first : first + SMALL_ROWS, :]
                for k in range(2):
                    for n in range(per):
                        at = first + 22 + k * per + n
                        r.thr[layer, k : k + 1, lanes((chan * per + n) * LANE)] = ref[at : at + 1, :]

    ins = dict(meta=(meta, SM), s=[(item, VM) for item in slots])
    outs = dict(prm=((layers, SMALL_ROWS, inner), f32), thr=((layers, 2, wide), f32))
    done = call("spread_small", body, ins, outs, {}, nbytes=200_000, direct=True)
    return done.prm, done.thr


def spread_gathered(every, row0, clip_n, chan_n, layers, inner, wide, per):
    def body(r):
        copy = pltpu.make_async_copy(r.every.at[:, pl.ds(row0, 2 * SMALL_PART)], r.part, r.sem.at[0])
        copy.start()
        copy.wait()
        for chan in range(chan_n):
            for clip in range(clip_n):
                rows = r.part[clip * chan_n + chan].astype(f32)
                r.own[clip * SMALL_PART : (clip + 1) * SMALL_PART] = rows[:SMALL_PART] + rows[SMALL_PART:]
            for layer in range(layers):
                first = layer * SLOT
                r.prm[layer, :, chan * LANE : (chan + 1) * LANE] = r.own[first : first + SMALL_ROWS, :]
                for k in range(2):
                    for n in range(per):
                        at = first + 22 + k * per + n
                        to = (chan * per + n) * LANE
                        r.thr[layer, k : k + 1, to : to + LANE] = r.own[at : at + 1, :]

    outs = dict(prm=((layers, SMALL_ROWS, inner), f32), thr=((layers, 2, wide), f32))
    scratch = dict(
        part=VM((clip_n * chan_n, 2 * SMALL_PART, LANE), bf16), own=VM((layers * SLOT, LANE), f32), sem=dma(1)
    )
    ins = dict(every=(every, HB))
    done = call("spread_small", body, ins, outs, scratch, nbytes=200_000, direct=True)
    return done.prm, done.thr


def wait_all(r, *names):
    for n in names:
        for k in range(4):
            r.ready(n + str(k))


def four(refs, rows):
    a, b, c, d = [ref[rows].astype(f32) for ref in refs]
    return (a + c) + (b + d)


def finish_upper(shares1, shares2, layers, classes, after=()):
    def body(r):
        wait_all(r, "one", "two")
        for half in range(2):
            cs = slice(half * LANE, (half + 1) * LANE)
            r.out_grad[layers - 1, :, cs] = four(r.one, slice(576 + half * LANE, 576 + (half + 1) * LANE))
            r.out_grad[0, :, cs] = four(r.two, slice(256 + half * LANE, 256 + (half + 1) * LANE))
        pooled, grads, total = [], [], []
        for ref in r.one:
            own, other = ref[832:848].astype(f32), ref[848:864].astype(f32)
            for v in (own, other):
                pooled.append(jnp.concatenate([v[0:1], v[1:2]], axis=1))
                grads.append(jnp.concatenate([v[2:3], v[3:4]], axis=1))
            total.append(grads[-2] + grads[-1])
        pooled = jnp.concatenate(pooled, axis=0).astype(bf16)
        grads = jnp.concatenate(grads, axis=0).astype(bf16)
        r.head_grad[...] = dot_tn(grads, pooled)[:classes]
        r.bias_grad[...] = (total[0] + total[2]) + (total[1] + total[3])

    outs = dict(
        out_grad=((layers, LANE, 256), f32), head_grad=((classes, 256), f32), bias_grad=((1, 256), f32)
    )
    ins = dict(one=[(item, LATE) for item in shares1], two=[(item, LATE) for item in shares2])
    return call("finish_upper", body, ins, outs, {}, nbytes=4_000_000, after=after, direct=True)


def finish_lower(shares, layers, smalls, after=()):
    def body(r):
        wait_all(r, "one", "two", "last")
        for layer, refs in ((0, r.last), (layers - 1, r.one)):
            for tap in range(9):
                r.conv_grad[layer, tap // 3, tap % 3] = four(refs, slice(tap * 64, (tap + 1) * 64))
        r.push("conv_grad")
        r.in_grad[0] = four(r.last, slice(576, 832))
        r.in_grad[layers - 1] = four(r.two, slice(0, 256))
        r.push("in_grad")
        r.sum[...] = four(r.last, slice(832, r.last[0].shape[0]))
        for out, (rows, shape) in zip(r.small, smalls):
            for layer, row in enumerate(rows):
                if len(shape) == 4:
                    for tap in range(9):
                        out[tap // 3, tap % 3, layer : layer + 1] = r.sum[row + tap : row + tap + 1, :]
                else:
                    for k in range(shape[1] // LANE):
                        out[layer : layer + 1, k * LANE : (k + 1) * LANE] = r.sum[row + k : row + k + 1, :]

    one, two, last = [[(item, LATE) for item in group] for group in shares]
    shapes = [(3, 3, shape[0], LANE) if len(shape) == 4 else shape for _, shape in smalls]
    outs = dict(
        in_grad=((layers, 256, LANE), f32), conv_grad=((layers, 3, 3, 64, LANE), f32),
        small=[(shape, f32) for shape in shapes],
    )
    scratch = dict(sum=VM((shares[2][0].shape[0] - 832, LANE), f32))
    ins = dict(one=one, two=two, last=last)
    done = call("finish_lower", body, ins, outs, scratch, nbytes=4_000_000, after=after)
    small = [jnp.transpose(item, (2, 0, 1, 3)) if item.ndim == 4 else item for item in done.small]
    return done.in_grad, done.conv_grad, small


def local(
    clip_input,
    seg_count,
    proj_in_master,
    conv_master,
    proj_out_master,
    head_master,
    gain_first,
    shift_first,
    taps_near,
    taps_far,
    gain_second,
    shift_second,
    gain_third,
    shift_third,
    head_bias,
    logit_grad,
    clip_n,
    chan_n,
):
    grid = Grid(clip_n, chan_n)
    clip, chan = grid.clip, grid.chan
    _, seg, high_map, wide_map, wide = clip_input.shape
    layers = proj_in_master.shape[0]
    inner = proj_in_master.shape[2] * chan_n
    classes = head_master.shape[1]
    class_pad = -(-classes // LANE) * LANE
    geo = Geometry(seg, high_map, wide_map)
    order_n = wide // CHUNK
    z = Sizes(geo, inner, wide, order_n)
    third_rows = wide // chan_n // LANE
    direct = clip_n == 8 and chan_n == 4 and proj_in_master.shape[1] == 256

    grad_low = logit_grad.astype(bf16)
    grad_rows = jnp.pad(grad_low, ((0, 15), (0, class_pad - classes)))
    bias_row = jnp.pad(head_bias, (0, class_pad - classes))[None]
    order = jnp.arange(order_n, dtype=jnp.int32)
    chans = lambda i, own: i
    if direct:
        z_to = (clip // 2 + jnp.arange(4, dtype=jnp.int32)) % 4
        order = jnp.concatenate([z_to * 2 + ((clip % 2) ^ 1), z_to * 2 + clip % 2]).astype(jnp.int32)
        chans = lambda i, own: own ^ FLIPS[i]
    meta = jnp.concatenate([seg_count.astype(jnp.int32), chan[None], clip[None], order])
    x0 = jnp.transpose(clip_input[0], (1, 2, 0, 3)).reshape(geo.rows, wide)
    own_small = pack_small(
        [
            gain_first,
            shift_first,
            taps_near,
            taps_far,
            gain_second,
            shift_second,
            gain_third,
            shift_third,
        ]
    )

    def gather_chan(own):
        if direct:
            return grid.all_chans(own)
        every = lax.all_gather(own, CHAN, axis=0, tiled=False)
        return [every[i] for i in range(chan_n)]

    if direct:
        masters = dict(first=proj_in_master, conv=conv_master, out=proj_out_master)
        packed = pack(dict(out=0, out1=1), masters, head_master.T, own_small, meta)
        by_core = lax.all_gather(packed, (CLIP, CHAN), axis=0, tiled=False)
        prm, thr = spread_gathered(by_core, 512 + 2 * HEAD_PART, clip_n, chan_n, layers, inner, wide, third_rows)
        numbers = in_order(chan_n)
        near = [along_column(0, 0), along_column(1, 0)]
        corners = [(0, 0), (1, 0), (0, 2), (1, 2), (1, 2)]
        places = [along_column(dx, flip ^ core) for core in (0, 1) for dx, flip in corners]
        full, low_part, high_part = grid.FULL, grid.LOW, grid.HIGH

        own_in = pack(dict(first=0), masters, after=[packed])
        column_in = grid.column(own_in)
        own_mid = pack(dict(conv=0), masters, after=[own_in])
        (in_a,) = grid.stack(column_in, [slice(0, 256)], after=[own_mid])
        in_x = grid.across_x(in_a)
        column_mid = grid.column(own_mid)
        in_source = Slots("wa", [in_a, in_x], near, {IN_OWN: [(0, 0, 0, 256), (1, 0, 0, 256)]}, chan_n)
        gate0 = kernel_gate_own(z, meta, in_source, x0, own_small)
        (conv_a,) = grid.stack(column_mid, [slice(0, 576)], after=[gate0.gr1])
        conv_x = grid.across_x(conv_a)
        own_up = pack(dict(first=1, conv=1), masters, after=[conv_a])
        column_up = grid.column(own_up)
        gated = grid.all_chans(gate0.gated, own_up)
        mid_source = Slots("wb", [conv_a, conv_x], near, {CONV_OWN: [(0, 0, 0, 9), (1, 0, 0, 9)]}, chan_n)
        conv0 = kernel_conv_own(z, meta, mid_source, gated, chans, own_small, after=[own_up])
        halves = gather_chan(conv0.half)

        (stack_up,) = grid.stack(column_up, [slice(0, 832)], after=[halves[1]])
        plane_up = [stack_up, grid.across_x(stack_up), grid.across(stack_up, 2)]
        plan = []
        for i in range(4):
            for k in range(2):
                plan.append((k, (..., FLIPS[i]), i, (k, slice(0, 256))))
                plan.append((2 + k, (..., FLIPS[i]), i, (k, slice(256, 832))))
        sent = copies([in_a, in_x, conv_a, conv_x], [(2, 832, LANE)] * 4, plan, meta, after=[stack_up])
        out_source = Slots("wc", [by_core], [numbers], {OUT: [(0, 0, 0, 2)]}, chan_n)
        third0 = kernel_third(z, meta, out_source, halves, chans, x0, thr[0], after=sent[:1])
        arrays_up = grid.corner(plane_up, 448, after=[third0.gr3])
        last = len(arrays_up)
        parts = {
            IN: [(i, 0, 0, 256) for i in full + low_part],
            CONV: [(i, 256, 0, 9) for i in full] + [(i, 256, 0, 3) for i in low_part]
            + [(i, 0, 3, 6) for i in high_part],
            OUT: [(last, 256, 0, 2)],
            HEAD: [(last, 512, 0, 2)],
        }
        parts[CONV_T] = parts[CONV]
        top_source = Slots("wd", arrays_up + [by_core], places + [numbers], parts, chan_n)
    else:
        prm, thr = spread_small(meta, chans, gather_chan(own_small), layers, inner, wide, third_rows)
        head_low = jnp.pad(head_master.astype(bf16), ((0, 0), (0, class_pad - classes)))
        head_low = lax.all_gather(head_low.T, CLIP, axis=1, tiled=True)
        gathered, own_cols = [], []
        for master, clip_axis, chan_axis in ((proj_in_master, 1, 2), (conv_master, 3, 4), (proj_out_master, 2, 1)):
            own_cols.append(lax.all_gather(master.astype(bf16), CLIP, axis=clip_axis, tiled=True))
            gathered.append(lax.all_gather(own_cols[-1], CHAN, axis=chan_axis, tiled=True))
        in_source = Whole("wa", {IN_OWN: own_cols[0][0]})
        mid_source = Whole("wb", {CONV_OWN: own_cols[1][0]})
        out_source = Whole("wc", {OUT: gathered[2][0]})
        top_source = Whole("wd", {IN: gathered[0][1], CONV: gathered[1][1], OUT: gathered[2][1], HEAD: head_low})
        wide_own, inner_own = wide // chan_n, inner // chan_n
        in_rows = lax.dynamic_slice_in_dim(gathered[0][0], chan * wide_own, wide_own, 0)
        conv_rows = lax.dynamic_slice_in_dim(gathered[1][0], chan * inner_own, inner_own, 2)
        rows_source = Whole("we", {IN_ROWS: in_rows, CONV_ROWS: conv_rows})
        gate0 = kernel_gate_own(z, meta, in_source, x0, own_small)
        conv0 = kernel_conv_own(z, meta, mid_source, gather_chan(gate0.gated), chans, own_small)
        third0 = kernel_third(z, meta, out_source, gather_chan(conv0.half), chans, x0, thr[0])

    x1 = third0.x_next
    top = kernel_top(z, meta, top_source, x1, prm[1], thr[1], grad_rows, bias_row)
    after_join, after_mid, after_low = [], [], []
    if direct:
        *sent, _ = lax.optimization_barrier((*sent, top.third))
        rows_a = sent[:1] + [grid.across(item, flip) for item, flip in zip(sent[1:], FLIPS[1:])]
        parts = {IN_ROWS: [(i, 0, 0, 256) for i in range(4)], CONV_ROWS: [(i, 256, 0, 9) for i in range(4)]}
        rows_source = Slots("we", rows_a, [own_pair(flip) for flip in FLIPS], parts, chan_n)
    join = kernel_join(z, meta, top_source, out_source, top, third0, prm[1], thr[0], x1, after=after_join)
    if direct:
        away1, away2 = grid.across_x(top.away), grid.across_x(join.away)
        folded1 = fold([(away1, top.home)], HEAD_ROWS, after=[join.third])
        shares1 = grid.send_z(folded1)
        after_mid = folded1[:1]
    mid0 = kernel_conv_back(z, meta, rows_source, join.ag2, third0, conv0.g, prm[0], after=after_mid)
    if direct:
        folded2 = fold([(away2, join.home)], after=[mid0.small2])
        shares2 = grid.send_z(folded2)
        after_low = folded2[:1] + shares1[1:]
    low = kernel_bottom(
        z, meta, mid0.gg, gate0, own_small, x0, [mid0.small2, top.small2], join.small, [join.third, top.third],
        after=after_low,
    )

    at = 2 * SMALL_ROWS
    small_places = [
        ((0, SMALL_ROWS), gain_first.shape),
        ((1, SMALL_ROWS + 1), shift_first.shape),
        ((2, SMALL_ROWS + 2), taps_near.shape),
        ((11, SMALL_ROWS + 11), taps_far.shape),
        ((at, at + 2), gain_second.shape),
        ((at + 1, at + 3), shift_second.shape),
        ((at + 4, at + 4 + 2 * third_rows), gain_third.shape),
        ((at + 4 + third_rows, at + 4 + 3 * third_rows), shift_third.shape),
    ]
    if direct:
        away3, away4 = grid.across_x(mid0.away), grid.across_x(low.away)
        folded3 = fold([(away3, mid0.home), (away4, low.home)])
        shares3 = grid.send_z(folded3)
        upper = finish_upper(shares1, shares2, layers, classes, after=folded3[:1])
        x_grad = kernel_input_grad(z, meta, rows_source, gather_chan(low.fg), chans, join.e3).x_grad
        in_share, mid_share, small_grads = finish_lower(
            [shares1, shares2, shares3], layers, small_places, after=[x_grad]
        )
        out_share = upper.out_grad
        head_share, bias_grad = upper.head_grad.T, upper.bias_grad[0, :classes]
    else:
        pooled_all = lax.all_gather(top.pooled_out.astype(bf16), CLIP, axis=0, tiled=True)
        grad_all = lax.all_gather(grad_low, CLIP, axis=0, tiled=True)
        own_rows = head_master.shape[0]
        pooled_own = lax.dynamic_slice_in_dim(pooled_all, clip * own_rows, own_rows, 1)
        head_share = dot_tn(pooled_own, grad_all)
        bias_grad = jnp.sum(grad_all.astype(f32), axis=0)

        def joined(item, first, rows):
            return jnp.concatenate([item.away, item.home], axis=0)[:, first : first + rows]

        in_terms = jnp.stack([joined(low, 0, 256), joined(join, 0, 256)]).reshape(layers, wide, LANE)
        mid_terms = jnp.stack([joined(mid0, 0, 576), joined(top, 0, 576)])
        mid_terms = mid_terms.reshape(layers, order_n, 3, 3, 64, LANE)
        mid_terms = jnp.transpose(mid_terms, (0, 2, 3, 1, 4, 5)).reshape(layers, 3, 3, inner, LANE)
        out_terms = jnp.stack([joined(join, 256, 256), joined(top, 576, 256)])
        out_terms = out_terms.reshape(layers, order_n, 2, LANE, LANE)
        out_terms = jnp.transpose(out_terms, (0, 3, 1, 2, 4)).reshape(layers, LANE, wide)
        in_share = lax.psum_scatter(in_terms, CLIP, scatter_dimension=1, tiled=True).astype(f32)
        mid_share = lax.psum_scatter(mid_terms, CLIP, scatter_dimension=3, tiled=True).astype(f32)
        out_share = lax.psum_scatter(out_terms, CLIP, scatter_dimension=2, tiled=True).astype(f32)
        small = lax.psum(low.home[0, 256:].astype(f32), CLIP)
        small_grads = []
        for rows, shape in small_places:
            count = 9 if len(shape) == 4 else shape[1] // LANE
            small_grads.append(jnp.stack([small[row : row + count] for row in rows]).reshape(shape))
        x_grad = kernel_input_grad(z, meta, rows_source, gather_chan(low.fg), chans, join.e3).x_grad

    input_grad = x_grad.reshape(high_map, wide_map, seg, -1)
    input_grad = jnp.transpose(input_grad, (2, 0, 1, 3))[None]
    return (
        top.logits[0:1, :classes],
        input_grad,
        in_share,
        mid_share,
        out_share,
        head_share,
        *small_grads,
        bias_grad,
    )


def solution(mesh):
    clip_n, chan_n = mesh.shape[CLIP], mesh.shape[CHAN]

    def program(*args):
        return local(*args, clip_n, chan_n)

    by_clip, by_chan = P(CLIP, None), P(None, CHAN)
    weights = (P(None, CLIP, CHAN), P(None, None, None, CLIP, CHAN), P(None, CHAN, CLIP), by_clip)
    taps = P(None, None, None, CHAN)
    small = (by_chan, by_chan, taps, taps, by_chan, by_chan, by_chan, by_chan, P())
    in_specs = (P(CLIP, None, None, None, None), P(CLIP)) + weights + small + (by_clip,)
    out_specs = (by_clip, P(CLIP, None, None, None, CHAN)) + weights + small
    return jax.shard_map(program, mesh=mesh, in_specs=in_specs, out_specs=out_specs, check_vma=False)
```

```python
import types

import jax
import jax.numpy as jnp
from jax import lax
from jax.experimental import pallas as pl
from jax.experimental.pallas import tpu as pltpu
from jax.sharding import PartitionSpec as P

EPS = 1e-05
LANE = 128
CHUNK = 256
SMALL_ROWS = 24
HEAD_ROWS = 16
HEAD_PART = 48
SLOT = 32
SMALL_PART = 8
DIGITS = "01"
MASKS = 3
CLIP, CHAN = "clip", "chan"
bf16 = jnp.bfloat16
f32 = jnp.float32


VM = pltpu.VMEM
SM = pltpu.SMEM
HB = pl.ANY
LATE = object()
SLICED = object()
ORDERED = object()
COUNT, OWN, CLIP_AT, ORDER = 0, 1, 2, 3
Space = types.SimpleNamespace


def _bytes(shape, dtype):
    size = jnp.dtype(dtype).itemsize
    for extent in shape:
        size *= extent
    return size


def _flat(items):
    flat, groups = {}, {}
    for name, item in items.items():
        if isinstance(item, list):
            groups[name] = [name + str(i) for i in range(len(item))]
            flat.update(zip(groups[name], item))
        else:
            flat[name] = item
    return flat, groups


def call(name, body, ins, outs, scratch, flops=0, nbytes=0, after=(), direct=False, settle=False, limit=60):
    ins, in_groups = _flat(dict(ins, unread=[(item, HB) for item in after]))
    outs, out_groups = _flat(outs)
    in_names, out_names = list(ins), list(outs)

    def kind(space):
        return [n for n in in_names if ins[n][1] is space]

    sliced, late, ordered = kind(SLICED), kind(LATE), kind(ORDERED)
    soon = kind(VM) if settle else []
    early = [n for n in out_names if _bytes(*outs[n]) > 65536 and not direct]
    part = {n: ins[n][2] for n in late if len(ins[n]) > 2}
    extra = dict(scratch)
    sems = {}
    for n in soon + sliced + late + ordered:
        shape = ins[n][0].shape
        extra[n] = VM(shape[1:] if n in part else shape, ins[n][0].dtype)
        count = {id(SLICED): shape[-1] // LANE, id(ORDERED): shape[-1] // CHUNK}.get(id(ins[n][1]), 1)
        sems[n] = pltpu.SemaphoreType.DMA((count,))
    for n in early:
        extra[n] = VM(*outs[n])
        sems[n] = pltpu.SemaphoreType.DMA((1,))
    extra_names, sem_names = list(extra), list(sems)

    def kernel(*refs):
        outer = dict(zip(in_names + out_names, refs))
        refs = refs[len(outer) :]
        inner = dict(zip(extra_names, refs))
        sem = dict(zip(sem_names, refs[len(inner) :]))
        every = {**outer, **inner}
        r = Space(**every)
        for group, names in {**in_groups, **out_groups}.items():
            setattr(r, group, [every[n] for n in names])

        def slice_copy(n, c, size):
            cs = lanes(c * size, size)
            return pltpu.make_async_copy(outer[n].at[:, cs], inner[n].at[:, cs], sem[n].at[c])

        def whole_copy(n):
            ref = outer[n].at[part[n]] if n in part else outer[n]
            return pltpu.make_async_copy(ref, inner[n], sem[n].at[0])

        def start_rest():
            if ordered:
                each = ins[ordered[0]][0].shape[1] // CHUNK // 2
                for j in range(each):
                    for p in range(2):
                        for n in ordered:
                            slice_copy(n, r.meta[ORDER + p * each + j], CHUNK).start()
            for n in late:
                whole_copy(n).start()

        def ready_lanes(c):
            for n in sliced:
                slice_copy(n, c, LANE).wait()

        def ready_chunk(chunk):
            for n in ordered:
                slice_copy(n, chunk, CHUNK).wait()

        def ready(n):
            whole_copy(n).wait()

        def push(n, *index):
            if n not in early:
                return
            src, dst = (inner[n].at[index], outer[n].at[index]) if index else (inner[n], outer[n])
            pltpu.make_async_copy(src, dst, sem[n].at[0]).start()

        r.ready, r.ready_lanes, r.ready_chunk, r.push = ready, ready_lanes, ready_chunk, push
        r.start_rest = start_rest
        r.settle = lambda: [whole_copy(n).wait() for n in soon]
        for n in soon:
            whole_copy(n).start()
        for c in range(ins[sliced[0]][0].shape[1] // LANE if sliced else 0):
            for n in sliced:
                slice_copy(n, c, LANE).start()
        if not ordered:
            start_rest()
        body(r)
        for n in early:
            pltpu.make_async_copy(inner[n], outer[n], sem[n].at[0]).wait()

    own = (LATE, SLICED, ORDERED)
    results = pl.pallas_call(
        kernel,
        name=name,
        out_shape=[jax.ShapeDtypeStruct(*outs[n]) for n in out_names],
        in_specs=[pl.BlockSpec(memory_space=HB if ins[n][1] in own or n in soon else ins[n][1]) for n in in_names],
        out_specs=[pl.BlockSpec(memory_space=HB if n in early else VM) for n in out_names],
        scratch_shapes=[extra[n] for n in extra_names] + [sems[n] for n in sem_names],
        compiler_params=pltpu.CompilerParams(vmem_limit_bytes=limit * 1024 * 1024),
        cost_estimate=pl.CostEstimate(flops=flops, bytes_accessed=nbytes, transcendentals=0),
    )(*[ins[n][0] for n in in_names])
    done = dict(zip(out_names, results))
    for group, names in out_groups.items():
        done[group] = [done[n] for n in names]
    return Space(**done)


def lanes(start, size=LANE):
    return pl.ds(pl.multiple_of(start, LANE), size)


def rows_at(start, size, unit):
    return pl.ds(pl.multiple_of(start, unit), size)


def dot(a, b):
    return jnp.dot(a, b, preferred_element_type=f32)


def dot_nt(a, b):
    return lax.dot_general(a, b, (((1,), (1,)), ((), ())), preferred_element_type=f32)


def dot_tn(a, b):
    return lax.dot_general(a, b, (((0,), (0,)), ((), ())), preferred_element_type=f32)


class Geometry:
    def __init__(self, seg, high, wide):
        self.seg, self.high, self.wide = seg, high, wide
        self.step = seg * wide
        self.rows = high * self.step

    def slab(self, h, w, first=0):
        start = first + (h * self.wide + w) * self.seg
        return slice(start, start + self.seg)

    def slabs(self):
        for h in range(self.high):
            for w in range(self.wide):
                yield self.slab(h, w), h, w


def fill_masks(r, geo):
    r.settle()
    count = r.meta[COUNT]
    seg = lax.broadcasted_iota(jnp.int32, (geo.seg, LANE), 0)
    r.mask[0] = jnp.where(seg < count, 1.0, 0.0)
    r.mask[1] = jnp.where(seg + 1 < count, 1.0, 0.0)
    r.mask[2] = jnp.where(seg + 1 < count, 0.5, 0.0)


def pixel_count(r, geo):
    return r.meta[COUNT].astype(f32) * float(geo.high * geo.wide)


def column_sum(v):
    return jnp.sum(v, axis=0, keepdims=True)


def zeros8():
    return jnp.zeros((8, LANE), f32)


def eights(v):
    return jnp.sum(v.reshape(v.shape[0] // 8, 8, LANE), axis=0)


def statistics(pre, cs, r, geo):
    n = pixel_count(r, geo)
    pilot = pre[0:1, cs]
    s1, s2 = zeros8(), zeros8()
    m = r.mask[0]
    for at, _, _ in geo.slabs():
        v = (pre[at, cs] - pilot) * m
        s1 = s1 + eights(v)
        s2 = s2 + eights(v * v)
    shift = column_sum(s1) / n
    var = jnp.maximum(column_sum(s2) / n - shift * shift, 0.0)
    return pilot + shift, lax.rsqrt(var + EPS)


def norm_back(n, gain, shift, s1, total, c):
    gain_grad = (c * total - shift * s1) / gain
    k1 = gain_grad / (n * gain)
    return gain_grad, s1 / n - shift * k1, c * k1


IN, CONV, CONV_T, OUT, HEAD, IN_OWN, CONV_OWN, IN_ROWS, CONV_ROWS = range(9)


class Slots:
    def __init__(self, name, arrays, rules, parts, chan_n):
        self.name, self.arrays, self.rules, self.parts, self.chan_n = name, arrays, rules, parts, chan_n

    def operands(self):
        return {self.name: [(array, HB) for array in self.arrays]}

    def start(self, kind, r, dst, sem):
        refs = getattr(r, self.name)
        own = r.meta[OWN]
        for no, row0, first, many in self.parts[kind]:
            ref = refs[no]

            def body(s, carry, ref=ref, rule=self.rules[no], row0=row0, first=first, many=many):
                clip, chan = rule(s, r.meta[CLIP_AT], own)

                def copy(src, to):
                    pltpu.make_async_copy(src, to, sem).start()

                if kind in (IN, IN_OWN, IN_ROWS):
                    start = clip * 256 + first - (own * 512 if kind == IN_ROWS else 0)
                    cs = slice(None) if kind == IN_OWN else lanes(chan * LANE)
                    copy(ref.at[s, pl.ds(row0, many)], dst.at[rows_at(start, many, LANE), cs])
                elif kind in (CONV, CONV_OWN, CONV_T, CONV_ROWS):
                    rows = rows_at(clip * 64 - (own * LANE if kind == CONV_ROWS else 0), 64, 64)
                    whole = first % 3 == 0 and many % 3 == 0
                    for a, b, src in self.taps(ref.at[s], row0, first, many, whole):
                        if kind == CONV:
                            copy(src, dst.at[a, b, rows, lanes(chan * LANE)])
                        elif kind == CONV_OWN:
                            copy(src, dst.at[a, b, rows, :])
                        elif whole:
                            for b in range(3):
                                copy(src.at[:, b], dst.at[a, rows, lanes(chan * LANE + b * 512)])
                        else:
                            copy(src, dst.at[a, rows, lanes(chan * LANE + b * 512)])
                elif kind == OUT:
                    for half in range(first, first + many):
                        src = ref.at[s, pl.ds(row0 + (half - first) * LANE, LANE)]
                        copy(src, dst.at[rows_at(chan * LANE, LANE, LANE), lanes(clip * 256 + half * LANE)])
                else:
                    rows = rows_at(chan * HEAD_PART, HEAD_PART, 16)
                    for half in range(2):
                        src = ref.at[s, pl.ds(row0 + half * HEAD_PART, HEAD_PART)]
                        copy(src, dst.at[rows, lanes(clip * 256 + half * LANE)])
                return carry

            lax.fori_loop(0, self.arrays[no].shape[0], body, 0)

    @staticmethod
    def taps(ref, row0, first, many, whole):
        if whole:
            block = ref.at[pl.ds(row0, many * 64)].reshape(many // 3, 3, 64, LANE)
            return [(pl.ds(first // 3, many // 3), slice(None), block)]
        each = range(first, first + many)
        return [(tap // 3, tap % 3, ref.at[pl.ds(row0 + (tap - first) * 64, 64)]) for tap in each]

    def wait_head(self, dst, sem):
        rows = self.chan_n * HEAD_PART
        dst[rows:, :] = jnp.zeros((dst.shape[0] - rows, dst.shape[1]), dst.dtype)
        arrived(dst.at[:rows], sem)


def along_column(dx, flip):
    return lambda s, clip, chan: ((clip // 2 - s) % 4 * 2 + ((clip % 2) ^ dx), chan ^ flip)


def in_order(chan_n):
    return lambda s, clip, chan: (s // chan_n, s % chan_n)


def own_pair(flip):
    return lambda s, clip, chan: (2 * chan + ((clip % 2) ^ s), chan ^ flip)


class Whole:
    def __init__(self, name, arrays):
        self.name, self.arrays = name, arrays

    def operands(self):
        return {self.name: [(array, HB) for array in self.arrays.values()]}

    def start(self, kind, r, dst, sem):
        stored = {CONV_T: CONV}.get(kind, kind)
        ref = getattr(r, self.name)[list(self.arrays).index(stored)]
        if kind in (CONV_T, CONV_ROWS):
            for b in range(3):
                pltpu.make_async_copy(ref.at[:, b], dst.at[:, :, pl.ds(b * 512, 512)], sem).start()
        else:
            pltpu.make_async_copy(ref, dst, sem).start()

    def wait_head(self, dst, sem):
        arrived(dst, sem)


def arrived(dst, sem):
    pltpu.make_async_copy(dst, dst, sem).wait()


def first_matmul(r, geo, x, weight, pre):
    pre[...] = dot(x[...], weight[...])


def conv_matmul(r, geo, g, weight, pre):
    total = None
    for a in range(3):
        w = weight[a].reshape(-1, pre.shape[1])
        part = dot(g[a * geo.step : a * geo.step + geo.rows, :], w)
        total = part if total is None else total + part
    pre[...] = total


def clear_border(ref, geo, width, left, right):
    zero = jnp.zeros((geo.step, ref.shape[1]), ref.dtype)
    ref[: geo.step, :] = zero
    ref[geo.rows + geo.step :, :] = zero
    side = jnp.zeros((geo.seg, width), ref.dtype)
    for h in range(geo.high):
        ref[geo.slab(h, 0, geo.step), left * width : (left + 1) * width] = side
        ref[geo.slab(h, geo.wide - 1, geo.step), right * width : (right + 1) * width] = side


def store_shifted(ref, value, h, w, c, width, geo, sign):
    value = value.astype(bf16)
    for b in range(3):
        to = w - sign * (b - 1)
        if 0 <= to < geo.wide:
            ref[geo.slab(h, to, geo.step), lanes(b * width + c * LANE)] = value


def taps_sum(field, prm, cs, h, w, geo, sign):
    total = None
    for a in range(3):
        for b in range(3):
            for first, reach in ((2, 1), (11, 2)):
                dh, dw = h + sign * reach * (a - 1), w + sign * reach * (b - 1)
                if not (0 <= dh < geo.high and 0 <= dw < geo.wide):
                    continue
                term = field[geo.slab(dh, dw), :] * prm[first + 3 * a + b : first + 1 + 3 * a + b, cs]
                total = term if total is None else total + term
    return total


def silu_parts(half):
    t = jnp.tanh(half)
    out = half * t + half
    return out, (1.0 + out) + t * (1.0 - out)


def gate_forward(r, geo, prm, pre):
    width = pre.shape[1]
    whole = width > LANE
    own = r.meta[OWN] if whole else 0
    if whole:
        clear_border(r.g, geo, width, 0, 2)

    def body(c, carry):
        cs = lanes(c * LANE)
        mean, rr = statistics(pre, cs, r, geo)
        gain, shift = prm[0:1, cs], prm[1:2, cs]
        scale = gain * rr
        r.gr1[0:1, cs] = scale
        mul = 0.5 * scale
        add = 0.5 * shift - mean * mul
        next_valid = r.mask[1]
        for at, _, _ in geo.slabs():
            half = pre[at, cs] * mul + add
            act, slope = silu_parts(half)
            r.h1[at, cs] = half.astype(bf16)
            r.d1[at, cs] = slope.astype(bf16)
            r.act[at, :] = act
            r.field[at, :] = (pltpu.roll(act, geo.seg - 1, axis=0) - act) * next_valid

        @pl.when(c == own)
        def _():
            r.diff[...] = r.field[...]

        for at, h, w in geo.slabs():
            t = jnp.tanh(taps_sum(r.field, prm, cs, h, w, geo, 1))
            act = r.act[at, :]
            plus = 1.5 + 0.5 * t
            r.plus[at, cs] = plus.astype(bf16)
            r.slope[at, cs] = (act - act * (t * t)).astype(bf16)
            if whole:
                store_shifted(r.g, act * plus, h, w, c, width, geo, 1)
            else:
                r.gated[at, :] = (act * plus).astype(bf16)
        for name in ("h1", "d1", "plus", "slope"):
            r.push(name, slice(None), cs)
        for b in range(3 if whole else 0):
            r.push("g", slice(None), lanes(b * width + c * LANE))
        return carry

    lax.fori_loop(0, width // LANE, body, 0)


def own_masked(r, geo, cs):
    m = r.mask[0]
    for at, _, _ in geo.slabs():
        r.act2_own[at, :] = (r.act2[at, cs].astype(f32) * m).astype(bf16)


def middle_forward(r, geo, prm, pre, act2):
    own = r.meta[OWN]

    def body(c, carry):
        cs = lanes(c * LANE)
        mean, rr = statistics(pre, cs, r, geo)
        gain, shift = prm[20:21, cs], prm[21:22, cs]
        scale = gain * rr
        r.gr2[0:1, cs] = scale
        mul = 0.5 * scale
        add = 0.5 * shift - mean * mul
        for at, _, _ in geo.slabs():
            half = pre[at, cs] * mul + add
            act, slope = silu_parts(half)
            r.h2[at, cs] = half.astype(bf16)
            r.d2[at, cs] = slope.astype(bf16)
            act2[at, cs] = act.astype(bf16)

        @pl.when(c == own)
        def _():
            own_masked(r, geo, cs)

        r.push("h2", slice(None), cs)
        r.push("d2", slice(None), cs)
        return carry

    lax.fori_loop(0, pre.shape[1] // LANE, body, 0)


def in_pairs(count, pick, load, work):
    load(pick(0, 0), 0)

    def step(j, carry):
        load(pick(j, 1), 1)
        work(pick(j, 0), 0, j, 0)
        load(pick(jnp.minimum(j + 1, count - 1), 0), 0)
        work(pick(j, 1), 1, j, 1)
        return carry

    lax.fori_loop(0, count, step, 0)


def third_forward(r, geo, thr, act2, weight, x):
    buffers = [r.br0, r.br1]

    def load(n, slot):
        buffers[slot][...] = dot(act2[...], weight[:, lanes(n * CHUNK, CHUNK)])

    def work(n, slot, j, p):
        br = buffers[slot]
        for half in range(CHUNK // LANE):
            ls = slice(half * LANE, (half + 1) * LANE)
            cs = lanes(n * CHUNK + half * LANE)
            mean, rr = statistics(br, ls, r, geo)
            gain, shift = thr[0:1, cs], thr[1:2, cs]
            mul = gain * rr
            add = shift - mean * mul
            r.gr3[0:1, cs] = mul
            for at, _, _ in geo.slabs():
                y = br[at, ls] * mul + add
                out, slope = silu_parts(0.5 * (x[at, cs].astype(f32) + y))
                r.y3[at, cs] = y.astype(bf16)
                r.d3[at, cs] = slope.astype(bf16)
                r.x_next[at, cs] = out.astype(bf16)
        cs = lanes(n * CHUNK, CHUNK)
        for name in ("y3", "d3", "x_next"):
            r.push(name, slice(None), cs)

    in_pairs(x.shape[1] // CHUNK // 2, lambda j, p: 2 * j + p, load, work)


def third_both(r, geo, thr, act2, weight, x, pg, parts):
    n_pix = pixel_count(r, geo)
    buffers = [r.br0, r.br1]
    each = parts[0].shape[0]

    def load(n, slot):
        buffers[slot][...] = dot(act2[...], weight[:, lanes(n * CHUNK, CHUNK)])

    def work(n, slot, j, p):
        br = buffers[slot]
        for half in range(CHUNK // LANE):
            ls = slice(half * LANE, (half + 1) * LANE)
            cs = lanes(n * CHUNK + half * LANE)
            mean, rr = statistics(br, ls, r, geo)
            gain, shift = thr[0:1, cs], thr[1:2, cs]
            mul = gain * rr
            add = shift - mean * mul
            m = r.mask[0]
            grad = (0.5 * pg[0:1, cs]) * m
            pool, s1, s2 = zeros8(), zeros8(), zeros8()
            for at, _, _ in geo.slabs():
                y = br[at, ls] * mul + add
                out, slope = silu_parts(0.5 * (x[at, cs].astype(f32) + y))
                pool = pool + eights(out * m)
                e = slope * grad
                s1 = s1 + eights(e)
                s2 = s2 + eights(e * y)
                br[at, ls] = y
                r.e[at, ls] = e
                r.d3[at, cs] = slope.astype(bf16)
            shift_grad = column_sum(s1)
            gain_grad, k0, k1 = norm_back(n_pix, gain, shift, shift_grad, column_sum(s2), 1.0)
            r.pooled[0:1, cs] = column_sum(pool) / n_pix
            r.third[0:1, cs] = gain_grad
            r.third[1:2, cs] = shift_grad
            k0, k1 = mul * k0, mul * k1
            for at, _, _ in geo.slabs():
                v = mul * r.e[at, ls] - (k0 + br[at, ls] * k1)
                r.bg[at, cs] = v.astype(bf16)
        r.push("d3", slice(None), lanes(n * CHUNK, CHUNK))

    in_pairs(each, lambda j, p: r.meta[ORDER + p * each + j], load, work)


def by_destination(r, parts, body):
    each = parts[0].shape[0]

    def step(j, carry):
        for p, ref in enumerate(parts):
            body(r.meta[ORDER + p * each + j], ref, j)
        return carry

    lax.fori_loop(0, each, step, 0)


def third_products(r, geo, act2_own, weight, parts, row0=0):
    r.wide[...] = dot_tn(act2_own[...], r.bg[...]).astype(bf16)

    def body(n, ref, place):
        for half in range(CHUNK // LANE):
            rows = slice(row0 + half * LANE, row0 + (half + 1) * LANE)
            ref[place, rows, :] = r.wide[:, lanes(n * CHUNK + half * LANE)]

    by_destination(r, parts, body)
    if row0 == 256:
        r.push("away")
        r.push("home")
    r.ag2[...] = dot_nt(r.bg[...], weight[...]).astype(bf16)
    r.push("ag2")


def conv_backward(r, geo, prm, wait, weight_t, sem, parts, top):
    own = r.meta[OWN]
    n_pix = pixel_count(r, geo)
    width = r.ag2.shape[1]
    clear_border(r.sg, geo, width, 2, 0)
    r.sgo[...] = jnp.zeros_like(r.sgo)

    def body(c, carry):
        cs = lanes(c * LANE)
        wait(c)
        s1, s2 = zeros8(), zeros8()
        m = r.mask[0]
        for at, _, _ in geo.slabs():
            e = (r.ag2[at, cs].astype(f32) * r.d2[at, cs].astype(f32)) * m
            r.e[at, 0:LANE] = e
            s1 = s1 + eights(e)
            s2 = s2 + eights(e * r.h2[at, cs].astype(f32))
        gain, shift, scale = prm[20:21, cs], prm[21:22, cs], r.gr2[0:1, cs]
        shift_grad = 0.5 * column_sum(s1)
        gain_grad, k0, k1 = norm_back(n_pix, gain, shift, shift_grad, 0.5 * column_sum(s2), 2.0)
        k0, k1, scale = scale * k0, scale * k1, 0.5 * scale
        for at, h, w in geo.slabs():
            v = scale * r.e[at, 0:LANE] - m * (k0 + r.h2[at, cs].astype(f32) * k1)
            store_shifted(r.sg, v, h, w, c, width, geo, -1)

        @pl.when(c == own)
        def _():
            r.small2[0:1, :] = gain_grad
            r.small2[1:2, :] = shift_grad
            centre = lanes(width + c * LANE)
            for a in range(3):
                for h in range(geo.high):
                    if 0 <= h - a + 1 < geo.high:
                        to = slice(h * geo.step, (h + 1) * geo.step)
                        start = (h - a + 2) * geo.step
                        r.sgo[to, a * LANE : (a + 1) * LANE] = r.sg[start : start + geo.step, centre]

        return carry

    lax.fori_loop(0, width // LANE, body, 0)
    if not top:
        r.ready("g")
    part = dot_tn(r.sgo[...], r.g[geo.step : geo.step + geo.rows, :])
    for a in range(3):
        for k in range(3 * width // LANE):
            block = part[a * LANE : (a + 1) * LANE, k * LANE : (k + 1) * LANE]
            b, first = k // (width // LANE), k % (width // LANE) * LANE
            r.wg[3 * a + b, first : first + LANE, :] = jnp.transpose(block).astype(bf16)

    def hand_out(n, ref, place):
        rows = rows_at(n * 64, 64, 64)
        for tap in range(9):
            ref[place, tap * 64 : (tap + 1) * 64, :] = r.wg[tap, rows, :]
        if top:
            pieces = [r.pooled[0:1, lanes(n * CHUNK, CHUNK)], r.grad[0:1, :].astype(f32)]
            pieces = [v[:, i * LANE : (i + 1) * LANE] for v in pieces for i in range(2)]
            pieces.append(jnp.zeros((HEAD_ROWS - 4, LANE), f32))
            ref[place, 832 : 832 + HEAD_ROWS, :] = jnp.concatenate(pieces, axis=0).astype(bf16)

    by_destination(r, parts, hand_out)
    r.push("away")
    r.push("home")
    arrived(weight_t, sem)
    total = None
    for a in range(3):
        lhs = r.sg[(2 - a) * geo.step : (2 - a) * geo.step + geo.rows, :]
        part = dot_nt(lhs, weight_t[a])
        total = part if total is None else total + part
    r.gg[...] = total.astype(bf16)
    r.push("gg")


def gate_backward(r, geo, prm):
    n_pix = pixel_count(r, geo)
    width = r.gg.shape[1]
    own = r.meta[OWN] if width > LANE else 0

    def body(c, carry):
        cs = lanes(c * LANE)
        r.ready_lanes(c)
        for at, _, _ in geo.slabs():
            grad = r.gg[at, cs].astype(f32)
            r.e[at, :] = grad * r.plus[at, cs].astype(f32)
            r.field[at, :] = grad * r.slope[at, cs].astype(f32)
        s1, s2 = zeros8(), zeros8()
        half_next, m = r.mask[2], r.mask[0]
        for at, h, w in geo.slabs():
            back = taps_sum(r.field, prm, cs, h, w, geo, -1) * half_next
            e = (r.e[at, :] + (pltpu.roll(back, 1, axis=0) - back)) * r.d1[at, cs].astype(f32)
            r.e[at, :] = e
            s1 = s1 + eights(e)
            s2 = s2 + eights(e * r.h1[at, cs].astype(f32))
        gain, shift, scale = prm[0:1, cs], prm[1:2, cs], r.gr1[0:1, cs]
        shift_grad = 0.5 * column_sum(s1)
        gain_grad, k0, k1 = norm_back(n_pix, gain, shift, shift_grad, 0.5 * column_sum(s2), 2.0)
        k0, k1, scale = scale * k0, scale * k1, 0.5 * scale
        for at, _, _ in geo.slabs():
            v = scale * r.e[at, :] - m * (k0 + r.h1[at, cs].astype(f32) * k1)
            r.fg[at, cs] = v.astype(bf16)

        @pl.when(c == own)
        def _():
            r.ready("diff")
            r.small[SMALL_ROWS - 4 :, :] = jnp.zeros((4, LANE), f32)
            r.small[0:1, :] = gain_grad
            r.small[1:2, :] = shift_grad
            for a in range(3):
                for b in range(3):
                    for first, reach in ((2, 1), (11, 2)):
                        total = zeros8()
                        for at, h, w in geo.slabs():
                            dh, dw = h - reach * (a - 1), w - reach * (b - 1)
                            if 0 <= dh < geo.high and 0 <= dw < geo.wide:
                                total = total + eights(r.diff[at, :] * r.field[geo.slab(dh, dw), :])
                        row = first + 3 * a + b
                        r.small[row : row + 1, :] = 0.25 * column_sum(total)

        return carry

    lax.fori_loop(0, width // LANE, body, 0)


def first_products(r, geo, x, parts):
    own = r.meta[OWN] if r.fg.shape[1] > LANE else 0
    r.wide[...] = dot_tn(r.fg[:, lanes(own * LANE)], x[...]).astype(bf16)

    def body(n, ref, place):
        for half in range(CHUNK // LANE):
            block = r.wide[:, lanes(n * CHUNK + half * LANE)]
            ref[place, half * LANE : (half + 1) * LANE, :] = jnp.transpose(block)

    by_destination(r, parts, body)


def third_backward(r, geo, thr, weight_in, pg, each):
    n_pix = pixel_count(r, geo)
    own = r.meta[OWN]
    per_own = r.e3.shape[1] // CHUNK
    buffers = [r.br0, r.br1]

    def load(n, slot):
        rows = rows_at(n * CHUNK, CHUNK, CHUNK)
        buffers[slot][...] = dot_nt(r.fg[...], weight_in[rows, :])

    def work(n, slot, j, p):
        br = buffers[slot]
        r.ready_chunk(n)
        for half in range(CHUNK // LANE):
            ls = slice(half * LANE, (half + 1) * LANE)
            cs = lanes(n * CHUNK + half * LANE)
            grad = (0.5 * pg[0:1, cs]) * r.mask[0]
            s1, s2 = zeros8(), zeros8()
            for at, _, _ in geo.slabs():
                out_grad = br[at, ls] + r.d3_next[at, cs].astype(f32) * grad
                e = out_grad * r.d3[at, cs].astype(f32)
                br[at, ls] = e
                s1 = s1 + eights(e)
                s2 = s2 + eights(e * r.y3[at, cs].astype(f32))
            gain, shift, scale = thr[0:1, cs], thr[1:2, cs], r.gr3[0:1, cs]
            shift_grad = 0.5 * column_sum(s1)
            gain_grad, k0, k1 = norm_back(n_pix, gain, shift, shift_grad, 0.5 * column_sum(s2), 1.0)
            r.third[0:1, cs] = gain_grad
            r.third[1:2, cs] = shift_grad
            k0, k1, scale = scale * k0, scale * k1, 0.5 * scale
            for at, _, _ in geo.slabs():
                v = scale * br[at, ls] - (k0 + r.y3[at, cs].astype(f32) * k1)
                r.bg[at, cs] = v.astype(bf16)
        owner = n // per_own

        @pl.when(owner == own)
        def _():
            r.e3[:, lanes((n - owner * per_own) * CHUNK, CHUNK)] = br[...].astype(bf16)

    in_pairs(each, lambda j, p: r.meta[ORDER + p * each + j], load, work)


class Sizes:
    def __init__(self, geo, inner, wide, order_n):
        self.geo, self.inner, self.wide, self.order_n = geo, inner, wide, order_n
        self.mask = VM((MASKS, geo.seg, LANE), f32)
        self.field = VM((geo.rows, LANE), f32)
        self.pair = VM((geo.rows, CHUNK), f32)

    def narrow(self, dtype=bf16):
        return ((self.geo.rows, self.inner), dtype)

    def slim(self, dtype=bf16):
        return ((self.geo.rows, LANE), dtype)

    def broad(self, dtype=bf16):
        return ((self.geo.rows, self.wide), dtype)

    def stacked(self):
        return ((self.geo.rows + 2 * self.geo.step, 3 * self.inner), bf16)

    def parts(self, rows):
        shape = ((self.order_n // 2, rows, LANE), bf16)
        return dict(away=shape, home=shape)

    def middle(self):
        return dict(h2=self.narrow(), d2=self.narrow(), gr2=((1, self.inner), f32), act2_own=self.slim())

    def gate(self, width):
        saved = ((self.geo.rows, width), bf16)
        return dict(h1=saved, d1=saved, plus=saved, slope=saved, diff=self.slim(f32), gr1=((1, width), f32))

    def conv_back_scratch(self, width):
        return dict(
            w_t=VM((3, width, 3 * self.inner), bf16),
            sg=VM(*self.stacked()),
            sgo=VM((self.geo.rows, 3 * LANE), bf16),
            wg=VM((9, self.inner, LANE), bf16),
        )

    def gate_back_scratch(self):
        return dict(mask=self.mask, field=self.field, e=self.field, wide=VM((LANE, self.wide), bf16))


def dma(count):
    return pltpu.SemaphoreType.DMA((count,))


def own_rows_of(prm, layer):
    return prm.at[pl.ds(layer * SLOT, SMALL_ROWS)]


def kernel_gate_own(z, meta, source, x, own_small, after=()):
    geo = z.geo

    def body(r):
        source.start(IN_OWN, r, r.w_in, r.sem.at[0])
        fill_masks(r, geo)
        r.ready("x")
        arrived(r.w_in, r.sem.at[0])
        first_matmul(r, geo, r.x, r.w_in, r.pre)
        gate_forward(r, geo, own_rows_of(r.prm, 0), r.pre)
        r.push("diff")
        r.push("gated")

    return call(
        "gate_own",
        body,
        dict(source.operands(), meta=(meta, SM), x=(x, LATE), prm=(own_small, VM)),
        dict(z.gate(LANE), gated=z.slim()),
        dict(
            field=z.field, act=z.field, mask=z.mask, pre=z.field,
            w_in=VM((z.wide, LANE), bf16), sem=dma(1),
        ),
        flops=4_000_000_000,
        nbytes=6_000_000,
        after=after,
    )


EXTRA = 16


def kernel_conv_own(z, meta, source, gated, chans, own_small, after=()):
    geo = z.geo

    def body(r):
        source.start(CONV_OWN, r, r.w_mid, r.sem.at[0])
        fill_masks(r, geo)
        clear_border(r.g, geo, z.inner, 0, 2)
        for i in range(len(gated)):
            r.ready("gated" + str(i))
            c = chans(i, r.meta[OWN])
            for at, h, w in geo.slabs():
                store_shifted(r.g, r.gated[i][at, :], h, w, c, z.inner, geo, 1)
        r.push("g")
        arrived(r.w_mid, r.sem.at[0])
        conv_matmul(r, geo, r.g, r.w_mid, r.pre)
        cs = slice(0, LANE)
        mean, rr = statistics(r.pre, cs, r, geo)
        prm = own_rows_of(r.prm, 0)
        scale = prm[20:21, cs] * rr
        mul = 0.5 * scale
        add = 0.5 * prm[21:22, cs] - mean * mul
        for at, _, _ in geo.slabs():
            r.half[at, :] = (r.pre[at, cs] * mul + add).astype(bf16)
        near = scale.astype(bf16).astype(f32)
        rows = jnp.concatenate([near, scale - near, jnp.zeros((EXTRA - 2, LANE), f32)], axis=0)
        r.half[geo.rows :, :] = rows.astype(bf16)
        r.push("half")

    return call(
        "conv_own",
        body,
        dict(
            source.operands(), meta=(meta, SM), prm=(own_small, VM),
            gated=[(item, LATE) for item in gated],
        ),
        dict(g=z.stacked(), half=((geo.rows + EXTRA, LANE), bf16)),
        dict(mask=z.mask, pre=z.field, w_mid=VM((3, 3, z.inner, LANE), bf16), sem=dma(1)),
        flops=6_000_000_000,
        nbytes=6_000_000,
        after=after,
    )


def kernel_third(z, meta, source, halves, chans, x, thr, after=()):
    geo = z.geo

    def body(r):
        source.start(OUT, r, r.w_out, r.sem.at[0])
        fill_masks(r, geo)
        own = r.meta[OWN]
        for i in range(len(halves)):
            r.ready("halves" + str(i))
            c = chans(i, r.meta[OWN])
            cs = lanes(c * LANE)
            for at, _, _ in geo.slabs():
                half = r.halves[i][at, :]
                act, slope = silu_parts(half.astype(f32))
                r.h2[at, cs] = half
                r.d2[at, cs] = slope.astype(bf16)
                r.act2[at, cs] = act.astype(bf16)
            tail = r.halves[i][geo.rows :, :].astype(f32)
            r.gr2[0:1, cs] = tail[0:1] + tail[1:2]

            @pl.when(c == own)
            def _():
                own_masked(r, geo, cs)

        for name in ("h2", "d2", "act2_own"):
            r.push(name)
        r.ready("x")
        arrived(r.w_out, r.sem.at[0])
        third_forward(r, geo, r.thr, r.act2, r.w_out, r.x)

    return call(
        "third_forward",
        body,
        dict(
            source.operands(), meta=(meta, SM), thr=(thr, VM),
            halves=[(item, LATE) for item in halves], x=(x, LATE),
        ),
        dict(
            z.middle(), y3=z.broad(), d3=z.broad(), x_next=z.broad(), gr3=((1, z.wide), f32),
        ),
        dict(
            mask=z.mask, w_out=VM((z.inner, z.wide), bf16), act2=VM(*z.narrow()), br0=z.pair, br1=z.pair,
            sem=dma(1),
        ),
        flops=12_000_000_000,
        nbytes=16_000_000,
        after=after,
    )


def kernel_top(z, meta, source, x, prm, thr, grad_low, bias, after=()):
    geo = z.geo

    def body(r):
        source.start(IN, r, r.w_in, r.sem.at[0])
        source.start(CONV, r, r.w_mid, r.sem.at[1])
        source.start(OUT, r, r.w_out, r.sem.at[2])
        source.start(HEAD, r, r.w_head, r.sem.at[3])
        source.start(CONV_T, r, r.w_t, r.sem.at[4])
        fill_masks(r, geo)
        r.ready("x")
        arrived(r.w_in, r.sem.at[0])
        first_matmul(r, geo, r.x, r.w_in, r.pre)
        gate_forward(r, geo, r.prm, r.pre)
        r.push("diff")
        arrived(r.w_mid, r.sem.at[1])
        conv_matmul(r, geo, r.g, r.w_mid, r.pre)
        middle_forward(r, geo, r.prm, r.pre, r.act2)
        arrived(r.w_out, r.sem.at[2])
        source.wait_head(r.w_head, r.sem.at[3])
        r.pg[...] = dot(r.grad[...], r.w_head[...])[0:1] / pixel_count(r, geo)
        third_both(r, geo, r.thr, r.act2, r.w_out, r.x, r.pg, [r.away, r.home])
        low = jnp.broadcast_to(r.pooled[...].astype(bf16), (16, z.wide))
        r.logits[...] = dot_nt(low, r.w_head[...])[0:8] + r.bias[...]
        r.pooled_out[...] = r.pooled[...]
        third_products(r, geo, r.act2_own, r.w_out, [r.away, r.home], 576)
        conv_backward(r, geo, r.prm, lambda c: None, r.w_t, r.sem.at[4], [r.away, r.home], True)

    row = ((1, z.wide), f32)
    return call(
        "top_both",
        body,
        dict(
            source.operands(), meta=(meta, SM), x=(x, LATE), prm=(prm, VM), thr=(thr, VM),
            grad=(grad_low, VM), bias=(bias, VM),
        ),
        dict(
            z.gate(z.inner), **z.parts(832 + HEAD_ROWS), g=z.stacked(), d3=z.broad(), pg=row, pooled_out=row,
            logits=((8, bias.shape[1]), f32), third=((2, z.wide), f32), gg=z.narrow(), small2=((2, LANE), f32),
        ),
        dict(
            z.conv_back_scratch(z.inner),
            **{name: VM(*value) for name, value in z.middle().items()},
            field=z.field, act=z.field, mask=z.mask, br0=z.pair, br1=z.pair, e=z.pair,
            pooled=VM(*row), ag2=VM(*z.narrow()), pre=VM(*z.narrow(f32)), act2=VM(*z.narrow()),
            w_in=VM((z.wide, z.inner), bf16), w_mid=VM((3, 3, z.inner, z.inner), bf16),
            w_out=VM((z.inner, z.wide), bf16), w_head=VM((bias.shape[1], z.wide), bf16),
            bg=VM(*z.broad()), wide=VM((LANE, z.wide), bf16), sem=dma(5),
        ),
        flops=60_000_000_000,
        nbytes=30_000_000,
        settle=True,
        after=after,
    )


def gate_back_ins(kept, prm):
    ins = {name: (getattr(kept, name), SLICED) for name in ("plus", "slope", "h1", "d1")}
    return dict(ins, diff=(kept.diff, LATE), gr1=(kept.gr1, VM), prm=(prm, VM))


def kernel_join(z, meta, source, source_below, kept, below, prm, thr, x, after=()):
    geo = z.geo

    def body(r):
        source.start(IN, r, r.w_in, r.sem.at[0])
        r.start_rest()
        source_below.start(OUT, r, r.w_out, r.sem.at[1])
        fill_masks(r, geo)
        gate_backward(r, geo, r.prm)
        arrived(r.w_in, r.sem.at[0])
        third_backward(r, geo, r.thr, r.w_in, r.pg, z.order_n // 2)
        r.push("e3")
        r.ready("x")
        first_products(r, geo, r.x, [r.away, r.home])
        arrived(r.w_out, r.sem.at[1])
        third_products(r, geo, r.act2_own, r.w_out, [r.away, r.home], 256)

    return call(
        "join_backward",
        body,
        dict(
            {**source.operands(), **source_below.operands()},
            **gate_back_ins(kept, prm), meta=(meta, SM), gg=(kept.gg, SLICED), thr=(thr, VM), pg=(kept.pg, VM),
            d3_next=(kept.d3, ORDERED), d3=(below.d3, ORDERED), y3=(below.y3, ORDERED), gr3=(below.gr3, VM),
            x=(x, LATE), act2_own=(below.act2_own, VM),
        ),
        dict(
            z.parts(512), small=((SMALL_ROWS, LANE), f32), third=((2, z.wide), f32), ag2=z.narrow(),
            e3=((geo.rows, z.wide // 4), bf16),
        ),
        dict(
            z.gate_back_scratch(), fg=VM(*z.narrow()), w_in=VM((z.wide, z.inner), bf16),
            w_out=VM((z.inner, z.wide), bf16), br0=z.pair, br1=z.pair, bg=VM(*z.broad()), sem=dma(2),
        ),
        flops=20_000_000_000,
        nbytes=30_000_000,
        settle=True,
        after=after,
    )


def kernel_conv_back(z, meta, source, ag2, kept, g, prm, after=()):
    geo = z.geo

    def body(r):
        source.start(CONV_ROWS, r, r.w_t, r.sem.at[0])
        fill_masks(r, geo)
        conv_backward(r, geo, r.prm, r.ready_lanes, r.w_t, r.sem.at[0], [r.away, r.home], False)

    return call(
        "conv_backward",
        body,
        dict(
            source.operands(), meta=(meta, SM), ag2=(ag2, SLICED), d2=(kept.d2, SLICED), h2=(kept.h2, SLICED),
            gr2=(kept.gr2, VM), prm=(prm, VM), g=(g, LATE),
        ),
        dict(z.parts(576), gg=z.slim(), small2=((2, LANE), f32)),
        dict(z.conv_back_scratch(LANE), mask=z.mask, e=z.field, sem=dma(1)),
        flops=12_000_000_000,
        nbytes=16_000_000,
        settle=True,
        after=after,
    )


def kernel_bottom(z, meta, gg, kept, own_small, x, seconds, join_small, thirds, after=()):
    geo = z.geo
    per = thirds[0].shape[1] // 4 // LANE
    total = -(-(2 * SMALL_ROWS + 4 + 4 * per) // 16) * 16

    def body(r):
        fill_masks(r, geo)
        gate_backward(r, geo, own_rows_of(r.prm, 0))
        r.push("fg")
        pieces = [r.small[...], r.join_small[...]] + [ref[...] for ref in r.seconds]
        for ref in r.thirds:
            own = r.meta[OWN] * per * LANE
            for k in range(2):
                pieces += [ref[k : k + 1, lanes(own + n * LANE)] for n in range(per)]
        filled = 2 * SMALL_ROWS + 4 + 4 * per
        pieces.append(jnp.zeros((total - filled, LANE), f32))
        both = jnp.concatenate(pieces, axis=0).astype(bf16)
        for ref in (r.away, r.home):
            for place in range(ref.shape[0]):
                ref[place, 256:, :] = both
        r.ready("x")
        first_products(r, geo, r.x, [r.away, r.home])
        r.push("away")
        r.push("home")

    return call(
        "bottom_backward",
        body,
        dict(
            gate_back_ins(kept, own_small), meta=(meta, SM), gg=(gg, SLICED), x=(x, LATE),
            join_small=(join_small, VM), seconds=[(item, VM) for item in seconds],
            thirds=[(item, VM) for item in thirds],
        ),
        dict(z.parts(256 + total), fg=z.slim()),
        dict(z.gate_back_scratch(), small=VM((SMALL_ROWS, LANE), f32)),
        flops=4_000_000_000,
        nbytes=10_000_000,
        settle=True,
        after=after,
    )


def kernel_input_grad(z, meta, source, fgs, chans, e3, after=()):
    geo = z.geo
    quarter = e3.shape[1]

    def body(r):
        source.start(IN_ROWS, r, r.w_in, r.sem.at[0])
        for i in range(len(fgs)):
            r.ready("fgs" + str(i))
            r.fg[:, lanes(chans(i, r.meta[OWN]) * LANE)] = r.fgs[i][...]
        r.ready("e3")
        arrived(r.w_in, r.sem.at[0])
        r.x_grad[...] = (dot_nt(r.fg[...], r.w_in[...]) + 0.5 * r.e3[...].astype(f32)).astype(bf16)
        r.push("x_grad")

    return call(
        "input_grad",
        body,
        dict(
            source.operands(), meta=(meta, SM), fgs=[(item, LATE) for item in fgs],
            e3=(e3, LATE),
        ),
        dict(x_grad=((geo.rows, quarter), bf16)),
        dict(w_in=VM((quarter, z.inner), bf16), fg=VM(*z.narrow()), sem=dma(1)),
        flops=1_000_000_000,
        nbytes=8_000_000,
        after=after,
    )


def fold(pairs, stack_rows=0, after=()):
    slots = pairs[0][1].shape[0]
    rows = [home.shape[1] for _, home in pairs]
    total = sum(rows) + stack_rows

    def body(r):
        for k, out in enumerate(r.s):
            row = 0
            for i in range(len(pairs)):
                n = i * slots + k
                for name in ("x", "h"):
                    r.ready(name + str(n))
                added = rows[i] - (stack_rows if i == 0 else 0)
                out[row : row + added] = (r.x[n][:added].astype(f32) + r.h[n][:added].astype(f32)).astype(bf16)
                row += added
                if i == 0 and stack_rows:
                    out[row : row + stack_rows] = r.h[n][added:]
                    out[row + stack_rows : row + 2 * stack_rows] = r.x[n][added:]
                    row += 2 * stack_rows
            r.push("s" + str(k))

    outs = dict(s=[((total, LANE), bf16)] * slots)
    ins = dict(
        x=[(recv, LATE, k) for recv, _ in pairs for k in range(slots)],
        h=[(home, LATE, k) for _, home in pairs for k in range(slots)],
    )
    return call("fold", body, ins, outs, {}, after=after).s


def copies(sources, outs, plan, meta=None, after=()):
    ins = dict(a=[(item, HB) for item in sources])
    if meta is not None:
        ins.update(meta=(meta, SM))

    def body(r):
        started = []
        for i, (src, src_at, dst, dst_at) in enumerate(plan):
            if isinstance(src_at, tuple) and src_at[0] is Ellipsis:
                src_at = ((r.meta[CLIP_AT] // 2 - (r.meta[OWN] ^ src_at[1])) % 4,)
            started.append(pltpu.make_async_copy(r.a[src].at[src_at], r.o[dst].at[dst_at], r.sem.at[i]))
            started[-1].start()
        for item, (_, _, dst, dst_at) in zip(started, plan):
            item.wait()
            r.push("o" + str(dst), *(dst_at if isinstance(dst_at, tuple) else (dst_at,)))

    outs = dict(o=[(shape, sources[0].dtype) for shape in outs])
    return call("copies", body, ins, outs, dict(sem=dma(len(plan))), nbytes=2_000_000, after=after).o


class Grid:
    FULL, LOW, HIGH = (0, 1, 2, 5, 6, 7), (3, 8), (4, 9)

    def __init__(self, clip_n, chan_n):
        self.clip_n, self.chan_n = clip_n, chan_n
        self.z_n = clip_n // 2
        self.clip, self.chan = lax.axis_index(CLIP).astype(jnp.int32), lax.axis_index(CHAN).astype(jnp.int32)

    def across_x(self, value):
        return lax.ppermute(value, CLIP, [(i, i ^ 1) for i in range(self.clip_n)])

    def along_z(self, value, k):
        return lax.ppermute(value, CLIP, [(i, (i + 2 * k) % self.clip_n) for i in range(self.clip_n)])

    def across(self, value, flip):
        return lax.ppermute(value, CHAN, [(i, i ^ flip) for i in range(self.chan_n)])

    def column(self, own):
        return [own] + [self.along_z(own, k) for k in range(1, self.z_n)]

    def stack(self, column, cuts, after=()):
        plan = [(k, rows, i, k) for i, rows in enumerate(cuts) for k in range(self.z_n)]
        shapes = [(self.z_n, rows.stop - rows.start, LANE) for rows in cuts]
        return copies(column, shapes, plan, after=after)

    def cut(self, plane, cut, after=()):
        rows = plane[0].shape[1]
        whole = slice(None)
        plan = [(0, (whole, slice(0, cut)), 0, whole), (1, (whole, slice(cut, rows)), 1, whole)]
        shapes = [(self.z_n, cut, LANE), (self.z_n, rows - cut, LANE)]
        return copies(plane[1:], shapes, plan, after=after)

    def corner(self, plane, low, high, first):
        turned = [self.across(low, 2), self.across_x(high)]
        *turned, _ = lax.optimization_barrier((*turned, first))
        arrays = list(plane) + turned
        return arrays + [self.across(item, 1) for item in arrays]

    def all_chans(self, own, first=None):
        over_y = self.across(own, 2)
        if first is not None:
            over_y, _ = lax.optimization_barrier((over_y, first))
        return [own, over_y, self.across(own, 1), self.across(over_y, 1)]

    def send_z(self, shares):
        return [shares[0]] + [self.along_z(shares[k], k) for k in range(1, self.z_n)]


FLIPS = (0, 2, 1, 3)


def pack(names, masters, head=None, small=None, meta=None, after=()):
    ins = {n: (masters[n.rstrip(DIGITS)], LATE, layer) for n, layer in names.items()}
    rows = dict(first=256, conv=576, out=256, out1=256, head=2 * HEAD_PART, small=2 * SMALL_PART)
    scratch = {}
    if head is not None:
        ins.update(head=(head, VM), small=(small, VM), meta=(meta, SM))
        scratch.update(padded=VM((4 * HEAD_PART, head.shape[1]), f32))

    def body(r):
        row = 0
        for n in ins:
            if n in names:
                r.ready(n)
            if n == "first":
                r.p[row : row + 256] = r.first[...].astype(bf16)
            elif n == "conv":
                for tap in range(9):
                    r.p[row + tap * 64 : row + tap * 64 + 64] = r.conv[tap // 3, tap % 3].astype(bf16)
            elif n.startswith("out"):
                for half in range(2):
                    block = getattr(r, n)[:, half * LANE : (half + 1) * LANE].astype(bf16)
                    r.p[row + half * LANE : row + (half + 1) * LANE] = block
            elif n == "head":
                r.padded[...] = jnp.zeros_like(r.padded)
                r.padded[: head.shape[0], :] = r.head[...]
                own = r.padded[rows_at(r.meta[OWN] * HEAD_PART, HEAD_PART, 16), :].astype(bf16)
                for half in range(2):
                    at = row + half * HEAD_PART
                    r.p[at : at + HEAD_PART] = own[:, half * LANE : (half + 1) * LANE]
            elif n == "small":
                part = r.small[rows_at(r.meta[CLIP_AT] * SMALL_PART, SMALL_PART, 8), :]
                near = part.astype(bf16).astype(f32)
                r.p[row : row + 2 * SMALL_PART] = jnp.concatenate([near, part - near], axis=0).astype(bf16)
            row += rows.get(n, 0)
        r.push("p")

    outs = dict(p=((sum(rows.get(n, 0) for n in ins), LANE), bf16))
    return call("pack", body, ins, outs, scratch, nbytes=2_000_000, after=after).p


def pack_small(items):
    layers = items[0].shape[0]
    items = [jnp.transpose(item, (1, 2, 0, 3)) if item.ndim == 4 else item for item in items]

    def body(r):
        r.s[...] = jnp.zeros_like(r.s)
        for layer in range(layers):
            row = layer * SLOT
            for ref in r.i:
                if len(ref.shape) == 4:
                    for tap in range(9):
                        r.s[row : row + 1] = 0.5 * ref[tap // 3, tap % 3, layer : layer + 1, :]
                        row += 1
                else:
                    for k in range(ref.shape[1] // LANE):
                        r.s[row : row + 1] = ref[layer : layer + 1, k * LANE : (k + 1) * LANE]
                        row += 1

    ins = dict(i=[(item, VM) for item in items])
    return call("pack_small", body, ins, dict(s=((layers * SLOT, LANE), f32)), {}, nbytes=200_000).s


def spread_small(meta, chans, slots, layers, inner, wide, per):
    def body(r):
        for i, ref in enumerate(r.s):
            chan = chans(i, r.meta[OWN])
            for layer in range(layers):
                first = layer * SLOT
                r.prm[layer, :, lanes(chan * LANE)] = ref[first : first + SMALL_ROWS, :]
                for k in range(2):
                    for n in range(per):
                        at = first + 22 + k * per + n
                        r.thr[layer, k : k + 1, lanes((chan * per + n) * LANE)] = ref[at : at + 1, :]

    ins = dict(meta=(meta, SM), s=[(item, VM) for item in slots])
    outs = dict(prm=((layers, SMALL_ROWS, inner), f32), thr=((layers, 2, wide), f32))
    done = call("spread_small", body, ins, outs, {}, nbytes=200_000, direct=True)
    return done.prm, done.thr


def spread_gathered(every, row0, clip_n, chan_n, layers, inner, wide, per):
    def body(r):
        copy = pltpu.make_async_copy(r.every.at[:, pl.ds(row0, 2 * SMALL_PART)], r.part, r.sem.at[0])
        copy.start()
        copy.wait()
        for chan in range(chan_n):
            for clip in range(clip_n):
                rows = r.part[clip * chan_n + chan].astype(f32)
                r.own[clip * SMALL_PART : (clip + 1) * SMALL_PART] = rows[:SMALL_PART] + rows[SMALL_PART:]
            for layer in range(layers):
                first = layer * SLOT
                r.prm[layer][:, chan * LANE : (chan + 1) * LANE] = r.own[first : first + SMALL_ROWS, :]
                for k in range(2):
                    for n in range(per):
                        at = first + 22 + k * per + n
                        to = (chan * per + n) * LANE
                        r.thr[layer][k : k + 1, to : to + LANE] = r.own[at : at + 1, :]

    outs = dict(prm=[((SMALL_ROWS, inner), f32)] * layers, thr=[((2, wide), f32)] * layers)
    scratch = dict(
        part=VM((clip_n * chan_n, 2 * SMALL_PART, LANE), bf16), own=VM((layers * SLOT, LANE), f32), sem=dma(1)
    )
    ins = dict(every=(every, HB))
    done = call("spread_small", body, ins, outs, scratch, nbytes=200_000, direct=True)
    return done.prm, done.thr


def wait_all(r, *names):
    for n in names:
        for k in range(4):
            r.ready(n + str(k))


def four(refs, rows):
    a, b, c, d = [ref[rows].astype(f32) for ref in refs]
    return (a + c) + (b + d)


def finish_upper(shares1, shares2, layers, classes, after=()):
    def body(r):
        wait_all(r, "one", "two")
        for half in range(2):
            cs = slice(half * LANE, (half + 1) * LANE)
            r.out_grad[layers - 1, :, cs] = four(r.one, slice(576 + half * LANE, 576 + (half + 1) * LANE))
            r.out_grad[0, :, cs] = four(r.two, slice(256 + half * LANE, 256 + (half + 1) * LANE))
        pooled, grads, total = [], [], []
        for ref in r.one:
            own, other = ref[832:848].astype(f32), ref[848:864].astype(f32)
            for v in (own, other):
                pooled.append(jnp.concatenate([v[0:1], v[1:2]], axis=1))
                grads.append(jnp.concatenate([v[2:3], v[3:4]], axis=1))
            total.append(grads[-2] + grads[-1])
        pooled = jnp.concatenate(pooled, axis=0).astype(bf16)
        grads = jnp.concatenate(grads, axis=0).astype(bf16)
        r.head_grad[...] = dot_tn(grads, pooled)[:classes]
        r.bias_grad[...] = (total[0] + total[2]) + (total[1] + total[3])

    outs = dict(
        out_grad=((layers, LANE, 256), f32), head_grad=((classes, 256), f32), bias_grad=((1, 256), f32)
    )
    ins = dict(one=[(item, LATE) for item in shares1], two=[(item, LATE) for item in shares2])
    return call("finish_upper", body, ins, outs, {}, nbytes=4_000_000, after=after, direct=True)


def finish_lower(shares, layers, smalls, after=()):
    def body(r):
        wait_all(r, "one", "two", "last")
        for layer, refs in ((0, r.last), (layers - 1, r.one)):
            for tap in range(9):
                r.conv_grad[layer, tap // 3, tap % 3] = four(refs, slice(tap * 64, (tap + 1) * 64))
        r.push("conv_grad")
        r.in_grad[0] = four(r.last, slice(576, 832))
        r.in_grad[layers - 1] = four(r.two, slice(0, 256))
        r.push("in_grad")
        r.sum[...] = four(r.last, slice(832, r.last[0].shape[0]))
        for out, (rows, shape) in zip(r.small, smalls):
            for layer, row in enumerate(rows):
                if len(shape) == 4:
                    for tap in range(9):
                        out[tap // 3, tap % 3, layer : layer + 1] = r.sum[row + tap : row + tap + 1, :]
                else:
                    for k in range(shape[1] // LANE):
                        out[layer : layer + 1, k * LANE : (k + 1) * LANE] = r.sum[row + k : row + k + 1, :]

    one, two, last = [[(item, LATE) for item in group] for group in shares]
    shapes = [(3, 3, shape[0], LANE) if len(shape) == 4 else shape for _, shape in smalls]
    outs = dict(
        in_grad=((layers, 256, LANE), f32), conv_grad=((layers, 3, 3, 64, LANE), f32),
        small=[(shape, f32) for shape in shapes],
    )
    scratch = dict(sum=VM((shares[2][0].shape[0] - 832, LANE), f32))
    ins = dict(one=one, two=two, last=last)
    done = call("finish_lower", body, ins, outs, scratch, nbytes=4_000_000, after=after)
    small = [jnp.transpose(item, (2, 0, 1, 3)) if item.ndim == 4 else item for item in done.small]
    return done.in_grad, done.conv_grad, small


def local(
    clip_input,
    seg_count,
    proj_in_master,
    conv_master,
    proj_out_master,
    head_master,
    gain_first,
    shift_first,
    taps_near,
    taps_far,
    gain_second,
    shift_second,
    gain_third,
    shift_third,
    head_bias,
    logit_grad,
    clip_n,
    chan_n,
):
    grid = Grid(clip_n, chan_n)
    clip, chan = grid.clip, grid.chan
    _, seg, high_map, wide_map, wide = clip_input.shape
    layers = proj_in_master.shape[0]
    inner = proj_in_master.shape[2] * chan_n
    classes = head_master.shape[1]
    class_pad = -(-classes // LANE) * LANE
    geo = Geometry(seg, high_map, wide_map)
    order_n = wide // CHUNK
    z = Sizes(geo, inner, wide, order_n)
    third_rows = wide // chan_n // LANE
    direct = clip_n == 8 and chan_n == 4 and proj_in_master.shape[1] == 256

    grad_low = logit_grad.astype(bf16)
    grad_rows = jnp.pad(grad_low, ((0, 15), (0, class_pad - classes)))
    bias_row = jnp.pad(head_bias, (0, class_pad - classes))[None]
    order = jnp.arange(order_n, dtype=jnp.int32)
    chans = lambda i, own: i
    if direct:
        z_to = (clip // 2 + jnp.arange(4, dtype=jnp.int32)) % 4
        order = jnp.concatenate([z_to * 2 + ((clip % 2) ^ 1), z_to * 2 + clip % 2]).astype(jnp.int32)
        chans = lambda i, own: own ^ FLIPS[i]
    meta = jnp.concatenate([seg_count.astype(jnp.int32), chan[None], clip[None], order])
    x0 = jnp.transpose(clip_input[0], (1, 2, 0, 3)).reshape(geo.rows, wide)
    own_small = pack_small(
        [
            gain_first,
            shift_first,
            taps_near,
            taps_far,
            gain_second,
            shift_second,
            gain_third,
            shift_third,
        ]
    )

    def gather_chan(own):
        if direct:
            return grid.all_chans(own)
        every = lax.all_gather(own, CHAN, axis=0, tiled=False)
        return [every[i] for i in range(chan_n)]

    if direct:
        masters = dict(first=proj_in_master, conv=conv_master, out=proj_out_master)
        packed = pack(dict(out=0, out1=1), masters, head_master.T, own_small, meta)
        by_core = lax.all_gather(packed, (CLIP, CHAN), axis=0, tiled=False)
        prm, thr = spread_gathered(by_core, 512 + 2 * HEAD_PART, clip_n, chan_n, layers, inner, wide, third_rows)
        numbers = in_order(chan_n)
        near = [along_column(0, 0), along_column(1, 0)]
        corners = [(0, 0), (1, 0), (0, 2), (1, 2), (1, 2)]
        places = [along_column(dx, flip ^ core) for core in (0, 1) for dx, flip in corners]
        full, low_part, high_part = grid.FULL, grid.LOW, grid.HIGH

        own_in = pack(dict(first=0), masters, after=[packed])
        column_in = grid.column(own_in)
        own_mid = pack(dict(conv=0), masters, after=[own_in])
        (in_a,) = grid.stack(column_in, [slice(0, 256)], after=[own_mid])
        in_x = grid.across_x(in_a)
        column_mid = grid.column(own_mid)
        in_source = Slots("wa", [in_a, in_x], near, {IN_OWN: [(0, 0, 0, 256), (1, 0, 0, 256)]}, chan_n)
        gate0 = kernel_gate_own(z, meta, in_source, x0, own_small)
        (conv_a,) = grid.stack(column_mid, [slice(0, 576)], after=[gate0.gr1])
        conv_x = grid.across_x(conv_a)
        own_up = pack(dict(first=1, conv=1), masters, after=[conv_a])
        column_up = grid.column(own_up)
        gated = grid.all_chans(gate0.gated, own_up)
        mid_source = Slots("wb", [conv_a, conv_x], near, {CONV_OWN: [(0, 0, 0, 9), (1, 0, 0, 9)]}, chan_n)
        conv0 = kernel_conv_own(z, meta, mid_source, gated, chans, own_small, after=[own_up])
        half, _ = lax.optimization_barrier((conv0.half, column_up[1]))
        halves = grid.all_chans(half)

        (stack_up,) = grid.stack(column_up, [slice(0, 832)], after=[conv0.half])
        plane_up = [stack_up, grid.across_x(stack_up), grid.across(stack_up, 2)]
        plan = []
        for i in range(4):
            for k in range(2):
                plan.append((k, (..., FLIPS[i]), i, (k, slice(0, 256))))
                plan.append((2 + k, (..., FLIPS[i]), i, (k, slice(256, 832))))
        sent = copies([in_a, in_x, conv_a, conv_x], [(2, 832, LANE)] * 4, plan, meta, after=[stack_up])
        cuts = grid.cut(plane_up, 448, after=sent[:1])
        out_source = Slots("wc", [by_core], [numbers], {OUT: [(0, 0, 0, 2)]}, chan_n)
        third0 = kernel_third(z, meta, out_source, halves, chans, x0, thr[0], after=sent[:1] + cuts[:1])
        arrays_up = grid.corner(plane_up, *cuts, third0.gr3)
        last = len(arrays_up)
        parts = {
            IN: [(i, 0, 0, 256) for i in full + low_part],
            CONV: [(i, 256, 0, 9) for i in full] + [(i, 256, 0, 3) for i in low_part]
            + [(i, 0, 3, 6) for i in high_part],
            OUT: [(last, 256, 0, 2)],
            HEAD: [(last, 512, 0, 2)],
        }
        parts[CONV_T] = parts[CONV]
        top_source = Slots("wd", arrays_up + [by_core], places + [numbers], parts, chan_n)
    else:
        prm, thr = spread_small(meta, chans, gather_chan(own_small), layers, inner, wide, third_rows)
        head_low = jnp.pad(head_master.astype(bf16), ((0, 0), (0, class_pad - classes)))
        head_low = lax.all_gather(head_low.T, CLIP, axis=1, tiled=True)
        gathered, own_cols = [], []
        for master, clip_axis, chan_axis in ((proj_in_master, 1, 2), (conv_master, 3, 4), (proj_out_master, 2, 1)):
            own_cols.append(lax.all_gather(master.astype(bf16), CLIP, axis=clip_axis, tiled=True))
            gathered.append(lax.all_gather(own_cols[-1], CHAN, axis=chan_axis, tiled=True))
        in_source = Whole("wa", {IN_OWN: own_cols[0][0]})
        mid_source = Whole("wb", {CONV_OWN: own_cols[1][0]})
        out_source = Whole("wc", {OUT: gathered[2][0]})
        top_source = Whole("wd", {IN: gathered[0][1], CONV: gathered[1][1], OUT: gathered[2][1], HEAD: head_low})
        wide_own, inner_own = wide // chan_n, inner // chan_n
        in_rows = lax.dynamic_slice_in_dim(gathered[0][0], chan * wide_own, wide_own, 0)
        conv_rows = lax.dynamic_slice_in_dim(gathered[1][0], chan * inner_own, inner_own, 2)
        rows_source = Whole("we", {IN_ROWS: in_rows, CONV_ROWS: conv_rows})
        gate0 = kernel_gate_own(z, meta, in_source, x0, own_small)
        conv0 = kernel_conv_own(z, meta, mid_source, gather_chan(gate0.gated), chans, own_small)
        third0 = kernel_third(z, meta, out_source, gather_chan(conv0.half), chans, x0, thr[0])

    x1 = third0.x_next
    top = kernel_top(z, meta, top_source, x1, prm[1], thr[1], grad_rows, bias_row)
    after_join, after_mid, after_low = [], [], []
    if direct:
        *sent, _ = lax.optimization_barrier((*sent, top.third))
        rows_a = sent[:1] + [grid.across(item, flip) for item, flip in zip(sent[1:], FLIPS[1:])]
        parts = {IN_ROWS: [(i, 0, 0, 256) for i in range(4)], CONV_ROWS: [(i, 256, 0, 9) for i in range(4)]}
        rows_source = Slots("we", rows_a, [own_pair(flip) for flip in FLIPS], parts, chan_n)
    join = kernel_join(z, meta, top_source, out_source, top, third0, prm[1], thr[0], x1, after=after_join)
    if direct:
        away1, away2 = grid.across_x(top.away), grid.across_x(join.away)
        folded1 = fold([(away1, top.home)], HEAD_ROWS, after=[join.third])
        shares1 = grid.send_z(folded1)
        after_mid = folded1[:1]
    mid0 = kernel_conv_back(z, meta, rows_source, join.ag2, third0, conv0.g, prm[0], after=after_mid)
    if direct:
        folded2 = fold([(away2, join.home)], after=[mid0.small2])
        shares2 = grid.send_z(folded2)
        after_low = folded2[:1] + shares1[1:]
    low = kernel_bottom(
        z, meta, mid0.gg, gate0, own_small, x0, [mid0.small2, top.small2], join.small, [join.third, top.third],
        after=after_low,
    )

    at = 2 * SMALL_ROWS
    small_places = [
        ((0, SMALL_ROWS), gain_first.shape),
        ((1, SMALL_ROWS + 1), shift_first.shape),
        ((2, SMALL_ROWS + 2), taps_near.shape),
        ((11, SMALL_ROWS + 11), taps_far.shape),
        ((at, at + 2), gain_second.shape),
        ((at + 1, at + 3), shift_second.shape),
        ((at + 4, at + 4 + 2 * third_rows), gain_third.shape),
        ((at + 4 + third_rows, at + 4 + 3 * third_rows), shift_third.shape),
    ]
    if direct:
        last_away, _ = lax.optimization_barrier((low.away, shares2[1]))
        away3, away4 = grid.across_x(mid0.away), grid.across_x(last_away)
        folded3 = fold([(away3, mid0.home), (away4, low.home)])
        shares3 = grid.send_z(folded3)
        upper = finish_upper(shares1, shares2, layers, classes, after=folded3[:1])
        x_grad = kernel_input_grad(z, meta, rows_source, gather_chan(low.fg), chans, join.e3).x_grad
        in_share, mid_share, small_grads = finish_lower(
            [shares1, shares2, shares3], layers, small_places, after=[x_grad]
        )
        out_share = upper.out_grad
        head_share, bias_grad = upper.head_grad.T, upper.bias_grad[0, :classes]
    else:
        pooled_all = lax.all_gather(top.pooled_out.astype(bf16), CLIP, axis=0, tiled=True)
        grad_all = lax.all_gather(grad_low, CLIP, axis=0, tiled=True)
        own_rows = head_master.shape[0]
        pooled_own = lax.dynamic_slice_in_dim(pooled_all, clip * own_rows, own_rows, 1)
        head_share = dot_tn(pooled_own, grad_all)
        bias_grad = jnp.sum(grad_all.astype(f32), axis=0)

        def joined(item, first, rows):
            return jnp.concatenate([item.away, item.home], axis=0)[:, first : first + rows]

        in_terms = jnp.stack([joined(low, 0, 256), joined(join, 0, 256)]).reshape(layers, wide, LANE)
        mid_terms = jnp.stack([joined(mid0, 0, 576), joined(top, 0, 576)])
        mid_terms = mid_terms.reshape(layers, order_n, 3, 3, 64, LANE)
        mid_terms = jnp.transpose(mid_terms, (0, 2, 3, 1, 4, 5)).reshape(layers, 3, 3, inner, LANE)
        out_terms = jnp.stack([joined(join, 256, 256), joined(top, 576, 256)])
        out_terms = out_terms.reshape(layers, order_n, 2, LANE, LANE)
        out_terms = jnp.transpose(out_terms, (0, 3, 1, 2, 4)).reshape(layers, LANE, wide)
        in_share = lax.psum_scatter(in_terms, CLIP, scatter_dimension=1, tiled=True).astype(f32)
        mid_share = lax.psum_scatter(mid_terms, CLIP, scatter_dimension=3, tiled=True).astype(f32)
        out_share = lax.psum_scatter(out_terms, CLIP, scatter_dimension=2, tiled=True).astype(f32)
        small = lax.psum(low.home[0, 256:].astype(f32), CLIP)
        small_grads = []
        for rows, shape in small_places:
            count = 9 if len(shape) == 4 else shape[1] // LANE
            small_grads.append(jnp.stack([small[row : row + count] for row in rows]).reshape(shape))
        x_grad = kernel_input_grad(z, meta, rows_source, gather_chan(low.fg), chans, join.e3).x_grad

    input_grad = x_grad.reshape(high_map, wide_map, seg, -1)
    input_grad = jnp.transpose(input_grad, (2, 0, 1, 3))[None]
    return (
        top.logits[0:1, :classes],
        input_grad,
        in_share,
        mid_share,
        out_share,
        head_share,
        *small_grads,
        bias_grad,
    )


def solution(mesh):
    clip_n, chan_n = mesh.shape[CLIP], mesh.shape[CHAN]

    def program(*args):
        return local(*args, clip_n, chan_n)

    by_clip, by_chan = P(CLIP, None), P(None, CHAN)
    weights = (P(None, CLIP, CHAN), P(None, None, None, CLIP, CHAN), P(None, CHAN, CLIP), by_clip)
    taps = P(None, None, None, CHAN)
    small = (by_chan, by_chan, taps, taps, by_chan, by_chan, by_chan, by_chan, P())
    in_specs = (P(CLIP, None, None, None, None), P(CLIP)) + weights + small + (by_clip,)
    out_specs = (by_clip, P(CLIP, None, None, None, CHAN)) + weights + small
    return jax.shard_map(program, mesh=mesh, in_specs=in_specs, out_specs=out_specs, check_vma=False)
```
